32 devices in a mesh: user: 16 (over z, x, core), tensor: 2 (over y).
Axes of the slice: x: 2, y: 2, z: 4, core: 2. Of those that a mesh axis runs over, the one named last changes fastest.
Arguments:
- events: bfloat16 [256, 128, 1024], P('user', None, 'tensor'), may hold values from -6 to 6
- cotangent: bfloat16 [256, 128, 1024], P('user', None, 'tensor'), may hold values from -6 to 6
- w_in: bfloat16 [1024, 4096], P('user', 'tensor'), may hold values from -0.1875 to 0.1875
- w_out: bfloat16 [1024, 1024], P('user', 'tensor'), may hold values from -0.1875 to 0.1875
- slot_source: int32 [256], P('user'), may hold values from 0 to 15, as said below
- slot_length: int32 [256], P('user'), may hold values from 1 to 127, as said below
Outputs:
- grad_x: bfloat16 [256, 128, 1024], P('user', None, 'tensor')
- grad_w_in: float32 [1024, 4096], P('user', 'tensor')
- grad_w_out: float32 [1024, 1024], P('user', 'tensor')
The draws below stay inside these ranges and needn't reach their ends.
Inputs may be any that keep to these rules, and one draw needn't show every extreme that they name: `slot_source`: the 16 slots of one host name distinct user shards, and for each slot j the entries h * 16 + j over all hosts h name every user shard once, so every history is placed exactly once. `slot_length`: the 16 slot lengths of one host sum to 1024.
All inputs are finite; a program needn't handle non-finite values.
Results may differ from the reference program's by a relative error of at most 0.023.
Values may be sent and summed in bfloat16 or wider, within the bound.
No kernel may reach another device: no remote copies, remote signals or barrier semaphores. Data moves between devices by JAX's collectives and lax.ppermute only.
A program may use at most 128 MiB of HBM per device.

```python
import jax
import jax.numpy as jnp
from jax import lax

D = 1024
HEADS = 8
HEAD_DIM = 128
SEQ_LEN = 128
HIST_DEV = 16
ROWS = 1024
NSEQ = 256
N_USER = 16


def placement_tables(key):
    base = jax.random.fold_in(key, 7)
    key_p, key_t, key_c, key_l, key_s = jax.random.split(base, 5)
    count = N_USER
    first = jax.random.permutation(key_p, count).astype(jnp.int32)
    second = jax.random.permutation(key_t, count).astype(jnp.int32)
    offsets = jax.random.permutation(key_c, count).astype(jnp.int32)[:HIST_DEV]
    owners = jnp.arange(count, dtype=jnp.int32)[:, None]
    second_inv = jnp.argsort(second, stable=True).astype(jnp.int32)
    first_inv = jnp.argsort(first, stable=True).astype(jnp.int32)
    sources = first_inv[(second_inv[owners] - offsets[None, :]) % count]
    halves = jax.random.randint(key_l, (count, HIST_DEV // 2), 1, SEQ_LEN).astype(jnp.int32)
    halves = halves.at[:, 0].set(SEQ_LEN - 1)
    pairs = jnp.stack([halves, SEQ_LEN - halves], axis=-1).reshape(count, HIST_DEV)
    scores = jax.random.randint(key_s, (count, HIST_DEV), 0, 1 << 20) * HIST_DEV + jnp.arange(HIST_DEV, dtype=jnp.int32)[None, :]
    order = jnp.argsort(scores, axis=1, stable=True)
    lengths = jnp.take_along_axis(pairs, order, axis=1)
    return (sources.reshape(-1).astype(jnp.int32), lengths.reshape(-1).astype(jnp.int32))


def draw_slot_source(key, part):
    return placement_tables(key)[0]


def draw_slot_length(key, part):
    return placement_tables(key)[1]


def raised(drawn, own_key, source, target, shards_of, factor):
    owner, partner = [(jnp.arange(drawn.shape[dim]) // (drawn.shape[dim] // shards_of)).reshape([-1 if axis == dim else 1 for axis in range(drawn.ndim)]) for dim in (source, target)]
    chosen = jax.random.permutation(own_key, shards_of)[partner]
    strong = (owner == chosen) | (owner == (partner + shards_of // 2) % shards_of)
    return jnp.where(strong, factor * drawn, drawn)


def steps_of(key, dims, pieces, low, top_value):
    def one(dim, blocks):
        heights = jax.random.uniform(jax.random.fold_in(jax.random.fold_in(key, 6), dim), (blocks,), jnp.float32, low / len(pieces), top_value / len(pieces))
        return jnp.repeat(jnp.exp(heights), dims[dim] // blocks).reshape((-1,) + (1,) * (len(dims) - dim - 1))

    factor_of = one(*pieces[0])
    for cut in pieces[1:]:
        factor_of = factor_of * one(*cut)
    return factor_of


def noise(own_key, shape, spread, limit, cuts=(), kind=jnp.bfloat16):
    loudness = steps_of(own_key, shape, cuts, -0.22, 0.18) if cuts else 1.0
    array = jax.random.normal(own_key, shape, jnp.float32) * spread * loudness
    return jnp.minimum(jnp.maximum(array, -limit), limit).astype(kind)


def heavy_noise(rng, shape, scale, reach, cuts, heavy, kind=jnp.bfloat16):
    array = scale * jax.random.normal(rng, shape, jnp.float32)
    if cuts:
        array = array * steps_of(rng, shape, cuts, -0.22, 0.18)
    return jnp.clip(raised(array, jax.random.fold_in(rng, 3), *heavy), -reach, reach).astype(kind)


def setup_inputs(seed: int = 0) -> dict:
    key_of = jax.random.split(jax.random.key(seed), 7)
    return {
        "events": noise(key_of[0], (NSEQ, SEQ_LEN, D), 1.0, 6.0, ((0, 16), (2, 2))),
        "cotangent": heavy_noise(key_of[1], (NSEQ, SEQ_LEN, D), 1.0, 6.0, ((0, 16), (2, 2)), (0, 2, 16, 2.0)),
        "w_in": noise(key_of[2], (D, 4 * D), D ** -0.5, 0.1875, ((0, 16), (1, 2))),
        "w_out": noise(key_of[3], (D, D), D ** -0.5, 0.1875, ((0, 16), (1, 2))),
        "slot_source": draw_slot_source(jax.random.fold_in(key_of[6], 71), 0),
        "slot_length": draw_slot_length(jax.random.fold_in(key_of[6], 71), 0),
    }


eps = 1e-05

def silu_grad(t):
    sig = jax.nn.sigmoid(t)
    return sig * (1.0 + t * (1.0 - sig))

def host_rows(lengths, sources):
    ends = jnp.cumsum(lengths).astype(jnp.int32)
    starts = (ends - lengths).astype(jnp.int32)
    rows = jnp.arange(ROWS, dtype=jnp.int32)
    segment = lax.optimization_barrier(jnp.sum((rows[:, None] >= ends[None, :]).astype(jnp.int32), axis=1)).astype(jnp.int32)
    onehot = (segment[:, None] == jnp.arange(HIST_DEV, dtype=jnp.int32)[None, :]).astype(jnp.int32)
    position = (rows - lax.optimization_barrier(jnp.sum(onehot * starts[None, :], axis=1))).astype(jnp.int32)
    source = lax.optimization_barrier(jnp.sum(onehot * sources[None, :], axis=1)).astype(jnp.int32)
    return (segment, position, source)

def host_pass(x_flat, d_flat, w_in, w_out, lengths, sources):
    segment, position, source = host_rows(lengths, sources)
    index = ((source * HIST_DEV + segment) * SEQ_LEN + position).astype(jnp.int32)
    xp = jnp.take(x_flat, index, axis=0)
    dp = jnp.take(d_flat, index, axis=0)
    xf = xp.astype(jnp.float32)
    centred = xf - lax.optimization_barrier(jnp.mean(xf, axis=1, keepdims=True))
    rstd = lax.rsqrt(lax.optimization_barrier(jnp.mean(centred * centred, axis=1, keepdims=True)) + eps)
    nf = centred * rstd
    nb = nf.astype(jnp.bfloat16)
    z = jnp.dot(nb, w_in, preferred_element_type=jnp.float32)
    g = jax.nn.silu(z).astype(jnp.bfloat16).reshape(ROWS, HEADS, 4, HEAD_DIM)
    mask = (segment[:, None] == segment[None, :]) & (position[None, :] <= position[:, None])
    dh = jnp.dot(dp, w_out, preferred_element_type=jnp.float32).reshape(ROWS, HEADS, HEAD_DIM)
    scale = HEAD_DIM ** (-0.5)

    def one_head(items):
        parts, grad_h = items
        upart, vpart, qpart, kpart = (parts[:, 0], parts[:, 1], parts[:, 2], parts[:, 3])
        scores = jnp.dot(qpart, kpart.T, preferred_element_type=jnp.float32) * scale
        attn = jnp.where(mask, jax.nn.silu(scores) / SEQ_LEN, 0.0).astype(jnp.bfloat16)
        yval = jnp.dot(attn, vpart, preferred_element_type=jnp.float32)
        ycen = yval - lax.optimization_barrier(jnp.mean(yval, axis=1, keepdims=True))
        yrstd = lax.rsqrt(lax.optimization_barrier(jnp.mean(ycen * ycen, axis=1, keepdims=True)) + eps)
        ynorm = ycen * yrstd
        uf = upart.astype(jnp.float32)
        hpart = (ynorm * uf).astype(jnp.bfloat16)
        grad_u = grad_h * ynorm
        grad_yn = grad_h * uf
        grad_y = ((grad_yn - lax.optimization_barrier(jnp.mean(grad_yn, axis=1, keepdims=True)) - ynorm * lax.optimization_barrier(jnp.mean(grad_yn * ynorm, axis=1, keepdims=True))) * yrstd).astype(jnp.bfloat16)
        grad_a = jnp.dot(grad_y, vpart.T, preferred_element_type=jnp.float32)
        grad_v = jnp.dot(attn.T, grad_y, preferred_element_type=jnp.float32)
        grad_s = jnp.where(mask, grad_a * silu_grad(scores) * (scale / SEQ_LEN), 0.0).astype(jnp.bfloat16)
        grad_q = jnp.dot(grad_s, kpart, preferred_element_type=jnp.float32)
        grad_k = jnp.dot(grad_s.T, qpart, preferred_element_type=jnp.float32)
        return (hpart, jnp.stack([grad_u, grad_v, grad_q, grad_k], axis=1))
    hparts, grads = lax.map(one_head, (g.transpose(1, 0, 2, 3), dh.transpose(1, 0, 2)))
    hb = hparts.transpose(1, 0, 2).reshape(ROWS, D)
    dgrad = grads.transpose(1, 0, 2, 3).reshape(ROWS, 4 * D)
    dz = (dgrad * silu_grad(z)).astype(jnp.bfloat16)
    grad_in = jnp.dot(nb.T, dz, preferred_element_type=jnp.float32)
    grad_out = jnp.dot(dp.T, hb, preferred_element_type=jnp.float32)
    dn = jnp.dot(dz, w_in.T, preferred_element_type=jnp.float32)
    branch = (dn - lax.optimization_barrier(jnp.mean(dn, axis=1, keepdims=True)) - nf * lax.optimization_barrier(jnp.mean(dn * nf, axis=1, keepdims=True))) * rstd
    dxp = (dp.astype(jnp.float32) + branch).astype(jnp.bfloat16)
    return (dxp, grad_in, grad_out, index)

def reference(events, cotangent, w_in, w_out, slot_source, slot_length):
    x_flat = events.reshape(NSEQ * SEQ_LEN, D)
    d_flat = cotangent.reshape(NSEQ * SEQ_LEN, D)
    sources = slot_source.reshape(N_USER, HIST_DEV)
    lengths = slot_length.reshape(N_USER, HIST_DEV)

    def step(carry, item):
        acc_in, acc_out = carry
        dxp, grad_in, grad_out, index = host_pass(x_flat, d_flat, w_in, w_out, item[0], item[1])
        return ((acc_in + grad_in, acc_out + grad_out), (dxp, index))
    start = (jnp.zeros((D, 4 * D), jnp.float32), jnp.zeros((D, D), jnp.float32))
    (grad_w_in, grad_w_out), (dxs, indices) = lax.scan(step, start, (lengths, sources))
    grad_x = jnp.zeros((NSEQ * SEQ_LEN, D), jnp.bfloat16).at[indices.reshape(-1)].set(dxs.reshape(-1, D))
    return (grad_x.reshape(NSEQ, SEQ_LEN, D), grad_w_in, grad_w_out)
```

```python
import functools

import jax
import jax.numpy as jnp
from jax import lax
from jax.experimental import pallas as pl
from jax.experimental.pallas import tpu as pltpu
from jax.sharding import PartitionSpec as P

HEAD_DIM = 128
SEQ_LEN = 128
GROUPS = 4
TILE = 2

eps = 1e-05
f32 = jnp.float32
bf16 = jnp.bfloat16


def dot_nn(a, b):
    return lax.dot_general(a, b, (((1,), (0,)), ((), ())), preferred_element_type=f32)


def dot_nt(a, b):
    return lax.dot_general(a, b, (((1,), (1,)), ((), ())), preferred_element_type=f32)


def dot_tn(a, b):
    return lax.dot_general(a, b, (((0,), (0,)), ((), ())), preferred_element_type=f32)


def sigmoid(t):
    return 0.5 * jnp.tanh(0.5 * t) + 0.5


def row_mean(t):
    return jnp.mean(t, axis=1, keepdims=True)


def history_pass(u, v, q, k, dh, causal):
    scale = HEAD_DIM ** (-0.5)
    s = dot_nt(q, k) * scale
    sig = sigmoid(s)
    silu = s * sig
    attn = jnp.where(causal, silu * (1.0 / SEQ_LEN), 0.0).astype(bf16)
    y = dot_nn(attn, v)
    cen = y - row_mean(y)
    rstd = lax.rsqrt(row_mean(cen * cen) + eps)
    yn = cen * rstd
    uf = u.astype(f32)
    hb = (yn * uf).astype(bf16)
    grad_u = dh * yn
    dyn = dh * uf
    dy = ((dyn - row_mean(dyn) - yn * row_mean(dyn * yn)) * rstd).astype(bf16)
    grad_a = dot_nt(dy, v)
    grad_v = dot_tn(attn, dy)
    slope = sig + silu * (1.0 - sig)
    grad_s = jnp.where(causal, grad_a * slope * (scale / SEQ_LEN), 0.0).astype(bf16)
    grad_q = dot_nn(grad_s, k)
    grad_k = dot_tn(grad_s, q)
    return hb, (grad_u, grad_v, grad_q, grad_k)


def group_kernel(first, last, heads, parts, *refs):
    refs = list(refs)
    lens_ref, part_ref, xo_ref, xr_ref, do_ref, dr_ref, w_hbm = refs[:7]
    refs = refs[7:]
    acc_hbm = None if first else refs.pop(0)
    gx_ref, bs_ref, grad_hbm, w_s, acc_s, nb_s, dm_s, dz_s, hb_s, out_s, sems = refs
    rows, own = xo_ref.shape
    width = own * parts
    cols_in = heads * 4 * HEAD_DIM
    cols = cols_in + heads * HEAD_DIM
    me = part_ref[0]

    def place(p):
        return pl.ds(pl.multiple_of(lax.rem(me + p, parts) * own, own), own)

    loads = []
    for p in range(parts):
        loads.append(
            pltpu.make_async_copy(
                w_hbm.at[place(p)], w_s.at[pl.ds(p * own, own)], sems.at[p]
            )
        )
        loads[-1].start()
    if not first:
        acc_load = pltpu.make_async_copy(acc_hbm, acc_s, sems.at[parts])
        acc_load.start()

    tr = min(TILE * SEQ_LEN, rows)
    causal = lax.broadcasted_iota(jnp.int32, (SEQ_LEN, SEQ_LEN), 0) >= lax.broadcasted_iota(
        jnp.int32, (SEQ_LEN, SEQ_LEN), 1
    )
    position = lax.broadcasted_iota(jnp.int32, (SEQ_LEN, 1), 0)

    for copy in loads:
        copy.wait()

    @pl.loop(0, rows // tr)
    def _(i):
        here = pl.ds(pl.multiple_of(i * tr, tr), tr)
        xo = xo_ref[here, :].astype(f32)
        xr = xr_ref[here, :].astype(f32)
        mean = (jnp.sum(xo, axis=1, keepdims=True) + jnp.sum(xr, axis=1, keepdims=True)) / width
        xo = xo - mean
        xr = xr - mean
        var = (
            jnp.sum(xo * xo, axis=1, keepdims=True) + jnp.sum(xr * xr, axis=1, keepdims=True)
        ) / width
        rstd = lax.rsqrt(var + eps)
        nb_s[here, :own] = (xo * rstd).astype(bf16)
        nb_s[here, own:] = (xr * rstd).astype(bf16)
        valid = jnp.concatenate(
            [position < lens_ref[i * (tr // SEQ_LEN) + n] for n in range(tr // SEQ_LEN)], axis=0
        )
        dm_s[here, :own] = jnp.where(valid, do_ref[here, :].astype(f32), 0.0).astype(bf16)
        dm_s[here, own:] = jnp.where(valid, dr_ref[here, :].astype(f32), 0.0).astype(bf16)
        dh = dot_nn(dm_s[here, :], w_s[:, cols_in:])
        for h in range(heads):
            c = h * 4 * HEAD_DIM
            z = dot_nn(nb_s[here, :], w_s[:, c : c + 4 * HEAD_DIM])
            sig = sigmoid(z)
            silu = z * sig
            slope = sig + silu * (1.0 - sig)
            g = silu.astype(bf16)
            for n in range(tr // SEQ_LEN):
                a, b = n * SEQ_LEN, (n + 1) * SEQ_LEN
                u, v, q, k = [g[a:b, e * HEAD_DIM : (e + 1) * HEAD_DIM] for e in range(4)]
                hb, grads = history_pass(
                    u, v, q, k, dh[a:b, h * HEAD_DIM : (h + 1) * HEAD_DIM], causal
                )
                there = pl.ds(pl.multiple_of(i * tr + a, SEQ_LEN), SEQ_LEN)
                hb_s[there, h * HEAD_DIM : (h + 1) * HEAD_DIM] = hb
                for e in range(4):
                    dz_s[there, c + e * HEAD_DIM : c + (e + 1) * HEAD_DIM] = (
                        grads[e] * slope[a:b, e * HEAD_DIM : (e + 1) * HEAD_DIM]
                    ).astype(bf16)
        dn = dot_nt(dz_s[here, :], w_s[:, :cols_in])
        no = xo * rstd
        nr = xr * rstd
        one = jnp.sum(dn, axis=1, keepdims=True) / width
        two = (
            jnp.sum(dn[:, :own] * no, axis=1, keepdims=True)
            + jnp.sum(dn[:, own:] * nr, axis=1, keepdims=True)
        ) / width
        gx_ref[here, :] = (
            dm_s[here, :own].astype(f32) + (dn[:, :own] - one - no * two) * rstd
        ).astype(bf16)
        bs_ref[here, :] = ((dn[:, own:] - one - nr * two) * rstd).astype(bf16)

    if not first:
        acc_load.wait()
    target = out_s if last else acc_s
    block = 4 * HEAD_DIM

    def add(lhs, rhs, lo, size):
        for r in range(0, width, 256):
            term = dot_tn(lhs[:, r : r + 256], rhs)
            if not first:
                term = term + acc_s[r : r + 256, pl.ds(lo, size)]
            target[r : r + 256, pl.ds(lo, size)] = term.astype(target.dtype)

    @pl.loop(0, cols_in // block)
    def _(j):
        lo = pl.multiple_of(j * block, block)
        add(nb_s, dz_s[:, pl.ds(lo, block)], lo, block)

    add(dm_s, hb_s[...], cols_in, cols - cols_in)

    stores = []
    if last:
        for p in range(parts):
            stores.append(
                pltpu.make_async_copy(
                    out_s.at[pl.ds(p * own, own)], grad_hbm.at[place(p)], sems.at[p]
                )
            )
    else:
        stores.append(pltpu.make_async_copy(acc_s, grad_hbm, sems.at[0]))
    for copy in stores:
        copy.start()
    for copy in stores:
        copy.wait()


def group_call(first, last, lens, part, xo, xr, do, dr, weights, acc):
    rows, own = xo.shape
    width, cols = weights.shape
    parts = width // own
    heads = cols // (5 * HEAD_DIM)
    whole = pl.BlockSpec(memory_space=pltpu.VMEM)
    smem = pl.BlockSpec(memory_space=pltpu.SMEM)
    anywhere = pl.BlockSpec(memory_space=pl.ANY)
    args = [lens, part, xo, xr, do, dr, weights] + ([] if first else [acc])
    specs = [smem, smem] + [whole] * 4 + [anywhere] * (1 if first else 2)
    kind = bf16 if last else f32
    flops = 2 * rows * width * cols * 2 + 2 * rows * width * heads * 4 * HEAD_DIM
    return pl.pallas_call(
        functools.partial(group_kernel, first, last, heads, parts),
        out_shape=(
            jax.ShapeDtypeStruct((rows, own), bf16),
            jax.ShapeDtypeStruct((rows, width - own), bf16),
            jax.ShapeDtypeStruct((width, cols), kind),
        ),
        in_specs=specs,
        out_specs=(whole, whole, anywhere),
        scratch_shapes=[
            pltpu.VMEM((width, cols), bf16),
            pltpu.VMEM((width, cols), f32),
            pltpu.VMEM((rows, width), bf16),
            pltpu.VMEM((rows, width), bf16),
            pltpu.VMEM((rows, heads * 4 * HEAD_DIM), bf16),
            pltpu.VMEM((rows, heads * HEAD_DIM), bf16),
            pltpu.VMEM((width, cols) if last else (16, 128), bf16),
            pltpu.SemaphoreType.DMA((parts + 1,)),
        ],
        compiler_params=pltpu.CompilerParams(vmem_limit_bytes=52 * 2**20),
        cost_estimate=pl.CostEstimate(
            flops=flops, bytes_accessed=16 * 2**20, transcendentals=rows * cols
        ),
    )(*args)


def exchange(block, tensor):
    if tensor == 2:
        return lax.ppermute(block, "tensor", [(0, 1), (1, 0)])
    own = block.shape[1]
    every = lax.all_gather(block, "tensor", axis=1, tiled=True)
    return jnp.roll(every, -lax.axis_index("tensor") * own, axis=1)[:, own:]


def give_back(block, own, tensor):
    if tensor == 2:
        return lax.ppermute(block, "tensor", [(0, 1), (1, 0)])
    every = jnp.concatenate([jnp.zeros((block.shape[0], own), block.dtype), block], axis=1)
    every = jnp.roll(every, lax.axis_index("tensor") * own, axis=1)
    return lax.psum_scatter(every, "tensor", scatter_dimension=1, tiled=True)


def local(events, cotangent, w_in, w_out, slot_source, slot_length):
    tensor = lax.axis_size("tensor")
    users = lax.axis_size("user")
    hist, seq_len, own = events.shape
    x = events.reshape(hist * seq_len, own)
    d = cotangent.reshape(hist * seq_len, own)
    rows = hist // GROUPS * seq_len
    xs = [x[g * rows : (g + 1) * rows] for g in range(GROUPS)]
    ds = [d[g * rows : (g + 1) * rows] for g in range(GROUPS)]
    pairs = []
    for g in range(GROUPS):
        pairs.append((exchange(xs[g], tensor), exchange(ds[g], tensor)))

    weights = lax.all_gather(
        jnp.concatenate([w_in, w_out], axis=1), "user", axis=0, tiled=True
    )
    table = lax.all_gather(slot_source * 256 + slot_length, "user", axis=0, tiled=True)
    table = table.reshape(users, hist)
    mine = (table // 256) == lax.axis_index("user")
    lens = jnp.sum(jnp.where(mine, table % 256, 0), axis=0)
    part = lax.axis_index("tensor").astype(jnp.int32).reshape(1)

    acc = None
    kept, sent = [], []
    for g in range(GROUPS):
        xr, dr = pairs[g]
        gx, bs, acc = group_call(
            g == 0,
            g == GROUPS - 1,
            lens[g * hist // GROUPS : (g + 1) * hist // GROUPS],
            part,
            xs[g],
            xr,
            ds[g],
            dr,
            weights,
            acc,
        )
        kept.append(gx)
        sent.append(give_back(bs, own, tensor))
    grads = lax.psum_scatter(acc, "user", scatter_dimension=0, tiled=True).astype(f32)
    grad_x = jnp.concatenate(
        [(k.astype(f32) + s.astype(f32)).astype(bf16) for k, s in zip(kept, sent)], axis=0
    )
    cols_in = w_in.shape[1]
    return (grad_x.reshape(hist, seq_len, own), grads[:, :cols_in], grads[:, cols_in:])


def solution(mesh):
    in_specs = (
        P("user", None, "tensor"),
        P("user", None, "tensor"),
        P("user", "tensor"),
        P("user", "tensor"),
        P("user"),
        P("user"),
    )
    out_specs = (P("user", None, "tensor"), P("user", "tensor"), P("user", "tensor"))
    return jax.shard_map(local, mesh=mesh, in_specs=in_specs, out_specs=out_specs, check_vma=False)
```

```python
import functools

import jax
import jax.numpy as jnp
from jax import lax
from jax.experimental import pallas as pl
from jax.experimental.pallas import tpu as pltpu
from jax.sharding import PartitionSpec as P

HEAD_DIM = 128
SEQ_LEN = 128
GROUPS = 4

eps = 1e-05
f32 = jnp.float32
bf16 = jnp.bfloat16


def dot_nn(a, b):
    return lax.dot_general(a, b, (((1,), (0,)), ((), ())), preferred_element_type=f32)


def dot_nt(a, b):
    return lax.dot_general(a, b, (((1,), (1,)), ((), ())), preferred_element_type=f32)


def dot_tn(a, b):
    return lax.dot_general(a, b, (((0,), (0,)), ((), ())), preferred_element_type=f32)


def sigmoid(t):
    return 0.5 * jnp.tanh(0.5 * t) + 0.5


def row_mean(t):
    return jnp.mean(t, axis=1, keepdims=True)


def attention(pairs, causal, g_s, dh_s, slope_s, hb_s, dz_s):
    scale = HEAD_DIM ** (-0.5)
    spans = [pl.ds(n * SEQ_LEN, SEQ_LEN) for _, n in pairs]
    lanes = [[pl.ds((4 * h + e) * HEAD_DIM, HEAD_DIM) for e in range(4)] for h, _ in pairs]
    heads = [pl.ds(h * HEAD_DIM, HEAD_DIM) for h, _ in pairs]
    every = range(len(pairs))

    def part(i, e):
        return g_s[spans[i], lanes[i][e]]

    s = [dot_nt(part(i, 2), part(i, 3)) * scale for i in every]
    sig = [sigmoid(t) for t in s]
    silu = [s[i] * sig[i] for i in every]
    attn = [jnp.where(causal, t * (1.0 / SEQ_LEN), 0.0).astype(bf16) for t in silu]
    slope = [
        jnp.where(causal, (sig[i] + silu[i] * (1.0 - sig[i])) * (scale / SEQ_LEN), 0.0)
        for i in every
    ]
    y = [dot_nn(attn[i], part(i, 1)) for i in every]
    cen = [t - row_mean(t) for t in y]
    rstd = [lax.rsqrt(row_mean(t * t) + eps) for t in cen]
    yn = [cen[i] * rstd[i] for i in every]
    uf = [part(i, 0).astype(f32) for i in every]
    dh = [dh_s[spans[i], heads[i]] for i in every]
    dyn = [dh[i] * uf[i] for i in every]
    one = [row_mean(t) for t in dyn]
    two = [row_mean(dyn[i] * yn[i]) for i in every]
    dy = [((dyn[i] - one[i] - yn[i] * two[i]) * rstd[i]).astype(bf16) for i in every]
    grad_a = [dot_nt(dy[i], part(i, 1)) for i in every]
    ds = [(grad_a[i] * slope[i]).astype(bf16) for i in every]

    def store(i, e, grad):
        dz_s[spans[i], lanes[i][e]] = (grad * slope_s[spans[i], lanes[i][e]]).astype(bf16)

    for i in every:
        hb_s[spans[i], heads[i]] = (yn[i] * uf[i]).astype(bf16)
        store(i, 0, dh[i] * yn[i])
    for i in every:
        store(i, 1, dot_tn(attn[i], dy[i]))
    for i in every:
        store(i, 2, dot_nn(ds[i], part(i, 3)))
    for i in every:
        store(i, 3, dot_tn(ds[i], part(i, 2)))


def split_order(count):
    rest = sorted(range(1, count), key=lambda j: abs(j - count / 2))
    return rest + [0]


def group_kernel(number, first, last, heads, parts, users, *refs):
    refs = list(refs)
    lens_ref, where_ref, xo_ref, do_ref, far_ref, w_hbm = refs[:6]
    refs = refs[6:]
    acc_hbm = None if first else refs.pop(0)
    gx_ref, bs_ref = refs[:2]
    refs = refs[2:]
    grads_hbm = [refs.pop(0) for _ in range(3 if last else 1)]
    (w_s, acc_s, nb_s, nt_s, dm_s, dt_s, dz_s, hb_s, g_s, slope_s, dh_s, out_s, sems) = refs
    rows, own = xo_ref.shape
    width = own * parts
    cols_in = heads * 4 * HEAD_DIM
    histories = rows // SEQ_LEN
    me, user = where_ref[0], where_ref[1]

    loads = []
    for p in range(parts):
        source = pl.ds(pl.multiple_of(lax.rem(me + p, parts) * own, own), own)
        loads.append(
            pltpu.make_async_copy(w_hbm.at[source], w_s.at[pl.ds(p * own, own)], sems.at[p])
        )
        loads[-1].start()
    if not first:
        acc_load = pltpu.make_async_copy(acc_hbm, acc_s, sems.at[parts])
        acc_load.start()

    causal = lax.broadcasted_iota(jnp.int32, (SEQ_LEN, SEQ_LEN), 0) >= lax.broadcasted_iota(
        jnp.int32, (SEQ_LEN, SEQ_LEN), 1
    )
    position = lax.broadcasted_iota(jnp.int32, (SEQ_LEN, 1), 0)
    half = min(2 * SEQ_LEN, rows)
    halves = [slice(lo, lo + half) for lo in range(0, rows, half)]

    norms = []
    for here in halves:
        xo = xo_ref[here, :].astype(f32)
        xr = far_ref[here, :].astype(f32)
        mean = (jnp.sum(xo, axis=1, keepdims=True) + jnp.sum(xr, axis=1, keepdims=True)) / width
        xo = xo - mean
        xr = xr - mean
        var = (
            jnp.sum(xo * xo, axis=1, keepdims=True) + jnp.sum(xr * xr, axis=1, keepdims=True)
        ) / width
        rstd = lax.rsqrt(var + eps)
        norms.append((mean, rstd))
        bo = (xo * rstd).astype(bf16)
        br = (xr * rstd).astype(bf16)
        nb_s[here, :own] = bo
        nb_s[here, own:] = br
        nt_s[:own, here] = bo.T
        nt_s[own:, here] = br.T
    for copy in loads:
        copy.wait()
    for h in range(heads):
        c = slice(h * 4 * HEAD_DIM, (h + 1) * 4 * HEAD_DIM)
        z = dot_nn(nb_s[...], w_s[:, c])
        sig = sigmoid(z)
        silu = z * sig
        g_s[:, c] = silu.astype(bf16)
        slope_s[:, c] = sig + silu * (1.0 - sig)
    for here in halves:
        valid = jnp.concatenate(
            [
                position < lens_ref[number * histories + n]
                for n in range(here.start // SEQ_LEN, here.stop // SEQ_LEN)
            ],
            axis=0,
        )
        there = slice(rows + here.start, rows + here.stop)
        do = jnp.where(valid, do_ref[here, :].astype(f32), 0.0).astype(bf16)
        dr = jnp.where(valid, far_ref[there, :].astype(f32), 0.0).astype(bf16)
        dm_s[here, :own] = do
        dm_s[here, own:] = dr
        dt_s[:own, here] = do.T
        dt_s[own:, here] = dr.T
    dh_s[...] = dot_nn(dm_s[...], w_s[:, cols_in:])

    if not first:
        acc_load.wait()
    target = out_s if last else acc_s

    def add(lhs, rhs, lo, size):
        for r in range(0, width, 256):
            term = dot_nn(lhs[r : r + 256, :], rhs[...])
            if not first:
                term = term + acc_s[r : r + 256, lo : lo + size]
            target[r : r + 256, lo : lo + size] = term.astype(target.dtype)

    block = 4 * HEAD_DIM
    step = max(1, 8 // histories)
    for lo in range(0, heads, step):
        hi = min(lo + step, heads)
        pairs = [(h, n) for h in range(lo, hi) for n in range(histories)]
        attention(pairs, causal, g_s, dh_s, slope_s, hb_s, dz_s)
        if lo > 0:
            for h in range(lo - step, lo):
                add(nt_s, dz_s.at[:, h * block : (h + 1) * block], h * block, block)
    for here, (mean, rstd) in zip(halves, norms):
        dn = dot_nt(dz_s[here, :], w_s[:, :cols_in])
        no = (xo_ref[here, :].astype(f32) - mean) * rstd
        nr = (far_ref[here, :].astype(f32) - mean) * rstd
        one = jnp.sum(dn, axis=1, keepdims=True) / width
        two = (
            jnp.sum(dn[:, :own] * no, axis=1, keepdims=True)
            + jnp.sum(dn[:, own:] * nr, axis=1, keepdims=True)
        ) / width
        gx_ref[here, :] = (
            dm_s[here, :own].astype(f32) + (dn[:, :own] - one - no * two) * rstd
        ).astype(bf16)
        bs_ref[here, :] = ((dn[:, own:] - one - nr * two) * rstd).astype(bf16)
    for h in range(max(0, heads - step), heads):
        add(nt_s, dz_s.at[:, h * block : (h + 1) * block], h * block, block)
    add(dt_s, hb_s, cols_in, heads * HEAD_DIM)

    stores = []
    if last:
        keep, send_a, send_b = grads_hbm
        size = width // users
        far = users // 4
        zi, xi, ci = user // 4, lax.rem(user // 2, 2), lax.rem(user, 2)
        for at, j in enumerate(split_order(far)):
            zd = lax.rem(zi + far - j, far)
            for xs in range(2):
                xd = xi if xs == 0 else 1 - xi
                for cs in range(2):
                    cd = ci if cs == 0 else 1 - ci
                    row = ((zd * 2 + xd) * 2 + cd) * size
                    row = lax.rem(row // own - me + parts, parts) * own + lax.rem(row, own)
                    slot = at * 2 + xs
                    there = keep
                    if cs == 1:
                        there = send_a if slot < far else send_b
                        slot = slot % far
                    stores.append(
                        pltpu.make_async_copy(
                            out_s.at[pl.ds(pl.multiple_of(row, size), size)],
                            there.at[pl.ds(slot * size, size)],
                            sems.at[len(stores)],
                        )
                    )
    else:
        stores.append(pltpu.make_async_copy(acc_s, grads_hbm[0], sems.at[0]))
    for copy in stores:
        copy.start()
    for copy in stores:
        copy.wait()


def group_call(number, count, users, lens, where, x, d, far, weights, acc):
    first, last = number == 0, number == count - 1
    rows, own = x.shape[0] // count, x.shape[1]
    width, cols = weights.shape
    parts = width // own
    heads = cols // (5 * HEAD_DIM)
    cols_in = heads * 4 * HEAD_DIM
    smem = pl.BlockSpec(memory_space=pltpu.SMEM)
    anywhere = pl.BlockSpec(memory_space=pl.ANY)
    mine = pl.BlockSpec((rows, own), lambda i: (number, 0))
    theirs = pl.BlockSpec(far.shape, lambda i: (0, 0))
    args = [lens, where, x, d, far, weights] + ([] if first else [acc])
    specs = [smem, smem, mine, mine, theirs] + [anywhere] * (1 if first else 2)
    if last:
        grads = [
            jax.ShapeDtypeStruct((width // 2, cols), bf16),
            jax.ShapeDtypeStruct((width // 4, cols), bf16),
            jax.ShapeDtypeStruct((width // 4, cols), bf16),
        ]
    else:
        grads = [jax.ShapeDtypeStruct((width, cols), f32)]
    flops = 4 * rows * width * cols + 2 * rows * width * cols_in
    return pl.pallas_call(
        functools.partial(group_kernel, number, first, last, heads, parts, users),
        grid=(1,),
        out_shape=[
            jax.ShapeDtypeStruct((rows, own), bf16),
            jax.ShapeDtypeStruct((rows, width - own), bf16),
        ]
        + grads,
        in_specs=specs,
        out_specs=[
            pl.BlockSpec((rows, own), lambda i: (0, 0)),
            pl.BlockSpec((rows, width - own), lambda i: (0, 0)),
        ]
        + [anywhere] * len(grads),
        scratch_shapes=[
            pltpu.VMEM((width, cols), bf16),
            pltpu.VMEM((width, cols), f32),
            pltpu.VMEM((rows, width), bf16),
            pltpu.VMEM((width, rows), bf16),
            pltpu.VMEM((rows, width), bf16),
            pltpu.VMEM((width, rows), bf16),
            pltpu.VMEM((rows, cols_in), bf16),
            pltpu.VMEM((rows, cols - cols_in), bf16),
            pltpu.VMEM((rows, cols_in), bf16),
            pltpu.VMEM((rows, cols_in), f32),
            pltpu.VMEM((rows, cols - cols_in), f32),
            pltpu.VMEM((width, cols) if last else (16, 128), bf16),
            pltpu.SemaphoreType.DMA((max(users, parts + 1),)),
        ],
        compiler_params=pltpu.CompilerParams(vmem_limit_bytes=56 * 2**20),
        cost_estimate=pl.CostEstimate(
            flops=flops, bytes_accessed=16 * 2**20, transcendentals=rows * cols
        ),
    )(*args)


def scatter_sum(keep, send_a, send_b, users):
    far = users // 4
    size = keep.shape[0] // (2 * far)

    def swap(bit):
        return [(i, i ^ bit) for i in range(users)]

    got = [lax.ppermute(t, "user", swap(1)) for t in (send_a, send_b)]

    def mine(at, xs):
        slot = at * 2 + xs
        other = got[0] if slot < far else got[1]
        low = slot % far * size
        return keep[slot * size : (slot + 1) * size].astype(f32) + other[low : low + size].astype(
            f32
        )

    total = None
    for at, j in enumerate(split_order(far)):
        across = lax.ppermute(mine(at, 1).astype(bf16), "user", swap(2))
        block = mine(at, 0) + across.astype(f32)
        if j == 0:
            return sum(total, block)
        pairs = [(i, (i - 4 * j) % users) for i in range(users)]
        moved = lax.ppermute(block.astype(bf16), "user", pairs).astype(f32)
        total = (total or []) + [moved]


def exchange(block, tensor):
    if tensor == 2:
        return lax.ppermute(block, "tensor", [(0, 1), (1, 0)])
    own = block.shape[1]
    every = lax.all_gather(block, "tensor", axis=1, tiled=True)
    return jnp.roll(every, -lax.axis_index("tensor") * own, axis=1)[:, own:]


def give_back(block, own, tensor):
    if tensor == 2:
        return lax.ppermute(block, "tensor", [(0, 1), (1, 0)])
    every = jnp.concatenate([jnp.zeros((block.shape[0], own), block.dtype), block], axis=1)
    every = jnp.roll(every, lax.axis_index("tensor") * own, axis=1)
    return lax.psum_scatter(every, "tensor", scatter_dimension=1, tiled=True)


def local(events, cotangent, w_in, w_out, slot_source, slot_length):
    tensor = lax.axis_size("tensor")
    users = lax.axis_size("user")
    hist, seq_len, own = events.shape
    x = events.reshape(hist * seq_len, own)
    d = cotangent.reshape(hist * seq_len, own)
    rows = hist // GROUPS * seq_len
    far = []
    for g in range(GROUPS):
        span = slice(g * rows, (g + 1) * rows)
        far.append(exchange(jnp.concatenate([x[span], d[span]], axis=0), tensor))

    weights = lax.all_gather(
        jnp.concatenate([w_in, w_out], axis=1), "user", axis=0, tiled=True
    )
    table = lax.all_gather(slot_source * 256 + slot_length, "user", axis=0, tiled=True)
    table = table.reshape(users, hist)
    user = lax.axis_index("user")
    lens = jnp.sum(jnp.where(table // 256 == user, table % 256, 0), axis=0)
    where = jnp.stack([lax.axis_index("tensor"), user]).astype(jnp.int32)

    acc = []
    kept, sent = [], []
    for g in range(GROUPS):
        gx, bs, *acc = group_call(
            g, GROUPS, users, lens, where, x, d, far[g], weights, acc[0] if acc else None
        )
        kept.append(gx)
        sent.append(give_back(bs, own, tensor))
    grads = scatter_sum(*acc, users)
    grad_x = jnp.concatenate(
        [(k.astype(f32) + s.astype(f32)).astype(bf16) for k, s in zip(kept, sent)], axis=0
    )
    cols_in = w_in.shape[1]
    return (grad_x.reshape(hist, seq_len, own), grads[:, :cols_in], grads[:, cols_in:])


def solution(mesh):
    in_specs = (
        P("user", None, "tensor"),
        P("user", None, "tensor"),
        P("user", "tensor"),
        P("user", "tensor"),
        P("user"),
        P("user"),
    )
    out_specs = (P("user", None, "tensor"), P("user", "tensor"), P("user", "tensor"))
    return jax.shard_map(local, mesh=mesh, in_specs=in_specs, out_specs=out_specs, check_vma=False)
```

```python
import functools

import jax
import jax.numpy as jnp
from jax import lax
from jax.experimental import pallas as pl
from jax.experimental.pallas import tpu as pltpu
from jax.sharding import PartitionSpec as P

HEAD_DIM = 128
SEQ_LEN = 128
GROUPS = ((0, 2), (2, 1), (3, 1))

eps = 1e-05
f32 = jnp.float32
bf16 = jnp.bfloat16


def dot_nn(a, b):
    return lax.dot_general(a, b, (((1,), (0,)), ((), ())), preferred_element_type=f32)


def dot_nt(a, b):
    return lax.dot_general(a, b, (((1,), (1,)), ((), ())), preferred_element_type=f32)


def dot_tn(a, b):
    return lax.dot_general(a, b, (((0,), (0,)), ((), ())), preferred_element_type=f32)


def sigmoid(t):
    return 0.5 * jnp.tanh(0.5 * t) + 0.5


def row_mean(t):
    return jnp.mean(t, axis=1, keepdims=True)


def attention(pairs, causal, g_s, dh_s, slope_s, hb_s, dz_s):
    scale = HEAD_DIM ** (-0.5)
    spans = [pl.ds(n * SEQ_LEN, SEQ_LEN) for _, n in pairs]
    lanes = [[pl.ds((4 * h + e) * HEAD_DIM, HEAD_DIM) for e in range(4)] for h, _ in pairs]
    heads = [pl.ds(h * HEAD_DIM, HEAD_DIM) for h, _ in pairs]
    every = range(len(pairs))

    def part(i, e):
        return g_s[spans[i], lanes[i][e]]

    s = [dot_nt(part(i, 2), part(i, 3)) * scale for i in every]
    sig = [sigmoid(t) for t in s]
    silu = [s[i] * sig[i] for i in every]
    attn = [jnp.where(causal, t * (1.0 / SEQ_LEN), 0.0).astype(bf16) for t in silu]
    slope = [
        jnp.where(causal, (sig[i] + silu[i] * (1.0 - sig[i])) * (scale / SEQ_LEN), 0.0)
        for i in every
    ]
    y = [dot_nn(attn[i], part(i, 1)) for i in every]
    cen = [t - row_mean(t) for t in y]
    rstd = [lax.rsqrt(row_mean(t * t) + eps) for t in cen]
    yn = [cen[i] * rstd[i] for i in every]
    uf = [part(i, 0).astype(f32) for i in every]
    dh = [dh_s[spans[i], heads[i]] for i in every]
    dyn = [dh[i] * uf[i] for i in every]
    one = [row_mean(t) for t in dyn]
    two = [row_mean(dyn[i] * yn[i]) for i in every]
    dy = [((dyn[i] - one[i] - yn[i] * two[i]) * rstd[i]).astype(bf16) for i in every]
    grad_a = [dot_nt(dy[i], part(i, 1)) for i in every]
    ds = [(grad_a[i] * slope[i]).astype(bf16) for i in every]

    def store(i, e, grad):
        dz_s[spans[i], lanes[i][e]] = (grad * slope_s[spans[i], lanes[i][e]]).astype(bf16)

    for i in every:
        hb_s[spans[i], heads[i]] = (yn[i] * uf[i]).astype(bf16)
        store(i, 0, dh[i] * yn[i])
    for i in every:
        store(i, 1, dot_tn(attn[i], dy[i]))
    for i in every:
        store(i, 2, dot_nn(ds[i], part(i, 3)))
    for i in every:
        store(i, 3, dot_tn(ds[i], part(i, 2)))


def split_order(count):
    rest = sorted(range(1, count), key=lambda j: abs(j - count / 2))
    return rest + [0]


def group_kernel(start, steps, first, last, heads, parts, users, *refs):
    refs = list(refs)
    lens_ref, where_ref, xo_ref, do_ref, far_ref, w_hbm = refs[:6]
    refs = refs[6:]
    acc_hbm = None if first else refs.pop(0)
    gx_ref, bs_ref = refs[:2]
    refs = refs[2:]
    grads_hbm = [refs.pop(0) for _ in range(2 if last else 1)]
    (w_s, acc_s, nb_s, nt_s, dm_s, dt_s, dz_s, hb_s, g_s, slope_s, dh_s, out_s) = refs[:12]
    load_sems, store_sems = refs[12:]
    rows, own = xo_ref.shape
    width = own * parts
    cols_in = heads * 4 * HEAD_DIM
    histories = rows // SEQ_LEN
    me, user = where_ref[0], where_ref[1]
    step = pl.program_id(0)

    def only(index, run):
        if steps == 1:
            run()
        else:
            pl.when(step == index)(run)

    loads = []
    for p in range(parts):
        source = pl.ds(pl.multiple_of(lax.rem(me + p, parts) * own, own), own)
        loads.append(
            pltpu.make_async_copy(w_hbm.at[source], w_s.at[pl.ds(p * own, own)], load_sems.at[p])
        )
    if not first:
        acc_load = pltpu.make_async_copy(acc_hbm, acc_s, load_sems.at[parts])

    def begin():
        for copy in loads:
            copy.start()
        if first:
            acc_s[...] = jnp.zeros_like(acc_s)
        else:
            acc_load.start()

    def loaded():
        for copy in loads:
            copy.wait()

    only(0, begin)

    causal = lax.broadcasted_iota(jnp.int32, (SEQ_LEN, SEQ_LEN), 0) >= lax.broadcasted_iota(
        jnp.int32, (SEQ_LEN, SEQ_LEN), 1
    )
    position = lax.broadcasted_iota(jnp.int32, (SEQ_LEN, 1), 0)
    half = min(2 * SEQ_LEN, rows)
    halves = [slice(lo, lo + half) for lo in range(0, rows, half)]

    rstds = []
    for here in halves:
        xo = xo_ref[here, :].astype(f32)
        xr = far_ref[here, :].astype(f32)
        mean = (jnp.sum(xo, axis=1, keepdims=True) + jnp.sum(xr, axis=1, keepdims=True)) / width
        xo = xo - mean
        xr = xr - mean
        var = (
            jnp.sum(xo * xo, axis=1, keepdims=True) + jnp.sum(xr * xr, axis=1, keepdims=True)
        ) / width
        rstd = lax.rsqrt(var + eps)
        rstds.append(rstd)
        bo = (xo * rstd).astype(bf16)
        br = (xr * rstd).astype(bf16)
        nb_s[here, :own] = bo
        nb_s[here, own:] = br
        nt_s[:own, here] = bo.T
        nt_s[own:, here] = br.T
    only(0, loaded)
    for h in range(heads):
        c = slice(h * 4 * HEAD_DIM, (h + 1) * 4 * HEAD_DIM)
        z = dot_nn(nb_s[...], w_s[:, c])
        sig = sigmoid(z)
        silu = z * sig
        g_s[:, c] = silu.astype(bf16)
        slope_s[:, c] = sig + silu * (1.0 - sig)
    for here in halves:
        base = start * histories + step * histories
        valid = jnp.concatenate(
            [
                (position < lens_ref[base + n]).astype(f32)
                for n in range(here.start // SEQ_LEN, here.stop // SEQ_LEN)
            ],
            axis=0,
        ).astype(bf16)
        there = slice(rows + here.start, rows + here.stop)
        do = do_ref[here, :] * valid
        dr = far_ref[there, :] * valid
        dm_s[here, :own] = do
        dm_s[here, own:] = dr
        dt_s[:own, here] = do.T
        dt_s[own:, here] = dr.T
    dh_s[...] = dot_nn(dm_s[...], w_s[:, cols_in:])

    if not first:
        only(0, acc_load.wait)
    target = out_s if last else acc_s
    size = width // users
    far = users // 4
    zi, xi, ci = user // 4, lax.rem(user // 2, 2), lax.rem(user, 2)
    stores = []

    def ship(lo, wide):
        lanes = pl.ds(lo, wide)
        if not last:
            stores.append(
                pltpu.make_async_copy(
                    acc_s.at[:, lanes], grads_hbm[0].at[:, lanes], store_sems.at[len(stores)]
                )
            )
            only(steps - 1, stores[-1].start)
            return
        keep, send = grads_hbm
        for at, j in enumerate(split_order(far)):
            zd = lax.rem(zi + far - j, far)
            for xs in range(2):
                xd = xi if xs == 0 else 1 - xi
                for cs in range(2):
                    cd = ci if cs == 0 else 1 - ci
                    row = ((zd * 2 + xd) * 2 + cd) * size
                    row = lax.rem(row // own - me + parts, parts) * own + lax.rem(row, own)
                    slot = xs * far + at
                    there = keep if cs == 0 else send
                    stores.append(
                        pltpu.make_async_copy(
                            out_s.at[pl.ds(pl.multiple_of(row, size), size), lanes],
                            there.at[pl.ds(slot * size, size), lanes],
                            store_sems.at[len(stores)],
                        )
                    )
                    only(steps - 1, stores[-1].start)

    def add(lhs, rhs, lo, wide):
        chunk = min(512, width)
        for r in range(0, width, chunk):
            term = dot_nn(lhs[r : r + chunk, :], rhs[...]) + acc_s[r : r + chunk, lo : lo + wide]
            target[r : r + chunk, lo : lo + wide] = term.astype(target.dtype)
        ship(lo, wide)

    block = 4 * HEAD_DIM
    stride = max(1, 8 // histories)
    for lo in range(0, heads, stride):
        hi = min(lo + stride, heads)
        pairs = [(h, n) for h in range(lo, hi) for n in range(histories)]
        attention(pairs, causal, g_s, dh_s, slope_s, hb_s, dz_s)
        for h in range(max(0, lo - stride), lo):
            add(nt_s, dz_s.at[:, h * block : (h + 1) * block], h * block, block)
    dn_all = dot_nt(dz_s[...], w_s[:, :cols_in])
    add(dt_s, hb_s, cols_in, heads * HEAD_DIM)
    for here, rstd in zip(halves, rstds):
        dn = dn_all[here, :]
        nf = nb_s[here, :].astype(f32)
        one = jnp.sum(dn, axis=1, keepdims=True) / width
        two = jnp.sum(dn * nf, axis=1, keepdims=True) / width
        branch = (dn - one - nf * two) * rstd
        gx_ref[here, :] = (dm_s[here, :own].astype(f32) + branch[:, :own]).astype(bf16)
        bs_ref[here, :] = branch[:, own:].astype(bf16)
    for h in range((heads - 1) // stride * stride, heads):
        add(nt_s, dz_s.at[:, h * block : (h + 1) * block], h * block, block)

    for copy in stores:
        only(steps - 1, copy.wait)


def group_call(group, blocks, users, lens, where, x, d, far, weights, acc):
    start, steps = group
    first, last = start == 0, start + steps == blocks
    rows, own = x.shape[0] // blocks, x.shape[1]
    width, cols = weights.shape
    parts = width // own
    heads = cols // (5 * HEAD_DIM)
    cols_in = heads * 4 * HEAD_DIM
    smem = pl.BlockSpec(memory_space=pltpu.SMEM)
    anywhere = pl.BlockSpec(memory_space=pl.ANY)
    mine = pl.BlockSpec((rows, own), lambda i: (start + i, 0))
    theirs = pl.BlockSpec((2 * rows, width - own), lambda i: (i, 0))
    args = [lens, where, x, d, far, weights] + ([] if first else [acc])
    specs = [smem, smem, mine, mine, theirs] + [anywhere] * (1 if first else 2)
    if last:
        grads = [jax.ShapeDtypeStruct((width // 2, cols), bf16)] * 2
    else:
        grads = [jax.ShapeDtypeStruct((width, cols), f32)]
    flops = steps * (4 * rows * width * cols + 2 * rows * width * cols_in)
    return pl.pallas_call(
        functools.partial(group_kernel, start, steps, first, last, heads, parts, users),
        grid=(steps,),
        out_shape=[
            jax.ShapeDtypeStruct((steps * rows, own), bf16),
            jax.ShapeDtypeStruct((steps * rows, width - own), bf16),
        ]
        + grads,
        in_specs=specs,
        out_specs=[
            pl.BlockSpec((rows, own), lambda i: (i, 0)),
            pl.BlockSpec((rows, width - own), lambda i: (i, 0)),
        ]
        + [anywhere] * len(grads),
        scratch_shapes=[
            pltpu.VMEM((width, cols), bf16),
            pltpu.VMEM((width, cols), f32),
            pltpu.VMEM((rows, width), bf16),
            pltpu.VMEM((width, rows), bf16),
            pltpu.VMEM((rows, width), bf16),
            pltpu.VMEM((width, rows), bf16),
            pltpu.VMEM((rows, cols_in), bf16),
            pltpu.VMEM((rows, cols - cols_in), bf16),
            pltpu.VMEM((rows, cols_in), bf16),
            pltpu.VMEM((rows, cols_in), f32),
            pltpu.VMEM((rows, cols - cols_in), f32),
            pltpu.VMEM((width, cols) if last else (16, 128), bf16),
            pltpu.SemaphoreType.DMA((parts + 1,)),
            pltpu.SemaphoreType.DMA(((users if last else 1) * (heads + 1),)),
        ],
        compiler_params=pltpu.CompilerParams(vmem_limit_bytes=56 * 2**20),
        cost_estimate=pl.CostEstimate(
            flops=flops, bytes_accessed=16 * 2**20, transcendentals=steps * rows * cols
        ),
    )(*args)


def scatter_parts(keep, send, users):
    far = users // 4
    order = split_order(far)
    size = keep.shape[0] // (2 * far)

    def swap(block, bit):
        return lax.ppermute(block, "user", [(i, i ^ bit) for i in range(users)])

    got = swap(send, 1)

    def both(lo, hi):
        span = slice(lo * size, hi * size)
        return keep[span].astype(f32) + got[span].astype(f32)

    cuts = [(0, 1), (1, far - 1), (far - 1, far)]
    across = [swap(both(far + lo, far + hi).astype(bf16), 2) for lo, hi in cuts]
    moved = []
    for (lo, hi), other in zip(cuts[:2], across):
        near = (both(lo, hi) + other.astype(f32)).astype(bf16)
        for at in range(lo, hi):
            pairs = [(i, (i - 4 * order[at]) % users) for i in range(users)]
            block = near[(at - lo) * size : (at - lo + 1) * size]
            moved.append(lax.ppermute(block, "user", pairs))
    return got, [across[2]] + moved


def finish_kernel(spans, cols_in, *refs):
    step = pl.program_id(0)
    rows = refs[: 2 * len(spans)]
    terms = refs[2 * len(spans) : -3]
    gx_ref, win_ref, wout_ref = refs[-3:]
    for (start, steps), kept, sent in zip(spans, rows[::2], rows[1::2]):

        @pl.when((step >= start) & (step < start + steps))
        def _(kept=kept, sent=sent):
            gx_ref[...] = (kept[...].astype(f32) + sent[...].astype(f32)).astype(bf16)

    @pl.when(step == 0)
    def _():
        total = terms[0][...].astype(f32)
        for term in terms[1:]:
            total = total + term[...].astype(f32)
        win_ref[...] = total[:, :cols_in]
        wout_ref[...] = total[:, cols_in:]


def finish(kept, sent, keep, got, rest, cols_in):
    blocks = sum(steps for _, steps in GROUPS)
    own = kept[0].shape[1]
    rows = sum(k.shape[0] for k in kept) // blocks
    size, cols = rest[0].shape
    slot = keep.shape[0] // (2 * size) - 1
    specs, args = [], []
    for (start, steps), k, t in zip(GROUPS, kept, sent):
        spec = pl.BlockSpec(
            (rows, own), lambda i, a=start, n=steps: (jnp.clip(i - a, 0, n - 1), 0)
        )
        specs += [spec, spec]
        args += [k, t]
    specs += [pl.BlockSpec((size, cols), lambda i: (slot, 0))] * 2
    specs += [pl.BlockSpec((size, cols), lambda i: (0, 0))] * len(rest)
    return pl.pallas_call(
        functools.partial(finish_kernel, GROUPS, cols_in),
        grid=(blocks,),
        out_shape=[
            jax.ShapeDtypeStruct((blocks * rows, own), bf16),
            jax.ShapeDtypeStruct((size, cols_in), f32),
            jax.ShapeDtypeStruct((size, cols - cols_in), f32),
        ],
        in_specs=specs,
        out_specs=[
            pl.BlockSpec((rows, own), lambda i: (i, 0)),
            pl.BlockSpec((size, cols_in), lambda i: (0, 0)),
            pl.BlockSpec((size, cols - cols_in), lambda i: (0, 0)),
        ],
        compiler_params=pltpu.CompilerParams(vmem_limit_bytes=32 * 2**20),
        cost_estimate=pl.CostEstimate(
            flops=blocks * rows * own, bytes_accessed=12 * 2**20, transcendentals=0
        ),
    )(*args, keep, got, *rest)


def exchange(block, tensor):
    if tensor == 2:
        return lax.ppermute(block, "tensor", [(0, 1), (1, 0)])
    own = block.shape[1]
    every = lax.all_gather(block, "tensor", axis=1, tiled=True)
    return jnp.roll(every, -lax.axis_index("tensor") * own, axis=1)[:, own:]


def give_back(block, own, tensor):
    if tensor == 2:
        return lax.ppermute(block, "tensor", [(0, 1), (1, 0)])
    every = jnp.concatenate([jnp.zeros((block.shape[0], own), block.dtype), block], axis=1)
    every = jnp.roll(every, lax.axis_index("tensor") * own, axis=1)
    return lax.psum_scatter(every, "tensor", scatter_dimension=1, tiled=True)


def local(events, cotangent, w_in, w_out, slot_source, slot_length):
    tensor = lax.axis_size("tensor")
    users = lax.axis_size("user")
    hist, seq_len, own = events.shape
    x = events.reshape(hist * seq_len, own)
    d = cotangent.reshape(hist * seq_len, own)
    blocks = sum(steps for _, steps in GROUPS)
    rows = hist // blocks * seq_len
    far, ahead = [], None
    for start, steps in GROUPS:
        spans = [slice(i * rows, (i + 1) * rows) for i in range(start, start + steps)]
        if ahead is not None:
            x, d, _ = lax.optimization_barrier((x, d, ahead))
        ahead = jnp.concatenate([t[span] for span in spans for t in (x, d)], axis=0)
        far.append(exchange(ahead, tensor))

    weights = lax.all_gather(
        jnp.concatenate([w_in, w_out], axis=1), "user", axis=0, tiled=True
    )
    table = lax.all_gather(slot_source * 256 + slot_length, "user", axis=0, tiled=True)
    table = table.reshape(users, hist)
    user = lax.axis_index("user")
    lens = jnp.sum(jnp.where(table // 256 == user, table % 256, 0), axis=0)
    where = jnp.stack([lax.axis_index("tensor"), user]).astype(jnp.int32)

    acc = []
    kept, sent = [], []
    for group, theirs in zip(GROUPS, far):
        gx, bs, *acc = group_call(
            group, blocks, users, lens, where, x, d, theirs, weights, acc[0] if acc else None
        )
        kept.append(gx)
        sent.append(give_back(bs, own, tensor))
    keep, send = acc
    got, rest = scatter_parts(keep, send, users)
    grad_x, grad_in, grad_out = finish(kept, sent, keep, got, rest, w_in.shape[1])
    return (grad_x.reshape(hist, seq_len, own), grad_in, grad_out)


def solution(mesh):
    in_specs = (
        P("user", None, "tensor"),
        P("user", None, "tensor"),
        P("user", "tensor"),
        P("user", "tensor"),
        P("user"),
        P("user"),
    )
    out_specs = (P("user", None, "tensor"), P("user", "tensor"), P("user", "tensor"))
    return jax.shard_map(local, mesh=mesh, in_specs=in_specs, out_specs=out_specs, check_vma=False)
```

```python
import functools

import jax
import jax.numpy as jnp
from jax import lax
from jax.experimental import pallas as pl
from jax.experimental.pallas import tpu as pltpu
from jax.sharding import PartitionSpec as P

HEAD_DIM = 128
SEQ_LEN = 128
GROUPS = ((0, 2), (2, 1), (3, 1))

eps = 1e-05
f32 = jnp.float32
bf16 = jnp.bfloat16


def dot_nn(a, b):
    return lax.dot_general(a, b, (((1,), (0,)), ((), ())), preferred_element_type=f32)


def dot_nt(a, b):
    return lax.dot_general(a, b, (((1,), (1,)), ((), ())), preferred_element_type=f32)


def dot_tn(a, b):
    return lax.dot_general(a, b, (((0,), (0,)), ((), ())), preferred_element_type=f32)


def row_mean(t):
    return jnp.mean(t, axis=1, keepdims=True)


def gates(t):
    sig = 0.5 * jnp.tanh(0.5 * t) + 0.5
    silu = t * sig
    return silu, sig + silu * (1.0 - sig)


def attention(pairs, causal, g_s, dh_s, slope_s, hb_s, dz_s):
    scale = HEAD_DIM ** (-0.5)
    spans = [pl.ds(n * SEQ_LEN, SEQ_LEN) for _, n in pairs]
    lanes = [[pl.ds((4 * h + e) * HEAD_DIM, HEAD_DIM) for e in range(4)] for h, _ in pairs]
    heads = [pl.ds(h * HEAD_DIM, HEAD_DIM) for h, _ in pairs]
    every = range(len(pairs))
    weight = causal * (1.0 / SEQ_LEN)

    def part(i, e):
        return g_s[spans[i], lanes[i][e]]

    s = [(dot_nt(part(i, 2), part(i, 3)) * scale).astype(bf16) for i in every]
    pair = [gates(t) for t in s]
    attn = [silu * weight for silu, _ in pair]
    slope = [t * weight for _, t in pair]
    y = [dot_nn(attn[i], part(i, 1)) for i in every]
    cen = [t - row_mean(t) for t in y]
    rstd = [lax.rsqrt(row_mean(t * t) + eps) for t in cen]
    yn = [cen[i] * rstd[i] for i in every]
    uf = [part(i, 0).astype(f32) for i in every]
    dh = [dh_s[spans[i], heads[i]] for i in every]
    dyn = [dh[i] * uf[i] for i in every]
    one = [row_mean(t) for t in dyn]
    two = [row_mean(dyn[i] * yn[i]) for i in every]
    dy = [((dyn[i] - one[i] - yn[i] * two[i]) * rstd[i]).astype(bf16) for i in every]
    grad_a = [dot_nt(dy[i], part(i, 1)) for i in every]
    ds = [(grad_a[i] * scale).astype(bf16) * slope[i] for i in every]

    def store(i, e, grad):
        dz_s[spans[i], lanes[i][e]] = grad.astype(bf16) * slope_s[spans[i], lanes[i][e]]

    for i in every:
        hb_s[spans[i], heads[i]] = (yn[i] * uf[i]).astype(bf16)
        store(i, 0, dh[i] * yn[i])
    for i in every:
        store(i, 1, dot_tn(attn[i], dy[i]))
    for i in every:
        store(i, 2, dot_nn(ds[i], part(i, 3)))
    for i in every:
        store(i, 3, dot_tn(ds[i], part(i, 2)))


def split_order(count):
    rest = sorted(range(1, count), key=lambda j: abs(j - count / 2))
    return rest + [0]


def group_kernel(start, steps, first, last, heads, parts, users, *refs):
    refs = list(refs)
    lens_ref, where_ref, xo_ref, do_ref, far_ref, w_hbm = refs[:6]
    refs = refs[6:]
    acc_hbm = None if first else refs.pop(0)
    refs = refs if first else refs[2:]
    gx_ref, bs_ref = refs[:2]
    refs = refs[2:]
    grads_hbm = [refs.pop(0) for _ in range(2 if last else 1)]
    (w_s, acc_s, nb_s, nt_s, dm_s, dt_s, dz_s, hb_s, g_s, slope_s, dh_s, out_s) = refs[:12]
    load_sems, store_sems = refs[12:]
    rows, own = xo_ref.shape
    width = own * parts
    cols_in = heads * 4 * HEAD_DIM
    histories = rows // SEQ_LEN
    me, user = where_ref[0], where_ref[1]
    step = pl.program_id(0)

    def only(index, run):
        if steps == 1:
            run()
        else:
            pl.when(step == index)(run)

    loads = []
    for p in range(parts):
        source = pl.ds(pl.multiple_of(lax.rem(me + p, parts) * own, own), own)
        loads.append(
            pltpu.make_async_copy(w_hbm.at[source], w_s.at[pl.ds(p * own, own)], load_sems.at[p])
        )
    if not first:
        acc_load = pltpu.make_async_copy(acc_hbm, acc_s, load_sems.at[parts])

    def begin():
        for copy in loads:
            copy.start()
        if first:
            acc_s[...] = jnp.zeros_like(acc_s)
        else:
            acc_load.start()

    def loaded():
        for copy in loads:
            copy.wait()

    only(0, begin)

    causal = lax.broadcasted_iota(jnp.int32, (SEQ_LEN, SEQ_LEN), 0) >= lax.broadcasted_iota(
        jnp.int32, (SEQ_LEN, SEQ_LEN), 1
    )
    causal = causal.astype(f32).astype(bf16)
    position = lax.broadcasted_iota(jnp.int32, (SEQ_LEN, 1), 0)
    half = min(2 * SEQ_LEN, rows)
    halves = [slice(lo, lo + half) for lo in range(0, rows, half)]

    rstds = []
    for here in halves:
        xo = xo_ref[here, :].astype(f32)
        xr = far_ref[here, :].astype(f32)
        mean = (jnp.sum(xo, axis=1, keepdims=True) + jnp.sum(xr, axis=1, keepdims=True)) / width
        xo = xo - mean
        xr = xr - mean
        var = (
            jnp.sum(xo * xo, axis=1, keepdims=True) + jnp.sum(xr * xr, axis=1, keepdims=True)
        ) / width
        rstd = lax.rsqrt(var + eps)
        rstds.append(rstd)
        bo = (xo * rstd).astype(bf16)
        br = (xr * rstd).astype(bf16)
        nb_s[here, :own] = bo
        nb_s[here, own:] = br
        nt_s[:own, here] = bo.T
        nt_s[own:, here] = br.T
    only(0, loaded)
    for h in range(heads):
        c = slice(h * 4 * HEAD_DIM, (h + 1) * 4 * HEAD_DIM)
        z = dot_nn(nb_s[...], w_s[:, c]).astype(bf16)
        g_s[:, c], slope_s[:, c] = gates(z)
    for here in halves:
        base = start * histories + step * histories
        valid = jnp.concatenate(
            [
                (position < lens_ref[base + n]).astype(f32)
                for n in range(here.start // SEQ_LEN, here.stop // SEQ_LEN)
            ],
            axis=0,
        ).astype(bf16)
        there = slice(rows + here.start, rows + here.stop)
        do = do_ref[here, :] * valid
        dr = far_ref[there, :] * valid
        dm_s[here, :own] = do
        dm_s[here, own:] = dr
        dt_s[:own, here] = do.T
        dt_s[own:, here] = dr.T
    dh_s[...] = dot_nn(dm_s[...], w_s[:, cols_in:])

    if not first:
        only(0, acc_load.wait)
    target = out_s if last else acc_s
    size = width // users
    far = users // 4
    zi, xi, ci = user // 4, lax.rem(user // 2, 2), lax.rem(user, 2)
    stores = []

    def ship(lo, wide):
        lanes = pl.ds(lo, wide)
        if not last:
            stores.append(
                pltpu.make_async_copy(
                    acc_s.at[:, lanes], grads_hbm[0].at[:, lanes], store_sems.at[len(stores)]
                )
            )
            only(steps - 1, stores[-1].start)
            return
        keep, send = grads_hbm
        for at, j in enumerate(split_order(far)):
            zd = lax.rem(zi + far - j, far)
            for xs in range(2):
                xd = xi if xs == 0 else 1 - xi
                for cs in range(2):
                    cd = ci if cs == 0 else 1 - ci
                    row = ((zd * 2 + xd) * 2 + cd) * size
                    row = lax.rem(row // own - me + parts, parts) * own + lax.rem(row, own)
                    slot = xs * far + at
                    there = keep if cs == 0 else send
                    stores.append(
                        pltpu.make_async_copy(
                            out_s.at[pl.ds(pl.multiple_of(row, size), size), lanes],
                            there.at[pl.ds(slot * size, size), lanes],
                            store_sems.at[len(stores)],
                        )
                    )
                    only(steps - 1, stores[-1].start)

    def add(lhs, rhs, lo, wide):
        chunk = min(512, width)
        for r in range(0, width, chunk):
            term = dot_nn(lhs[r : r + chunk, :], rhs[...]) + acc_s[r : r + chunk, lo : lo + wide]
            target[r : r + chunk, lo : lo + wide] = term.astype(target.dtype)
        ship(lo, wide)

    block = 4 * HEAD_DIM
    stride = max(1, 8 // histories)
    for lo in range(0, heads, stride):
        hi = min(lo + stride, heads)
        pairs = [(h, n) for h in range(lo, hi) for n in range(histories)]
        attention(pairs, causal, g_s, dh_s, slope_s, hb_s, dz_s)
        for h in range(max(0, lo - stride), lo):
            add(nt_s, dz_s.at[:, h * block : (h + 1) * block], h * block, block)
    dn_all = dot_nt(dz_s[...], w_s[:, :cols_in])
    add(dt_s, hb_s, cols_in, heads * HEAD_DIM)
    for here, rstd in zip(halves, rstds):
        dn = dn_all[here, :]
        nf = nb_s[here, :].astype(f32)
        one = jnp.sum(dn, axis=1, keepdims=True) / width
        two = jnp.sum(dn * nf, axis=1, keepdims=True) / width
        branch = (dn - one - nf * two) * rstd
        gx_ref[here, :] = (dm_s[here, :own].astype(f32) + branch[:, :own]).astype(bf16)
        bs_ref[here, :] = branch[:, own:].astype(bf16)
    for h in range((heads - 1) // stride * stride, heads):
        add(nt_s, dz_s.at[:, h * block : (h + 1) * block], h * block, block)

    for copy in stores:
        only(steps - 1, copy.wait)


def group_call(group, blocks, users, lens, where, x, d, far, weights, past):
    start, steps = group
    first, last = start == 0, start + steps == blocks
    rows, own = x.shape[0] // blocks, x.shape[1]
    width, cols = weights.shape
    parts = width // own
    heads = cols // (5 * HEAD_DIM)
    cols_in = heads * 4 * HEAD_DIM
    smem = pl.BlockSpec(memory_space=pltpu.SMEM)
    anywhere = pl.BlockSpec(memory_space=pl.ANY)
    mine = pl.BlockSpec((rows, own), lambda i: (start + i, 0))
    theirs = pl.BlockSpec((2 * rows, width - own), lambda i: (i, 0))
    args = [lens, where, x, d, far, weights] + past
    specs = [smem, smem, mine, mine, theirs] + [anywhere] * (1 + len(past))
    if last:
        grads = [jax.ShapeDtypeStruct((width // 2, cols), bf16)] * 2
    else:
        grads = [jax.ShapeDtypeStruct((width, cols), f32)]
    flops = steps * (4 * rows * width * cols + 2 * rows * width * cols_in)
    return pl.pallas_call(
        functools.partial(group_kernel, start, steps, first, last, heads, parts, users),
        grid=(steps,),
        out_shape=[
            jax.ShapeDtypeStruct((blocks * rows, own), bf16),
            jax.ShapeDtypeStruct((blocks * rows, width - own), bf16),
        ]
        + grads,
        in_specs=specs,
        out_specs=[
            pl.BlockSpec((rows, own), lambda i: (start + i, 0)),
            pl.BlockSpec((rows, width - own), lambda i: (start + i, 0)),
        ]
        + [anywhere] * len(grads),
        input_output_aliases={} if first else {7: 0, 8: 1},
        scratch_shapes=[
            pltpu.VMEM((width, cols), bf16),
            pltpu.VMEM((width, cols), f32),
            pltpu.VMEM((rows, width), bf16),
            pltpu.VMEM((width, rows), bf16),
            pltpu.VMEM((rows, width), bf16),
            pltpu.VMEM((width, rows), bf16),
            pltpu.VMEM((rows, cols_in), bf16),
            pltpu.VMEM((rows, cols - cols_in), bf16),
            pltpu.VMEM((rows, cols_in), bf16),
            pltpu.VMEM((rows, cols_in), bf16),
            pltpu.VMEM((rows, cols - cols_in), f32),
            pltpu.VMEM((width, cols) if last else (16, 128), bf16),
            pltpu.SemaphoreType.DMA((parts + 1,)),
            pltpu.SemaphoreType.DMA(((users if last else 1) * (heads + 1),)),
        ],
        compiler_params=pltpu.CompilerParams(vmem_limit_bytes=56 * 2**20),
        cost_estimate=pl.CostEstimate(
            flops=flops, bytes_accessed=16 * 2**20, transcendentals=steps * rows * cols
        ),
    )(*args)


def scatter_parts(keep, send, users):
    far = users // 4
    order = split_order(far)
    size = keep.shape[0] // (2 * far)

    def swap(block, bit):
        return lax.ppermute(block, "user", [(i, i ^ bit) for i in range(users)])

    got = swap(send, 1)

    def both(lo, hi):
        span = slice(lo * size, hi * size)
        return keep[span].astype(f32) + got[span].astype(f32)

    cuts = [(0, 1), (1, far - 1), (far - 1, far)]
    across = [swap(both(far + lo, far + hi).astype(bf16), 2) for lo, hi in cuts]
    moved = []
    for (lo, hi), other in zip(cuts[:2], across):
        near = (both(lo, hi) + other.astype(f32)).astype(bf16)
        for at in range(lo, hi):
            pairs = [(i, (i - 4 * order[at]) % users) for i in range(users)]
            block = near[(at - lo) * size : (at - lo + 1) * size]
            moved.append(lax.ppermute(block, "user", pairs))
    return got, [across[2]] + moved


def finish_kernel(cols_in, kept_ref, sent_ref, *refs):
    terms = refs[:-3]
    gx_ref, win_ref, wout_ref = refs[-3:]
    gx_ref[...] = (kept_ref[...].astype(f32) + sent_ref[...].astype(f32)).astype(bf16)

    @pl.when(pl.program_id(0) == 0)
    def _():
        total = terms[0][...].astype(f32)
        for term in terms[1:]:
            total = total + term[...].astype(f32)
        win_ref[...] = total[:, :cols_in]
        wout_ref[...] = total[:, cols_in:]


def finish(kept, sent, keep, got, rest, cols_in):
    rows, own = kept.shape
    size, cols = rest[0].shape
    slot = keep.shape[0] // (2 * size) - 1
    steps = 4
    lines = pl.BlockSpec((rows // steps, own), lambda i: (i, 0))
    specs = [lines] * 2
    specs += [pl.BlockSpec((size, cols), lambda i: (slot, 0))] * 2
    specs += [pl.BlockSpec((size, cols), lambda i: (0, 0))] * len(rest)
    return pl.pallas_call(
        functools.partial(finish_kernel, cols_in),
        grid=(steps,),
        out_shape=[
            jax.ShapeDtypeStruct((rows, own), bf16),
            jax.ShapeDtypeStruct((size, cols_in), f32),
            jax.ShapeDtypeStruct((size, cols - cols_in), f32),
        ],
        in_specs=specs,
        out_specs=[
            lines,
            pl.BlockSpec((size, cols_in), lambda i: (0, 0)),
            pl.BlockSpec((size, cols - cols_in), lambda i: (0, 0)),
        ],
        compiler_params=pltpu.CompilerParams(vmem_limit_bytes=32 * 2**20),
        cost_estimate=pl.CostEstimate(
            flops=rows * own, bytes_accessed=12 * 2**20, transcendentals=0
        ),
    )(kept, sent, keep, got, *rest)


def exchange(block, tensor):
    if tensor == 2:
        return lax.ppermute(block, "tensor", [(0, 1), (1, 0)])
    own = block.shape[1]
    every = lax.all_gather(block, "tensor", axis=1, tiled=True)
    return jnp.roll(every, -lax.axis_index("tensor") * own, axis=1)[:, own:]


def give_back(block, own, tensor):
    if tensor == 2:
        return lax.ppermute(block, "tensor", [(0, 1), (1, 0)])
    every = jnp.concatenate([jnp.zeros((block.shape[0], own), block.dtype), block], axis=1)
    every = jnp.roll(every, lax.axis_index("tensor") * own, axis=1)
    return lax.psum_scatter(every, "tensor", scatter_dimension=1, tiled=True)


def local(events, cotangent, w_in, w_out, slot_source, slot_length):
    tensor = lax.axis_size("tensor")
    users = lax.axis_size("user")
    hist, seq_len, own = events.shape
    x = events.reshape(hist * seq_len, own)
    d = cotangent.reshape(hist * seq_len, own)
    blocks = sum(steps for _, steps in GROUPS)
    rows = hist // blocks * seq_len
    far, ahead = [], None
    for start, steps in GROUPS:
        spans = [slice(i * rows, (i + 1) * rows) for i in range(start, start + steps)]
        if ahead is not None:
            x, d, _ = lax.optimization_barrier((x, d, ahead))
        ahead = jnp.concatenate([t[span] for span in spans for t in (x, d)], axis=0)
        far.append(exchange(ahead, tensor))

    weights = lax.all_gather(
        jnp.concatenate([w_in, w_out], axis=1), "user", axis=0, tiled=True
    )
    table = lax.all_gather(slot_source * 256 + slot_length, "user", axis=0, tiled=True)
    table = table.reshape(users, hist)
    user = lax.axis_index("user")
    lens = jnp.sum(jnp.where(table // 256 == user, table % 256, 0), axis=0)
    where = jnp.stack([lax.axis_index("tensor"), user]).astype(jnp.int32)

    past = []
    for group, theirs in zip(GROUPS, far):
        kept, bs, *grads = group_call(
            group, blocks, users, lens, where, x, d, theirs, weights, past
        )
        past = grads + [kept, bs]
    sent = give_back(bs, own, tensor)
    keep, send = grads
    got, rest = scatter_parts(keep, send, users)
    grad_x, grad_in, grad_out = finish(kept, sent, keep, got, rest, w_in.shape[1])
    return (grad_x.reshape(hist, seq_len, own), grad_in, grad_out)


def solution(mesh):
    in_specs = (
        P("user", None, "tensor"),
        P("user", None, "tensor"),
        P("user", "tensor"),
        P("user", "tensor"),
        P("user"),
        P("user"),
    )
    out_specs = (P("user", None, "tensor"), P("user", "tensor"), P("user", "tensor"))
    return jax.shard_map(local, mesh=mesh, in_specs=in_specs, out_specs=out_specs, check_vma=False)
```

```python
import functools

import jax
import jax.numpy as jnp
from jax import lax
from jax.experimental import pallas as pl
from jax.experimental.pallas import tpu as pltpu
from jax.sharding import PartitionSpec as P

HEAD_DIM = 128
SEQ_LEN = 128
GROUPS = ((0, 2), (2, 1), (3, 1))

eps = 1e-05
f32 = jnp.float32
bf16 = jnp.bfloat16


def dot_nn(a, b):
    return lax.dot_general(a, b, (((1,), (0,)), ((), ())), preferred_element_type=f32)


def dot_nt(a, b):
    return lax.dot_general(a, b, (((1,), (1,)), ((), ())), preferred_element_type=f32)


def dot_tn(a, b):
    return lax.dot_general(a, b, (((0,), (0,)), ((), ())), preferred_element_type=f32)


def row_mean(t):
    return jnp.mean(t, axis=1, keepdims=True)


def gates(t):
    sig = 0.5 * jnp.tanh(0.5 * t) + 0.5
    silu = t * sig
    return silu, sig + silu * (1.0 - sig)


def attention(units, span, mask, g_s, dh_s, slope_s, hb_s, dz_s):
    scale = HEAD_DIM ** (-0.5)
    spans = [pl.ds(n * span, span) for _, n in units]
    lanes = [[pl.ds((4 * h + e) * HEAD_DIM, HEAD_DIM) for e in range(4)] for h, _ in units]
    heads = [pl.ds(h * HEAD_DIM, HEAD_DIM) for h, _ in units]
    every = range(len(units))

    def part(i, e):
        return g_s[spans[i], lanes[i][e]]

    s = [dot_nt(part(i, 2), part(i, 3)) * scale for i in every]
    pair = [gates(t) for t in s]
    attn = [jnp.where(mask, silu * (1.0 / SEQ_LEN), 0.0).astype(bf16) for silu, _ in pair]
    slope = [jnp.where(mask, t * (scale / SEQ_LEN), 0.0) for _, t in pair]
    y = [dot_nn(attn[i], part(i, 1)) for i in every]
    cen = [t - row_mean(t) for t in y]
    rstd = [lax.rsqrt(row_mean(t * t) + eps) for t in cen]
    yn = [cen[i] * rstd[i] for i in every]
    uf = [part(i, 0).astype(f32) for i in every]
    dh = [dh_s[spans[i], heads[i]] for i in every]
    dyn = [dh[i] * uf[i] for i in every]
    one = [row_mean(t) for t in dyn]
    two = [row_mean(dyn[i] * yn[i]) for i in every]
    dy = [((dyn[i] - one[i] - yn[i] * two[i]) * rstd[i]).astype(bf16) for i in every]
    grad_a = [dot_nt(dy[i], part(i, 1)) for i in every]
    ds = [(grad_a[i] * slope[i]).astype(bf16) for i in every]

    def store(i, e, grad):
        dz_s[spans[i], lanes[i][e]] = (grad * slope_s[spans[i], lanes[i][e]]).astype(bf16)

    for i in every:
        hb_s[spans[i], heads[i]] = (yn[i] * uf[i]).astype(bf16)
        store(i, 0, dh[i] * yn[i])
    for i in every:
        store(i, 1, dot_tn(attn[i], dy[i]))
    for i in every:
        store(i, 2, dot_nn(ds[i], part(i, 3)))
    for i in every:
        store(i, 3, dot_tn(ds[i], part(i, 2)))


def split_order(count):
    rest = sorted(range(1, count), key=lambda j: abs(j - count / 2))
    return rest + [0]


def group_kernel(start, steps, first, last, heads, parts, users, *refs):
    refs = list(refs)
    lens_ref, where_ref, xo_ref, do_ref, far_ref, w_hbm = refs[:6]
    refs = refs[6:]
    acc_hbm = None if first else refs.pop(0)
    refs = refs if first else refs[2:]
    gx_ref, bs_ref = refs[:2]
    refs = refs[2:]
    grads_hbm = [refs.pop(0) for _ in range(2 if last else 1)]
    (w_s, acc_s, nb_s, nt_s, dm_s, dt_s, dz_s, hb_s, g_s, slope_s, dh_s, out_s) = refs[:12]
    load_sems, store_sems = refs[12:]
    rows, own = xo_ref.shape
    width = own * parts
    cols_in = heads * 4 * HEAD_DIM
    histories = rows // SEQ_LEN
    me, user = where_ref[0], where_ref[1]
    step = pl.program_id(0)

    def only(index, run):
        if steps == 1:
            run()
        else:
            pl.when(step == index)(run)

    loads = []
    for p in range(parts):
        source = pl.ds(pl.multiple_of(lax.rem(me + p, parts) * own, own), own)
        loads.append(
            pltpu.make_async_copy(w_hbm.at[source], w_s.at[pl.ds(p * own, own)], load_sems.at[p])
        )
    if not first:
        acc_load = pltpu.make_async_copy(acc_hbm, acc_s, load_sems.at[parts])

    def begin():
        for copy in loads:
            copy.start()
        if first:
            acc_s[...] = jnp.zeros_like(acc_s)
        else:
            acc_load.start()

    def loaded():
        for copy in loads:
            copy.wait()

    only(0, begin)

    position = lax.broadcasted_iota(jnp.int32, (SEQ_LEN, 1), 0)
    half = min(2 * SEQ_LEN, rows)
    halves = [slice(lo, lo + half) for lo in range(0, rows, half)]
    query = lax.broadcasted_iota(jnp.int32, (half, half), 0)
    key = lax.broadcasted_iota(jnp.int32, (half, half), 1)
    mask = (key <= query) & (key // SEQ_LEN == query // SEQ_LEN)

    rstds = []
    for here in halves:
        xo = xo_ref[here, :].astype(f32)
        xr = far_ref[here, :].astype(f32)
        mean = (jnp.sum(xo, axis=1, keepdims=True) + jnp.sum(xr, axis=1, keepdims=True)) / width
        xo = xo - mean
        xr = xr - mean
        var = (
            jnp.sum(xo * xo, axis=1, keepdims=True) + jnp.sum(xr * xr, axis=1, keepdims=True)
        ) / width
        rstd = lax.rsqrt(var + eps)
        rstds.append(rstd)
        bo = (xo * rstd).astype(bf16)
        br = (xr * rstd).astype(bf16)
        nb_s[here, :own] = bo
        nb_s[here, own:] = br
        nt_s[:own, here] = bo.T
        nt_s[own:, here] = br.T
    only(0, loaded)
    for h in range(heads):
        c = slice(h * 4 * HEAD_DIM, (h + 1) * 4 * HEAD_DIM)
        silu, slope_s[:, c] = gates(dot_nn(nb_s[...], w_s[:, c]))
        g_s[:, c] = silu.astype(bf16)
    for here in halves:
        base = start * histories + step * histories
        valid = jnp.concatenate(
            [
                (position < lens_ref[base + n]).astype(f32)
                for n in range(here.start // SEQ_LEN, here.stop // SEQ_LEN)
            ],
            axis=0,
        ).astype(bf16)
        there = slice(rows + here.start, rows + here.stop)
        do = do_ref[here, :] * valid
        dr = far_ref[there, :] * valid
        dm_s[here, :own] = do
        dm_s[here, own:] = dr
        dt_s[:own, here] = do.T
        dt_s[own:, here] = dr.T
    dh_s[...] = dot_nn(dm_s[...], w_s[:, cols_in:])

    if not first:
        only(0, acc_load.wait)
    target = out_s if last else acc_s
    size = width // users
    far = users // 4
    zi, xi, ci = user // 4, lax.rem(user // 2, 2), lax.rem(user, 2)
    stores = []

    def ship(lo, wide):
        lanes = pl.ds(lo, wide)
        if not last:
            stores.append(
                pltpu.make_async_copy(
                    acc_s.at[:, lanes], grads_hbm[0].at[:, lanes], store_sems.at[len(stores)]
                )
            )
            only(steps - 1, stores[-1].start)
            return
        keep, send = grads_hbm
        for at, j in enumerate(split_order(far)):
            zd = lax.rem(zi + far - j, far)
            for xs in range(2):
                xd = xi if xs == 0 else 1 - xi
                for cs in range(2):
                    cd = ci if cs == 0 else 1 - ci
                    row = ((zd * 2 + xd) * 2 + cd) * size
                    row = lax.rem(row // own - me + parts, parts) * own + lax.rem(row, own)
                    slot = xs * far + at
                    there = keep if cs == 0 else send
                    stores.append(
                        pltpu.make_async_copy(
                            out_s.at[pl.ds(pl.multiple_of(row, size), size), lanes],
                            there.at[pl.ds(slot * size, size), lanes],
                            store_sems.at[len(stores)],
                        )
                    )
                    only(steps - 1, stores[-1].start)

    def add(lhs, rhs, lo, wide):
        chunk = min(512, width)
        for r in range(0, width, chunk):
            term = dot_nn(lhs[r : r + chunk, :], rhs[...]) + acc_s[r : r + chunk, lo : lo + wide]
            target[r : r + chunk, lo : lo + wide] = term.astype(target.dtype)
        ship(lo, wide)

    block = 4 * HEAD_DIM
    stride = max(1, 8 // histories)
    for lo in range(0, heads, stride):
        hi = min(lo + stride, heads)
        units = [(h, n) for h in range(lo, hi) for n in range(len(halves))]
        attention(units, half, mask, g_s, dh_s, slope_s, hb_s, dz_s)
        for h in range(max(0, lo - stride), lo):
            add(nt_s, dz_s.at[:, h * block : (h + 1) * block], h * block, block)
    dn_all = dot_nt(dz_s[...], w_s[:, :cols_in])
    add(dt_s, hb_s, cols_in, heads * HEAD_DIM)
    for here, rstd in zip(halves, rstds):
        dn = dn_all[here, :]
        nf = nb_s[here, :].astype(f32)
        one = jnp.sum(dn, axis=1, keepdims=True) / width
        two = jnp.sum(dn * nf, axis=1, keepdims=True) / width
        branch = (dn - one - nf * two) * rstd
        gx_ref[here, :] = (dm_s[here, :own].astype(f32) + branch[:, :own]).astype(bf16)
        bs_ref[here, :] = branch[:, own:].astype(bf16)
    for h in range((heads - 1) // stride * stride, heads):
        add(nt_s, dz_s.at[:, h * block : (h + 1) * block], h * block, block)

    for copy in stores:
        only(steps - 1, copy.wait)


def group_call(group, blocks, users, lens, where, x, d, far, weights, past):
    start, steps = group
    first, last = start == 0, start + steps == blocks
    rows, own = x.shape[0] // blocks, x.shape[1]
    width, cols = weights.shape
    parts = width // own
    heads = cols // (5 * HEAD_DIM)
    cols_in = heads * 4 * HEAD_DIM
    smem = pl.BlockSpec(memory_space=pltpu.SMEM)
    anywhere = pl.BlockSpec(memory_space=pl.ANY)
    mine = pl.BlockSpec((rows, own), lambda i: (start + i, 0))
    theirs = pl.BlockSpec((2 * rows, width - own), lambda i: (i, 0))
    args = [lens, where, x, d, far, weights] + past
    specs = [smem, smem, mine, mine, theirs] + [anywhere] * (1 + len(past))
    if last:
        grads = [jax.ShapeDtypeStruct((width // 2, cols), bf16)] * 2
    else:
        grads = [jax.ShapeDtypeStruct((width, cols), f32)]
    flops = steps * (4 * rows * width * cols + 2 * rows * width * cols_in)
    return pl.pallas_call(
        functools.partial(group_kernel, start, steps, first, last, heads, parts, users),
        grid=(steps,),
        out_shape=[
            jax.ShapeDtypeStruct((blocks * rows, own), bf16),
            jax.ShapeDtypeStruct((blocks * rows, width - own), bf16),
        ]
        + grads,
        in_specs=specs,
        out_specs=[
            pl.BlockSpec((rows, own), lambda i: (start + i, 0)),
            pl.BlockSpec((rows, width - own), lambda i: (start + i, 0)),
        ]
        + [anywhere] * len(grads),
        input_output_aliases={} if first else {7: 0, 8: 1},
        scratch_shapes=[
            pltpu.VMEM((width, cols), bf16),
            pltpu.VMEM((width, cols), f32),
            pltpu.VMEM((rows, width), bf16),
            pltpu.VMEM((width, rows), bf16),
            pltpu.VMEM((rows, width), bf16),
            pltpu.VMEM((width, rows), bf16),
            pltpu.VMEM((rows, cols_in), bf16),
            pltpu.VMEM((rows, cols - cols_in), bf16),
            pltpu.VMEM((rows, cols_in), bf16),
            pltpu.VMEM((rows, cols_in), f32),
            pltpu.VMEM((rows, cols - cols_in), f32),
            pltpu.VMEM((width, cols) if last else (16, 128), bf16),
            pltpu.SemaphoreType.DMA((parts + 1,)),
            pltpu.SemaphoreType.DMA(((users if last else 1) * (heads + 1),)),
        ],
        compiler_params=pltpu.CompilerParams(vmem_limit_bytes=56 * 2**20),
        cost_estimate=pl.CostEstimate(
            flops=flops, bytes_accessed=16 * 2**20, transcendentals=steps * rows * cols
        ),
    )(*args)


def scatter_parts(keep, send, users):
    far = users // 4
    order = split_order(far)
    size = keep.shape[0] // (2 * far)

    def swap(block, bit):
        return lax.ppermute(block, "user", [(i, i ^ bit) for i in range(users)])

    got = swap(send, 1)

    def both(lo, hi):
        span = slice(lo * size, hi * size)
        return keep[span].astype(f32) + got[span].astype(f32)

    cuts = [(0, 1), (1, far - 1), (far - 1, far)]
    across = [swap(both(far + lo, far + hi).astype(bf16), 2) for lo, hi in cuts]
    moved = []
    for (lo, hi), other in zip(cuts[:2], across):
        near = (both(lo, hi) + other.astype(f32)).astype(bf16)
        for at in range(lo, hi):
            pairs = [(i, (i - 4 * order[at]) % users) for i in range(users)]
            block = near[(at - lo) * size : (at - lo + 1) * size]
            moved.append(lax.ppermute(block, "user", pairs))
    return got, [across[2]] + moved


def finish_kernel(cols_in, kept_ref, sent_ref, *refs):
    terms = refs[:-3]
    gx_ref, win_ref, wout_ref = refs[-3:]
    gx_ref[...] = (kept_ref[...].astype(f32) + sent_ref[...].astype(f32)).astype(bf16)

    @pl.when(pl.program_id(0) == 0)
    def _():
        total = terms[0][...].astype(f32)
        for term in terms[1:]:
            total = total + term[...].astype(f32)
        win_ref[...] = total[:, :cols_in]
        wout_ref[...] = total[:, cols_in:]


def finish(kept, sent, keep, got, rest, cols_in):
    rows, own = kept.shape
    size, cols = rest[0].shape
    slot = keep.shape[0] // (2 * size) - 1
    steps = 4
    lines = pl.BlockSpec((rows // steps, own), lambda i: (i, 0))
    specs = [lines] * 2
    specs += [pl.BlockSpec((size, cols), lambda i: (slot, 0))] * 2
    specs += [pl.BlockSpec((size, cols), lambda i: (0, 0))] * len(rest)
    return pl.pallas_call(
        functools.partial(finish_kernel, cols_in),
        grid=(steps,),
        out_shape=[
            jax.ShapeDtypeStruct((rows, own), bf16),
            jax.ShapeDtypeStruct((size, cols_in), f32),
            jax.ShapeDtypeStruct((size, cols - cols_in), f32),
        ],
        in_specs=specs,
        out_specs=[
            lines,
            pl.BlockSpec((size, cols_in), lambda i: (0, 0)),
            pl.BlockSpec((size, cols - cols_in), lambda i: (0, 0)),
        ],
        compiler_params=pltpu.CompilerParams(vmem_limit_bytes=32 * 2**20),
        cost_estimate=pl.CostEstimate(
            flops=rows * own, bytes_accessed=12 * 2**20, transcendentals=0
        ),
    )(kept, sent, keep, got, *rest)


def exchange(block, tensor):
    if tensor == 2:
        return lax.ppermute(block, "tensor", [(0, 1), (1, 0)])
    own = block.shape[1]
    every = lax.all_gather(block, "tensor", axis=1, tiled=True)
    return jnp.roll(every, -lax.axis_index("tensor") * own, axis=1)[:, own:]


def give_back(block, own, tensor):
    if tensor == 2:
        return lax.ppermute(block, "tensor", [(0, 1), (1, 0)])
    every = jnp.concatenate([jnp.zeros((block.shape[0], own), block.dtype), block], axis=1)
    every = jnp.roll(every, lax.axis_index("tensor") * own, axis=1)
    return lax.psum_scatter(every, "tensor", scatter_dimension=1, tiled=True)


def local(events, cotangent, w_in, w_out, slot_source, slot_length):
    tensor = lax.axis_size("tensor")
    users = lax.axis_size("user")
    hist, seq_len, own = events.shape
    x = events.reshape(hist * seq_len, own)
    d = cotangent.reshape(hist * seq_len, own)
    blocks = sum(steps for _, steps in GROUPS)
    rows = hist // blocks * seq_len
    far, ahead = [], None
    for start, steps in GROUPS:
        spans = [slice(i * rows, (i + 1) * rows) for i in range(start, start + steps)]
        if ahead is not None:
            x, d, _ = lax.optimization_barrier((x, d, ahead))
        ahead = jnp.concatenate([t[span] for span in spans for t in (x, d)], axis=0)
        far.append(exchange(ahead, tensor))

    weights = lax.all_gather(
        jnp.concatenate([w_in, w_out], axis=1), "user", axis=0, tiled=True
    )
    table = lax.all_gather(slot_source * 256 + slot_length, "user", axis=0, tiled=True)
    table = table.reshape(users, hist)
    user = lax.axis_index("user")
    lens = jnp.sum(jnp.where(table // 256 == user, table % 256, 0), axis=0)
    where = jnp.stack([lax.axis_index("tensor"), user]).astype(jnp.int32)

    past = []
    for group, theirs in zip(GROUPS, far):
        kept, bs, *grads = group_call(
            group, blocks, users, lens, where, x, d, theirs, weights, past
        )
        past = grads + [kept, bs]
    sent = give_back(bs, own, tensor)
    keep, send = grads
    got, rest = scatter_parts(keep, send, users)
    grad_x, grad_in, grad_out = finish(kept, sent, keep, got, rest, w_in.shape[1])
    return (grad_x.reshape(hist, seq_len, own), grad_in, grad_out)


def solution(mesh):
    in_specs = (
        P("user", None, "tensor"),
        P("user", None, "tensor"),
        P("user", "tensor"),
        P("user", "tensor"),
        P("user"),
        P("user"),
    )
    out_specs = (P("user", None, "tensor"), P("user", "tensor"), P("user", "tensor"))
    return jax.shard_map(local, mesh=mesh, in_specs=in_specs, out_specs=out_specs, check_vma=False)
```

```python
import functools

import jax
import jax.numpy as jnp
from jax import lax
from jax.experimental import pallas as pl
from jax.experimental.pallas import tpu as pltpu
from jax.sharding import PartitionSpec as P

HEAD_DIM = 128
SEQ_LEN = 128
GROUPS = ((0, 2), (2, 1), (3, 1))

eps = 1e-05
f32 = jnp.float32
bf16 = jnp.bfloat16


def dot_nn(a, b):
    return lax.dot_general(a, b, (((1,), (0,)), ((), ())), preferred_element_type=f32)


def dot_nt(a, b):
    return lax.dot_general(a, b, (((1,), (1,)), ((), ())), preferred_element_type=f32)


def row_mean(t):
    return jnp.mean(t, axis=1, keepdims=True)


def gates(t):
    sig = 0.5 * jnp.tanh(0.5 * t) + 0.5
    silu = t * sig
    return silu, sig + silu * (1.0 - sig)


def attention(units, masks, g_s, dh_s, slope_s, hb_s, dz_s):
    scale = HEAD_DIM ** (-0.5)
    spans = [pl.ds(n * SEQ_LEN, SEQ_LEN) for _, n in units]
    lanes = [[pl.ds((4 * h + e) * HEAD_DIM, HEAD_DIM) for e in range(4)] for h, _ in units]
    heads = [pl.ds(h * HEAD_DIM, HEAD_DIM) for h, _ in units]
    every = range(len(units))

    def part(i, e):
        return g_s[spans[i], lanes[i][e]]

    def weigh(i, mask, rows, cols):
        silu, slope = gates(dot_nt(part(i, rows), part(i, cols)) * scale)
        attn = jnp.where(mask, silu * (1.0 / SEQ_LEN), 0.0).astype(bf16)
        return attn, jnp.where(mask, slope * (scale / SEQ_LEN), 0.0)

    by_query = [weigh(i, masks[0], 2, 3) for i in every]
    by_key = [weigh(i, masks[1], 3, 2) for i in every]
    y = [dot_nn(by_query[i][0], part(i, 1)) for i in every]
    cen = [t - row_mean(t) for t in y]
    rstd = [lax.rsqrt(row_mean(t * t) + eps) for t in cen]
    yn = [cen[i] * rstd[i] for i in every]
    uf = [part(i, 0).astype(f32) for i in every]
    dh = [dh_s[spans[i], heads[i]] for i in every]
    dyn = [dh[i] * uf[i] for i in every]
    one = [row_mean(t) for t in dyn]
    two = [row_mean(dyn[i] * yn[i]) for i in every]
    dy = [((dyn[i] - one[i] - yn[i] * two[i]) * rstd[i]).astype(bf16) for i in every]
    ds = [(dot_nt(dy[i], part(i, 1)) * by_query[i][1]).astype(bf16) for i in every]
    ds_key = [(dot_nt(part(i, 1), dy[i]) * by_key[i][1]).astype(bf16) for i in every]

    def store(i, e, grad):
        dz_s[spans[i], lanes[i][e]] = (grad * slope_s[spans[i], lanes[i][e]]).astype(bf16)

    for i in every:
        hb_s[spans[i], heads[i]] = (yn[i] * uf[i]).astype(bf16)
        store(i, 0, dh[i] * yn[i])
    for i in every:
        store(i, 1, dot_nn(by_key[i][0], dy[i]))
    for i in every:
        store(i, 2, dot_nn(ds[i], part(i, 3)))
    for i in every:
        store(i, 3, dot_nn(ds_key[i], part(i, 2)))


def split_order(count):
    rest = sorted(range(1, count), key=lambda j: abs(j - count / 2))
    return rest + [0]


def group_kernel(start, steps, first, last, heads, parts, users, *refs):
    refs = list(refs)
    lens_ref, where_ref, xo_ref, do_ref, far_ref, w_hbm = refs[:6]
    refs = refs[6:]
    acc_hbm = None if first else refs.pop(0)
    refs = refs if first else refs[2:]
    gx_ref, bs_ref = refs[:2]
    refs = refs[2:]
    grads_hbm = [refs.pop(0) for _ in range(2 if last else 1)]
    (w_s, acc_s, nb_s, nt_s, dm_s, dt_s, dz_s, hb_s, g_s, slope_s, dh_s, out_s) = refs[:12]
    load_sems, store_sems = refs[12:]
    rows, own = xo_ref.shape
    width = own * parts
    cols_in = heads * 4 * HEAD_DIM
    histories = rows // SEQ_LEN
    me, user = where_ref[0], where_ref[1]
    step = pl.program_id(0)

    def only(index, run):
        if steps == 1:
            run()
        else:
            pl.when(step == index)(run)

    loads = []
    for p in range(parts):
        source = pl.ds(pl.multiple_of(lax.rem(me + p, parts) * own, own), own)
        loads.append(
            pltpu.make_async_copy(w_hbm.at[source], w_s.at[pl.ds(p * own, own)], load_sems.at[p])
        )
    if not first:
        acc_load = pltpu.make_async_copy(acc_hbm, acc_s, load_sems.at[parts])

    def begin():
        for copy in loads:
            copy.start()
        if first:
            acc_s[...] = jnp.zeros_like(acc_s)
        else:
            acc_load.start()

    def loaded():
        for copy in loads:
            copy.wait()

    only(0, begin)

    position = lax.broadcasted_iota(jnp.int32, (SEQ_LEN, 1), 0)
    half = min(2 * SEQ_LEN, rows)
    halves = [slice(lo, lo + half) for lo in range(0, rows, half)]
    query = lax.broadcasted_iota(jnp.int32, (SEQ_LEN, SEQ_LEN), 0)
    key = lax.broadcasted_iota(jnp.int32, (SEQ_LEN, SEQ_LEN), 1)
    masks = (key <= query, query <= key)
    side = 256
    unit = (
        lax.broadcasted_iota(jnp.int32, (side, side), 0)
        == lax.broadcasted_iota(jnp.int32, (side, side), 1)
    )
    unit = jnp.where(unit, 1.0, 0.0).astype(bf16)

    def turn(source, target):
        for lo in range(0, width, side):
            target[lo : lo + side, :] = dot_nt(unit, source[:, lo : lo + side]).astype(bf16)

    rstds = []
    for here in halves:
        xo = xo_ref[here, :].astype(f32)
        xr = far_ref[here, :].astype(f32)
        mean = (jnp.sum(xo, axis=1, keepdims=True) + jnp.sum(xr, axis=1, keepdims=True)) / width
        xo = xo - mean
        xr = xr - mean
        var = (
            jnp.sum(xo * xo, axis=1, keepdims=True) + jnp.sum(xr * xr, axis=1, keepdims=True)
        ) / width
        rstd = lax.rsqrt(var + eps)
        rstds.append(rstd)
        bo = (xo * rstd).astype(bf16)
        br = (xr * rstd).astype(bf16)
        nb_s[here, :own] = bo
        nb_s[here, own:] = br
    only(0, loaded)
    for h in range(heads):
        c = slice(h * 4 * HEAD_DIM, (h + 1) * 4 * HEAD_DIM)
        silu, slope_s[:, c] = gates(dot_nn(nb_s[...], w_s[:, c]))
        g_s[:, c] = silu.astype(bf16)
    for here in halves:
        base = start * histories + step * histories
        valid = jnp.concatenate(
            [
                (position < lens_ref[base + n]).astype(f32)
                for n in range(here.start // SEQ_LEN, here.stop // SEQ_LEN)
            ],
            axis=0,
        ).astype(bf16)
        there = slice(rows + here.start, rows + here.stop)
        do = do_ref[here, :] * valid
        dr = far_ref[there, :] * valid
        dm_s[here, :own] = do
        dm_s[here, own:] = dr
    dh_s[...] = dot_nn(dm_s[...], w_s[:, cols_in:])
    turn(nb_s, nt_s)
    turn(dm_s, dt_s)

    if not first:
        only(0, acc_load.wait)
    target = out_s if last else acc_s
    size = width // users
    far = users // 4
    zi, xi, ci = user // 4, lax.rem(user // 2, 2), lax.rem(user, 2)
    stores = []

    def ship(lo, wide):
        lanes = pl.ds(lo, wide)
        if not last:
            stores.append(
                pltpu.make_async_copy(
                    acc_s.at[:, lanes], grads_hbm[0].at[:, lanes], store_sems.at[len(stores)]
                )
            )
            only(steps - 1, stores[-1].start)
            return
        keep, send = grads_hbm
        for at, j in enumerate(split_order(far)):
            zd = lax.rem(zi + far - j, far)
            for xs in range(2):
                xd = xi if xs == 0 else 1 - xi
                for cs in range(2):
                    cd = ci if cs == 0 else 1 - ci
                    row = ((zd * 2 + xd) * 2 + cd) * size
                    row = lax.rem(row // own - me + parts, parts) * own + lax.rem(row, own)
                    slot = xs * far + at
                    there = keep if cs == 0 else send
                    stores.append(
                        pltpu.make_async_copy(
                            out_s.at[pl.ds(pl.multiple_of(row, size), size), lanes],
                            there.at[pl.ds(slot * size, size), lanes],
                            store_sems.at[len(stores)],
                        )
                    )
                    only(steps - 1, stores[-1].start)

    def add(lhs, rhs, lo, wide):
        chunk = min(512, width)
        for r in range(0, width, chunk):
            term = dot_nn(lhs[r : r + chunk, :], rhs[...]) + acc_s[r : r + chunk, lo : lo + wide]
            target[r : r + chunk, lo : lo + wide] = term.astype(target.dtype)
        ship(lo, wide)

    block = 4 * HEAD_DIM
    stride = max(1, 8 // histories)
    for lo in range(0, heads, stride):
        hi = min(lo + stride, heads)
        units = [(h, n) for h in range(lo, hi) for n in range(histories)]
        attention(units, masks, g_s, dh_s, slope_s, hb_s, dz_s)
        for h in range(max(0, lo - stride), lo):
            add(nt_s, dz_s.at[:, h * block : (h + 1) * block], h * block, block)
    dn_all = dot_nt(dz_s[...], w_s[:, :cols_in])
    add(dt_s, hb_s, cols_in, heads * HEAD_DIM)
    for here, rstd in zip(halves, rstds):
        dn = dn_all[here, :]
        nf = nb_s[here, :].astype(f32)
        one = jnp.sum(dn, axis=1, keepdims=True) / width
        two = jnp.sum(dn * nf, axis=1, keepdims=True) / width
        branch = (dn - one - nf * two) * rstd
        gx_ref[here, :] = (dm_s[here, :own].astype(f32) + branch[:, :own]).astype(bf16)
        bs_ref[here, :] = branch[:, own:].astype(bf16)
    for h in range((heads - 1) // stride * stride, heads):
        add(nt_s, dz_s.at[:, h * block : (h + 1) * block], h * block, block)

    for copy in stores:
        only(steps - 1, copy.wait)


def group_call(group, blocks, users, lens, where, x, d, far, weights, past):
    start, steps = group
    first, last = start == 0, start + steps == blocks
    rows, own = x.shape[0] // blocks, x.shape[1]
    width, cols = weights.shape
    parts = width // own
    heads = cols // (5 * HEAD_DIM)
    cols_in = heads * 4 * HEAD_DIM
    smem = pl.BlockSpec(memory_space=pltpu.SMEM)
    anywhere = pl.BlockSpec(memory_space=pl.ANY)
    mine = pl.BlockSpec((rows, own), lambda i: (start + i, 0))
    theirs = pl.BlockSpec((2 * rows, width - own), lambda i: (i, 0))
    args = [lens, where, x, d, far, weights] + past
    specs = [smem, smem, mine, mine, theirs] + [anywhere] * (1 + len(past))
    if last:
        grads = [jax.ShapeDtypeStruct((width // 2, cols), bf16)] * 2
    else:
        grads = [jax.ShapeDtypeStruct((width, cols), f32)]
    flops = steps * (4 * rows * width * cols + 2 * rows * width * cols_in)
    return pl.pallas_call(
        functools.partial(group_kernel, start, steps, first, last, heads, parts, users),
        grid=(steps,),
        out_shape=[
            jax.ShapeDtypeStruct((blocks * rows, own), bf16),
            jax.ShapeDtypeStruct((blocks * rows, width - own), bf16),
        ]
        + grads,
        in_specs=specs,
        out_specs=[
            pl.BlockSpec((rows, own), lambda i: (start + i, 0)),
            pl.BlockSpec((rows, width - own), lambda i: (start + i, 0)),
        ]
        + [anywhere] * len(grads),
        input_output_aliases={} if first else {7: 0, 8: 1},
        scratch_shapes=[
            pltpu.VMEM((width, cols), bf16),
            pltpu.VMEM((width, cols), f32),
            pltpu.VMEM((rows, width), bf16),
            pltpu.VMEM((width, rows), bf16),
            pltpu.VMEM((rows, width), bf16),
            pltpu.VMEM((width, rows), bf16),
            pltpu.VMEM((rows, cols_in), bf16),
            pltpu.VMEM((rows, cols - cols_in), bf16),
            pltpu.VMEM((rows, cols_in), bf16),
            pltpu.VMEM((rows, cols_in), f32),
            pltpu.VMEM((rows, cols - cols_in), f32),
            pltpu.VMEM((width, cols) if last else (16, 128), bf16),
            pltpu.SemaphoreType.DMA((parts + 1,)),
            pltpu.SemaphoreType.DMA(((users if last else 1) * (heads + 1),)),
        ],
        compiler_params=pltpu.CompilerParams(vmem_limit_bytes=56 * 2**20),
        cost_estimate=pl.CostEstimate(
            flops=flops, bytes_accessed=16 * 2**20, transcendentals=steps * rows * cols
        ),
    )(*args)


def scatter_parts(keep, send, users):
    far = users // 4
    order = split_order(far)
    size = keep.shape[0] // (2 * far)

    def swap(block, bit):
        return lax.ppermute(block, "user", [(i, i ^ bit) for i in range(users)])

    got = swap(send, 1)

    def both(lo, hi):
        span = slice(lo * size, hi * size)
        return keep[span].astype(f32) + got[span].astype(f32)

    cuts = [(0, 1), (1, far - 1), (far - 1, far)]
    across = [swap(both(far + lo, far + hi).astype(bf16), 2) for lo, hi in cuts]
    moved = []
    for (lo, hi), other in zip(cuts[:2], across):
        near = (both(lo, hi) + other.astype(f32)).astype(bf16)
        for at in range(lo, hi):
            pairs = [(i, (i - 4 * order[at]) % users) for i in range(users)]
            block = near[(at - lo) * size : (at - lo + 1) * size]
            moved.append(lax.ppermute(block, "user", pairs))
    return got, [across[2]] + moved


def finish_kernel(cols_in, kept_ref, sent_ref, *refs):
    terms = refs[:-3]
    gx_ref, win_ref, wout_ref = refs[-3:]
    gx_ref[...] = (kept_ref[...].astype(f32) + sent_ref[...].astype(f32)).astype(bf16)

    @pl.when(pl.program_id(0) == 0)
    def _():
        total = terms[0][...].astype(f32)
        for term in terms[1:]:
            total = total + term[...].astype(f32)
        win_ref[...] = total[:, :cols_in]
        wout_ref[...] = total[:, cols_in:]


def finish(kept, sent, keep, got, rest, cols_in):
    rows, own = kept.shape
    size, cols = rest[0].shape
    slot = keep.shape[0] // (2 * size) - 1
    steps = 4
    lines = pl.BlockSpec((rows // steps, own), lambda i: (i, 0))
    specs = [lines] * 2
    specs += [pl.BlockSpec((size, cols), lambda i: (slot, 0))] * 2
    specs += [pl.BlockSpec((size, cols), lambda i: (0, 0))] * len(rest)
    return pl.pallas_call(
        functools.partial(finish_kernel, cols_in),
        grid=(steps,),
        out_shape=[
            jax.ShapeDtypeStruct((rows, own), bf16),
            jax.ShapeDtypeStruct((size, cols_in), f32),
            jax.ShapeDtypeStruct((size, cols - cols_in), f32),
        ],
        in_specs=specs,
        out_specs=[
            lines,
            pl.BlockSpec((size, cols_in), lambda i: (0, 0)),
            pl.BlockSpec((size, cols - cols_in), lambda i: (0, 0)),
        ],
        compiler_params=pltpu.CompilerParams(vmem_limit_bytes=32 * 2**20),
        cost_estimate=pl.CostEstimate(
            flops=rows * own, bytes_accessed=12 * 2**20, transcendentals=0
        ),
    )(kept, sent, keep, got, *rest)


def exchange(block, tensor):
    if tensor == 2:
        return lax.ppermute(block, "tensor", [(0, 1), (1, 0)])
    own = block.shape[1]
    every = lax.all_gather(block, "tensor", axis=1, tiled=True)
    return jnp.roll(every, -lax.axis_index("tensor") * own, axis=1)[:, own:]


def give_back(block, own, tensor):
    if tensor == 2:
        return lax.ppermute(block, "tensor", [(0, 1), (1, 0)])
    every = jnp.concatenate([jnp.zeros((block.shape[0], own), block.dtype), block], axis=1)
    every = jnp.roll(every, lax.axis_index("tensor") * own, axis=1)
    return lax.psum_scatter(every, "tensor", scatter_dimension=1, tiled=True)


def local(events, cotangent, w_in, w_out, slot_source, slot_length):
    tensor = lax.axis_size("tensor")
    users = lax.axis_size("user")
    hist, seq_len, own = events.shape
    x = events.reshape(hist * seq_len, own)
    d = cotangent.reshape(hist * seq_len, own)
    blocks = sum(steps for _, steps in GROUPS)
    rows = hist // blocks * seq_len
    far, ahead = [], None
    for start, steps in GROUPS:
        spans = [slice(i * rows, (i + 1) * rows) for i in range(start, start + steps)]
        if ahead is not None:
            x, d, _ = lax.optimization_barrier((x, d, ahead))
        ahead = jnp.concatenate([t[span] for span in spans for t in (x, d)], axis=0)
        far.append(exchange(ahead, tensor))

    weights = lax.all_gather(
        jnp.concatenate([w_in, w_out], axis=1), "user", axis=0, tiled=True
    )
    table = lax.all_gather(slot_source * 256 + slot_length, "user", axis=0, tiled=True)
    table = table.reshape(users, hist)
    user = lax.axis_index("user")
    lens = jnp.sum(jnp.where(table // 256 == user, table % 256, 0), axis=0)
    where = jnp.stack([lax.axis_index("tensor"), user]).astype(jnp.int32)

    past = []
    for group, theirs in zip(GROUPS, far):
        kept, bs, *grads = group_call(
            group, blocks, users, lens, where, x, d, theirs, weights, past
        )
        past = grads + [kept, bs]
    sent = give_back(bs, own, tensor)
    keep, send = grads
    got, rest = scatter_parts(keep, send, users)
    grad_x, grad_in, grad_out = finish(kept, sent, keep, got, rest, w_in.shape[1])
    return (grad_x.reshape(hist, seq_len, own), grad_in, grad_out)


def solution(mesh):
    in_specs = (
        P("user", None, "tensor"),
        P("user", None, "tensor"),
        P("user", "tensor"),
        P("user", "tensor"),
        P("user"),
        P("user"),
    )
    out_specs = (P("user", None, "tensor"), P("user", "tensor"), P("user", "tensor"))
    return jax.shard_map(local, mesh=mesh, in_specs=in_specs, out_specs=out_specs, check_vma=False)
```

```python
import functools

import jax
import jax.numpy as jnp
from jax import lax
from jax.experimental import pallas as pl
from jax.experimental.pallas import tpu as pltpu
from jax.sharding import PartitionSpec as P

HEAD_DIM = 128
SEQ_LEN = 128
GROUPS = ((0, 2), (2, 1), (3, 1))

eps = 1e-05
f32 = jnp.float32
bf16 = jnp.bfloat16


def dot_nn(a, b):
    return lax.dot_general(a, b, (((1,), (0,)), ((), ())), preferred_element_type=f32)


def dot_nt(a, b):
    return lax.dot_general(a, b, (((1,), (1,)), ((), ())), preferred_element_type=f32)


def dot_tn(a, b):
    return lax.dot_general(a, b, (((0,), (0,)), ((), ())), preferred_element_type=f32)


def row_mean(t):
    return jnp.mean(t, axis=1, keepdims=True)


def gates(t):
    sig = 0.5 * jnp.tanh(0.5 * t) + 0.5
    silu = t * sig
    return silu, sig + silu * (1.0 - sig)


def attention(pairs, causal, g_s, dh_s, slope_s, hb_s, dz_s):
    scale = HEAD_DIM ** (-0.5)
    spans = [pl.ds(n * SEQ_LEN, SEQ_LEN) for _, n in pairs]
    lanes = [[pl.ds((4 * h + e) * HEAD_DIM, HEAD_DIM) for e in range(4)] for h, _ in pairs]
    heads = [pl.ds(h * HEAD_DIM, HEAD_DIM) for h, _ in pairs]
    every = range(len(pairs))
    def part(i, e):
        return g_s[spans[i], lanes[i][e]]

    s = [dot_nt(part(i, 2), part(i, 3)) * scale for i in every]
    pair = [gates(t) for t in s]
    attn = [jnp.where(causal, silu * (1.0 / SEQ_LEN), 0.0).astype(bf16) for silu, _ in pair]
    slope = [jnp.where(causal, t * (scale / SEQ_LEN), 0.0) for _, t in pair]
    y = [dot_nn(attn[i], part(i, 1)) for i in every]
    cen = [t - row_mean(t) for t in y]
    rstd = [lax.rsqrt(row_mean(t * t) + eps) for t in cen]
    yn = [cen[i] * rstd[i] for i in every]
    uf = [part(i, 0).astype(f32) for i in every]
    dh = [dh_s[spans[i], heads[i]] for i in every]
    dyn = [dh[i] * uf[i] for i in every]
    one = [row_mean(t) for t in dyn]
    two = [row_mean(dyn[i] * yn[i]) for i in every]
    dy = [((dyn[i] - one[i] - yn[i] * two[i]) * rstd[i]).astype(bf16) for i in every]
    grad_a = [dot_nt(dy[i], part(i, 1)) for i in every]
    ds = [(grad_a[i] * slope[i]).astype(bf16) for i in every]

    def store(i, e, grad):
        dz_s[spans[i], lanes[i][e]] = (grad * slope_s[spans[i], lanes[i][e]]).astype(bf16)

    for i in every:
        hb_s[spans[i], heads[i]] = (yn[i] * uf[i]).astype(bf16)
        store(i, 0, dh[i] * yn[i])
    for i in every:
        store(i, 1, dot_tn(attn[i], dy[i]))
    for i in every:
        store(i, 2, dot_nn(ds[i], part(i, 3)))
    for i in every:
        store(i, 3, dot_tn(ds[i], part(i, 2)))


def split_order(count):
    rest = sorted(range(1, count), key=lambda j: abs(j - count / 2))
    return rest + [0]


def piece_order(far):
    slow = [0] + split_order(far)[:-1]
    return [(j, xs, cs) for cs in range(2) for xs in range(2) for j in slow]


def gather_parts(shard, users):
    def swap(block, bit):
        return lax.ppermute(block, "user", [(i, i ^ bit) for i in range(users)])

    pieces = [shard]
    for j in split_order(users // 4)[:-1]:
        pairs = [(i, (i - 4 * j) % users) for i in range(users)]
        pieces.append(lax.ppermute(shard, "user", pairs))
    pieces += [swap(piece, 2) for piece in pieces]
    return pieces + [swap(piece, 1) for piece in pieces]


def group_kernel(start, steps, first, last, heads, parts, users, *refs):
    refs = list(refs)
    lens_ref, where_ref, xo_ref, do_ref, far_ref = refs[:5]
    pieces, refs = refs[5 : 5 + users], refs[5 + users :]
    acc_hbm = None if first else refs.pop(0)
    refs = refs if first else refs[2:]
    gx_ref, bs_ref = refs[:2]
    refs = refs[2:]
    grads_hbm = [refs.pop(0) for _ in range(2 if last else 1)]
    (w_s, acc_s, nb_s, nt_s, dm_s, dt_s, dz_s, hb_s, g_s, slope_s, dh_s, out_s) = refs[:12]
    load_sems, store_sems = refs[12:]
    rows, own = xo_ref.shape
    width = own * parts
    cols_in = heads * 4 * HEAD_DIM
    histories = rows // SEQ_LEN
    me, user = where_ref[0], where_ref[1]
    step = pl.program_id(0)

    def only(index, run):
        if steps == 1:
            run()
        else:
            pl.when(step == index)(run)

    size = width // users
    far = users // 4
    zi, xi, ci = user // 4, lax.rem(user // 2, 2), lax.rem(user, 2)

    def rows_of(j, xs, cs):
        zd = lax.rem(zi + j, far)
        xd = xi if xs == 0 else 1 - xi
        cd = ci if cs == 0 else 1 - ci
        row = ((zd * 2 + xd) * 2 + cd) * size
        row = lax.rem(row // own - me + parts, parts) * own + lax.rem(row, own)
        return pl.ds(pl.multiple_of(row, size), size)

    loads = []
    for piece, (j, xs, cs) in zip(pieces, piece_order(far)):
        loads.append(
            pltpu.make_async_copy(piece, w_s.at[rows_of(j, xs, cs)], load_sems.at[len(loads)])
        )
    if not first:
        acc_load = pltpu.make_async_copy(acc_hbm, acc_s, load_sems.at[users])

    def begin():
        for copy in loads:
            copy.start()
        if first:
            acc_s[...] = jnp.zeros_like(acc_s)
        else:
            acc_load.start()

    def loaded():
        for copy in loads:
            copy.wait()

    only(0, begin)

    causal = lax.broadcasted_iota(jnp.int32, (SEQ_LEN, SEQ_LEN), 0) >= lax.broadcasted_iota(
        jnp.int32, (SEQ_LEN, SEQ_LEN), 1
    )
    position = lax.broadcasted_iota(jnp.int32, (SEQ_LEN, 1), 0)
    half = min(2 * SEQ_LEN, rows)
    halves = [slice(lo, lo + half) for lo in range(0, rows, half)]

    rstds = []
    for here in halves:
        xo = xo_ref[here, :].astype(f32)
        xr = far_ref[here, :].astype(f32)
        mean = (jnp.sum(xo, axis=1, keepdims=True) + jnp.sum(xr, axis=1, keepdims=True)) / width
        xo = xo - mean
        xr = xr - mean
        var = (
            jnp.sum(xo * xo, axis=1, keepdims=True) + jnp.sum(xr * xr, axis=1, keepdims=True)
        ) / width
        rstd = lax.rsqrt(var + eps)
        rstds.append(rstd)
        bo = (xo * rstd).astype(bf16)
        br = (xr * rstd).astype(bf16)
        nb_s[here, :own] = bo
        nb_s[here, own:] = br
        nt_s[:own, here] = bo.T
        nt_s[own:, here] = br.T
    only(0, loaded)
    for h in range(heads):
        c = slice(h * 4 * HEAD_DIM, (h + 1) * 4 * HEAD_DIM)
        silu, slope_s[:, c] = gates(dot_nn(nb_s[...], w_s[:, c]))
        g_s[:, c] = silu.astype(bf16)
    for here in halves:
        base = start * histories + step * histories
        valid = jnp.concatenate(
            [
                (position < lens_ref[base + n]).astype(f32)
                for n in range(here.start // SEQ_LEN, here.stop // SEQ_LEN)
            ],
            axis=0,
        ).astype(bf16)
        there = slice(rows + here.start, rows + here.stop)
        do = do_ref[here, :] * valid
        dr = far_ref[there, :] * valid
        dm_s[here, :own] = do
        dm_s[here, own:] = dr
        dt_s[:own, here] = do.T
        dt_s[own:, here] = dr.T
    dh_s[...] = dot_nn(dm_s[...], w_s[:, cols_in:])

    if not first:
        only(0, acc_load.wait)
    target = out_s if last else acc_s
    stores = []

    def ship(lo, wide):
        lanes = pl.ds(lo, wide)
        if not last:
            stores.append(
                pltpu.make_async_copy(
                    acc_s.at[:, lanes], grads_hbm[0].at[:, lanes], store_sems.at[len(stores)]
                )
            )
            only(steps - 1, stores[-1].start)
            return
        keep, send = grads_hbm
        for at, j in enumerate(split_order(far)):
            for xs in range(2):
                for cs in range(2):
                    there = keep if cs == 0 else send
                    stores.append(
                        pltpu.make_async_copy(
                            out_s.at[rows_of(far - j, xs, cs), lanes],
                            there.at[pl.ds((xs * far + at) * size, size), lanes],
                            store_sems.at[len(stores)],
                        )
                    )
                    only(steps - 1, stores[-1].start)

    def add(lhs, rhs, lo, wide):
        chunk = min(512, width)
        for r in range(0, width, chunk):
            term = dot_nn(lhs[r : r + chunk, :], rhs[...]) + acc_s[r : r + chunk, lo : lo + wide]
            target[r : r + chunk, lo : lo + wide] = term.astype(target.dtype)
        ship(lo, wide)

    block = 4 * HEAD_DIM
    stride = max(1, 8 // histories)
    for lo in range(0, heads, stride):
        hi = min(lo + stride, heads)
        pairs = [(h, n) for h in range(lo, hi) for n in range(histories)]
        attention(pairs, causal, g_s, dh_s, slope_s, hb_s, dz_s)
        for h in range(max(0, lo - stride), lo):
            add(nt_s, dz_s.at[:, h * block : (h + 1) * block], h * block, block)
    dn_all = dot_nt(dz_s[...], w_s[:, :cols_in])
    add(dt_s, hb_s, cols_in, heads * HEAD_DIM)
    for here, rstd in zip(halves, rstds):
        dn = dn_all[here, :]
        nf = nb_s[here, :].astype(f32)
        one = jnp.sum(dn, axis=1, keepdims=True) / width
        two = jnp.sum(dn * nf, axis=1, keepdims=True) / width
        branch = (dn - one - nf * two) * rstd
        gx_ref[here, :] = (dm_s[here, :own].astype(f32) + branch[:, :own]).astype(bf16)
        bs_ref[here, :] = branch[:, own:].astype(bf16)
    for h in range((heads - 1) // stride * stride, heads):
        add(nt_s, dz_s.at[:, h * block : (h + 1) * block], h * block, block)

    for copy in stores:
        only(steps - 1, copy.wait)


def group_call(group, blocks, users, parts, lens, where, x, d, far, pieces, past):
    start, steps = group
    first, last = start == 0, start + steps == blocks
    rows, own = x.shape[0] // blocks, x.shape[1]
    width, cols = own * parts, pieces[0].shape[1]
    heads = cols // (5 * HEAD_DIM)
    cols_in = heads * 4 * HEAD_DIM
    smem = pl.BlockSpec(memory_space=pltpu.SMEM)
    anywhere = pl.BlockSpec(memory_space=pl.ANY)
    mine = pl.BlockSpec((rows, own), lambda i: (start + i, 0))
    theirs = pl.BlockSpec((2 * rows, width - own), lambda i: (i, 0))
    args = [lens, where, x, d, far] + pieces + past
    specs = [smem, smem, mine, mine, theirs] + [anywhere] * (users + len(past))
    if last:
        grads = [jax.ShapeDtypeStruct((width // 2, cols), bf16)] * 2
    else:
        grads = [jax.ShapeDtypeStruct((width, cols), f32)]
    flops = steps * (4 * rows * width * cols + 2 * rows * width * cols_in)
    return pl.pallas_call(
        functools.partial(group_kernel, start, steps, first, last, heads, parts, users),
        grid=(steps,),
        out_shape=[
            jax.ShapeDtypeStruct((blocks * rows, own), bf16),
            jax.ShapeDtypeStruct((blocks * rows, width - own), bf16),
        ]
        + grads,
        in_specs=specs,
        out_specs=[
            pl.BlockSpec((rows, own), lambda i: (start + i, 0)),
            pl.BlockSpec((rows, width - own), lambda i: (start + i, 0)),
        ]
        + [anywhere] * len(grads),
        input_output_aliases={} if first else {users + 6: 0, users + 7: 1},
        scratch_shapes=[
            pltpu.VMEM((width, cols), bf16),
            pltpu.VMEM((width, cols), f32),
            pltpu.VMEM((rows, width), bf16),
            pltpu.VMEM((width, rows), bf16),
            pltpu.VMEM((rows, width), bf16),
            pltpu.VMEM((width, rows), bf16),
            pltpu.VMEM((rows, cols_in), bf16),
            pltpu.VMEM((rows, cols - cols_in), bf16),
            pltpu.VMEM((rows, cols_in), bf16),
            pltpu.VMEM((rows, cols_in), f32),
            pltpu.VMEM((rows, cols - cols_in), f32),
            pltpu.VMEM((width, cols) if last else (16, 128), bf16),
            pltpu.SemaphoreType.DMA((users + 1,)),
            pltpu.SemaphoreType.DMA(((users if last else 1) * (heads + 1),)),
        ],
        compiler_params=pltpu.CompilerParams(vmem_limit_bytes=56 * 2**20),
        cost_estimate=pl.CostEstimate(
            flops=flops, bytes_accessed=16 * 2**20, transcendentals=steps * rows * cols
        ),
    )(*args)


def scatter_parts(keep, send, users):
    far = users // 4
    order = split_order(far)
    size = keep.shape[0] // (2 * far)

    def swap(block, bit):
        return lax.ppermute(block, "user", [(i, i ^ bit) for i in range(users)])

    got = swap(send, 1)

    def both(lo, hi):
        span = slice(lo * size, hi * size)
        return keep[span].astype(f32) + got[span].astype(f32)

    cuts = [(0, 1), (1, far - 1), (far - 1, far)]
    across = [swap(both(far + lo, far + hi).astype(bf16), 2) for lo, hi in cuts]
    moved = []
    for (lo, hi), other in zip(cuts[:2], across):
        near = (both(lo, hi) + other.astype(f32)).astype(bf16)
        for at in range(lo, hi):
            pairs = [(i, (i - 4 * order[at]) % users) for i in range(users)]
            block = near[(at - lo) * size : (at - lo + 1) * size]
            moved.append(lax.ppermute(block, "user", pairs))
    return got, [across[2]] + moved


def finish_kernel(cols_in, kept_ref, sent_ref, *refs):
    terms = refs[:-3]
    gx_ref, win_ref, wout_ref = refs[-3:]
    gx_ref[...] = (kept_ref[...].astype(f32) + sent_ref[...].astype(f32)).astype(bf16)

    @pl.when(pl.program_id(0) == 0)
    def _():
        total = terms[0][...].astype(f32)
        for term in terms[1:]:
            total = total + term[...].astype(f32)
        win_ref[...] = total[:, :cols_in]
        wout_ref[...] = total[:, cols_in:]


def finish(kept, sent, keep, got, rest, cols_in):
    rows, own = kept.shape
    size, cols = rest[0].shape
    slot = keep.shape[0] // (2 * size) - 1
    steps = 4
    lines = pl.BlockSpec((rows // steps, own), lambda i: (i, 0))
    specs = [lines] * 2
    specs += [pl.BlockSpec((size, cols), lambda i: (slot, 0))] * 2
    specs += [pl.BlockSpec((size, cols), lambda i: (0, 0))] * len(rest)
    return pl.pallas_call(
        functools.partial(finish_kernel, cols_in),
        grid=(steps,),
        out_shape=[
            jax.ShapeDtypeStruct((rows, own), bf16),
            jax.ShapeDtypeStruct((size, cols_in), f32),
            jax.ShapeDtypeStruct((size, cols - cols_in), f32),
        ],
        in_specs=specs,
        out_specs=[
            lines,
            pl.BlockSpec((size, cols_in), lambda i: (0, 0)),
            pl.BlockSpec((size, cols - cols_in), lambda i: (0, 0)),
        ],
        compiler_params=pltpu.CompilerParams(vmem_limit_bytes=32 * 2**20),
        cost_estimate=pl.CostEstimate(
            flops=rows * own, bytes_accessed=12 * 2**20, transcendentals=0
        ),
    )(kept, sent, keep, got, *rest)


def exchange(block, tensor):
    if tensor == 2:
        return lax.ppermute(block, "tensor", [(0, 1), (1, 0)])
    own = block.shape[1]
    every = lax.all_gather(block, "tensor", axis=1, tiled=True)
    return jnp.roll(every, -lax.axis_index("tensor") * own, axis=1)[:, own:]


def give_back(block, own, tensor):
    if tensor == 2:
        return lax.ppermute(block, "tensor", [(0, 1), (1, 0)])
    every = jnp.concatenate([jnp.zeros((block.shape[0], own), block.dtype), block], axis=1)
    every = jnp.roll(every, lax.axis_index("tensor") * own, axis=1)
    return lax.psum_scatter(every, "tensor", scatter_dimension=1, tiled=True)


def local(events, cotangent, w_in, w_out, slot_source, slot_length):
    tensor = lax.axis_size("tensor")
    users = lax.axis_size("user")
    hist, seq_len, own = events.shape
    x = events.reshape(hist * seq_len, own)
    d = cotangent.reshape(hist * seq_len, own)
    blocks = sum(steps for _, steps in GROUPS)
    rows = hist // blocks * seq_len
    far, ahead = [], None
    for start, steps in GROUPS:
        spans = [slice(i * rows, (i + 1) * rows) for i in range(start, start + steps)]
        if ahead is not None:
            x, d, _ = lax.optimization_barrier((x, d, ahead))
        ahead = jnp.concatenate([t[span] for span in spans for t in (x, d)], axis=0)
        far.append(exchange(ahead, tensor))

    pieces = gather_parts(jnp.concatenate([w_in, w_out], axis=1), users)
    slots = jnp.pad((slot_source * 256 + slot_length)[None], ((0, 7), (0, 128 - hist)))
    table = lax.all_gather(slots, "user", axis=0, tiled=True)
    table = table.reshape(users, 8, 128)[:, 0, :hist]
    user = lax.axis_index("user")
    lens = jnp.sum(jnp.where(table // 256 == user, table % 256, 0), axis=0)
    where = jnp.stack([lax.axis_index("tensor"), user]).astype(jnp.int32)

    past = []
    for group, theirs in zip(GROUPS, far):
        kept, bs, *grads = group_call(
            group, blocks, users, tensor, lens, where, x, d, theirs, pieces, past
        )
        past = grads + [kept, bs]
    sent = give_back(bs, own, tensor)
    keep, send = grads
    got, rest = scatter_parts(keep, send, users)
    grad_x, grad_in, grad_out = finish(kept, sent, keep, got, rest, w_in.shape[1])
    return (grad_x.reshape(hist, seq_len, own), grad_in, grad_out)


def solution(mesh):
    in_specs = (
        P("user", None, "tensor"),
        P("user", None, "tensor"),
        P("user", "tensor"),
        P("user", "tensor"),
        P("user"),
        P("user"),
    )
    out_specs = (P("user", None, "tensor"), P("user", "tensor"), P("user", "tensor"))
    return jax.shard_map(local, mesh=mesh, in_specs=in_specs, out_specs=out_specs, check_vma=False)
```

```python
import functools

import jax
import jax.numpy as jnp
from jax import lax
from jax.experimental import pallas as pl
from jax.experimental.pallas import tpu as pltpu
from jax.sharding import PartitionSpec as P

HEAD_DIM = 128
SEQ_LEN = 128
SLOTS = 128
GROUPS = ((0, 2), (2, 1), (3, 1))

eps = 1e-05
f32 = jnp.float32
bf16 = jnp.bfloat16


def dot_nn(a, b):
    return lax.dot_general(a, b, (((1,), (0,)), ((), ())), preferred_element_type=f32)


def dot_nt(a, b):
    return lax.dot_general(a, b, (((1,), (1,)), ((), ())), preferred_element_type=f32)


def dot_tn(a, b):
    return lax.dot_general(a, b, (((0,), (0,)), ((), ())), preferred_element_type=f32)


def row_mean(t):
    return jnp.mean(t, axis=1, keepdims=True)


def gates(t):
    sig = 0.5 * jnp.tanh(0.5 * t) + 0.5
    silu = t * sig
    return silu, sig + silu * (1.0 - sig)


def attention(pairs, causal, g_s, dh_s, slope_s, hb_s, dz_s):
    scale = HEAD_DIM ** (-0.5)
    spans = [pl.ds(n * SEQ_LEN, SEQ_LEN) for _, n in pairs]
    lanes = [[pl.ds((4 * h + e) * HEAD_DIM, HEAD_DIM) for e in range(4)] for h, _ in pairs]
    heads = [pl.ds(h * HEAD_DIM, HEAD_DIM) for h, _ in pairs]
    every = range(len(pairs))
    def part(i, e):
        return g_s[spans[i], lanes[i][e]]

    s = [dot_nt(part(i, 2), part(i, 3)) * scale for i in every]
    pair = [gates(t) for t in s]
    attn = [jnp.where(causal, silu * (1.0 / SEQ_LEN), 0.0).astype(bf16) for silu, _ in pair]
    slope = [jnp.where(causal, t * (scale / SEQ_LEN), 0.0) for _, t in pair]
    y = [dot_nn(attn[i], part(i, 1)) for i in every]
    cen = [t - row_mean(t) for t in y]
    rstd = [lax.rsqrt(row_mean(t * t) + eps) for t in cen]
    yn = [cen[i] * rstd[i] for i in every]
    uf = [part(i, 0).astype(f32) for i in every]
    dh = [dh_s[spans[i], heads[i]] for i in every]
    dyn = [dh[i] * uf[i] for i in every]
    one = [row_mean(t) for t in dyn]
    two = [row_mean(dyn[i] * yn[i]) for i in every]
    dy = [((dyn[i] - one[i] - yn[i] * two[i]) * rstd[i]).astype(bf16) for i in every]
    grad_a = [dot_nt(dy[i], part(i, 1)) for i in every]
    ds = [(grad_a[i] * slope[i]).astype(bf16) for i in every]

    def store(i, e, grad):
        dz_s[spans[i], lanes[i][e]] = (grad * slope_s[spans[i], lanes[i][e]]).astype(bf16)

    for i in every:
        hb_s[spans[i], heads[i]] = (yn[i] * uf[i]).astype(bf16)
        store(i, 0, dh[i] * yn[i])
    for i in every:
        store(i, 1, dot_tn(attn[i], dy[i]))
    for i in every:
        store(i, 2, dot_nn(ds[i], part(i, 3)))
    for i in every:
        store(i, 3, dot_tn(ds[i], part(i, 2)))


def split_order(count):
    rest = sorted(range(1, count), key=lambda j: abs(j - count / 2))
    return rest + [0]


def piece_order(far):
    slow = [0] + split_order(far)[:-1]
    return [(j, xs, cs) for cs in range(2) for xs in range(2) for j in slow]


def gather_parts(shard, users):
    def swap(block, bit):
        return lax.ppermute(block, "user", [(i, i ^ bit) for i in range(users)])

    pieces = [shard]
    for j in split_order(users // 4)[:-1]:
        pairs = [(i, (i - 4 * j) % users) for i in range(users)]
        pieces.append(lax.ppermute(shard, "user", pairs))
    pieces += [swap(piece, 2) for piece in pieces]
    return pieces + [swap(piece, 1) for piece in pieces]


def group_kernel(start, steps, first, last, heads, parts, users, *refs):
    refs = list(refs)
    where_ref, xo_ref, do_ref, far_ref = refs[:4]
    pieces, refs = refs[4 : 4 + users], refs[4 + users :]
    acc_hbm = None if first else refs.pop(0)
    refs = refs if first else refs[2:]
    gx_ref, bs_ref = refs[:2]
    refs = refs[2:]
    grads_hbm = [refs.pop(0) for _ in range(2 if last else 1)]
    (w_s, acc_s, nb_s, nt_s, dm_s, dt_s, dz_s, hb_s, g_s, slope_s, dh_s, out_s) = refs[:12]
    load_sems, store_sems = refs[12:]
    rows, own = xo_ref.shape
    width = own * parts
    cols_in = heads * 4 * HEAD_DIM
    cols = cols_in + heads * HEAD_DIM
    histories = rows // SEQ_LEN
    me, user = where_ref[0], where_ref[1]
    step = pl.program_id(0)

    def only(index, run):
        if steps == 1:
            run()
        else:
            pl.when(step == index)(run)

    size = width // users
    far = users // 4
    zi, xi, ci = user // 4, lax.rem(user // 2, 2), lax.rem(user, 2)

    def rows_of(j, xs, cs):
        zd = lax.rem(zi + j, far)
        xd = xi if xs == 0 else 1 - xi
        cd = ci if cs == 0 else 1 - ci
        row = ((zd * 2 + xd) * 2 + cd) * size
        row = lax.rem(row // own - me + parts, parts) * own + lax.rem(row, own)
        return pl.ds(pl.multiple_of(row, size), size)

    loads = []
    for piece, (j, xs, cs) in zip(pieces, piece_order(far)):
        loads.append(
            pltpu.make_async_copy(piece, w_s.at[rows_of(j, xs, cs)], load_sems.at[len(loads)])
        )
    if not first:
        acc_load = pltpu.make_async_copy(acc_hbm, acc_s, load_sems.at[users])

    def begin():
        for copy in loads:
            copy.start()
        if first:
            acc_s[...] = jnp.zeros_like(acc_s)
        else:
            acc_load.start()

    def loaded():
        for copy in loads:
            copy.wait()

    only(0, begin)

    causal = lax.broadcasted_iota(jnp.int32, (SEQ_LEN, SEQ_LEN), 0) >= lax.broadcasted_iota(
        jnp.int32, (SEQ_LEN, SEQ_LEN), 1
    )
    position = lax.broadcasted_iota(jnp.int32, (SEQ_LEN, 1), 0).astype(f32)
    half = min(2 * SEQ_LEN, rows)
    halves = [slice(lo, lo + half) for lo in range(0, rows, half)]

    rstds = []
    for here in halves:
        xo = xo_ref[here, :].astype(f32)
        xr = far_ref[here, :].astype(f32)
        mean = (jnp.sum(xo, axis=1, keepdims=True) + jnp.sum(xr, axis=1, keepdims=True)) / width
        xo = xo - mean
        xr = xr - mean
        var = (
            jnp.sum(xo * xo, axis=1, keepdims=True) + jnp.sum(xr * xr, axis=1, keepdims=True)
        ) / width
        rstd = lax.rsqrt(var + eps)
        rstds.append(rstd)
        bo = (xo * rstd).astype(bf16)
        br = (xr * rstd).astype(bf16)
        nb_s[here, :own] = bo
        nb_s[here, own:] = br
        nt_s[:own, here] = bo.T
        nt_s[own:, here] = br.T
    only(0, loaded)
    for h in range(heads):
        c = slice(h * 4 * HEAD_DIM, (h + 1) * 4 * HEAD_DIM)
        silu, slope_s[:, c] = gates(dot_nn(nb_s[...], w_s[:, c]))
        g_s[:, c] = silu.astype(bf16)
    table = w_s[:, cols:].astype(f32)
    lengths = pltpu.roll(table, SLOTS // 2, 1)
    lane = lax.broadcasted_iota(jnp.int32, (1, SLOTS), 1)
    lengths = jnp.where(table == user.astype(f32), lengths, 0.0)
    lengths = jnp.sum(lengths, axis=0, keepdims=True)
    for here in halves:
        base = start * histories + step * histories
        valid = jnp.concatenate(
            [
                (
                    position
                    < jnp.sum(jnp.where(lane == base + n, lengths, 0.0), axis=1, keepdims=True)
                ).astype(f32)
                for n in range(here.start // SEQ_LEN, here.stop // SEQ_LEN)
            ],
            axis=0,
        ).astype(bf16)
        there = slice(rows + here.start, rows + here.stop)
        do = do_ref[here, :] * valid
        dr = far_ref[there, :] * valid
        dm_s[here, :own] = do
        dm_s[here, own:] = dr
        dt_s[:own, here] = do.T
        dt_s[own:, here] = dr.T
    dh_s[...] = dot_nn(dm_s[...], w_s[:, cols_in:cols])

    if not first:
        only(0, acc_load.wait)
    target = out_s if last else acc_s
    stores = []

    def ship(lo, wide):
        lanes = pl.ds(lo, wide)
        if not last:
            stores.append(
                pltpu.make_async_copy(
                    acc_s.at[:, lanes], grads_hbm[0].at[:, lanes], store_sems.at[len(stores)]
                )
            )
            only(steps - 1, stores[-1].start)
            return
        keep, send = grads_hbm
        for at, j in enumerate(split_order(far)):
            for xs in range(2):
                for cs in range(2):
                    there = keep if cs == 0 else send
                    stores.append(
                        pltpu.make_async_copy(
                            out_s.at[rows_of(far - j, xs, cs), lanes],
                            there.at[pl.ds((xs * far + at) * size, size), lanes],
                            store_sems.at[len(stores)],
                        )
                    )
                    only(steps - 1, stores[-1].start)

    def add(lhs, rhs, lo, wide):
        chunk = min(512, width)
        for r in range(0, width, chunk):
            term = dot_nn(lhs[r : r + chunk, :], rhs[...]) + acc_s[r : r + chunk, lo : lo + wide]
            target[r : r + chunk, lo : lo + wide] = term.astype(target.dtype)
        ship(lo, wide)

    block = 4 * HEAD_DIM
    stride = max(1, 8 // histories)
    for lo in range(0, heads, stride):
        hi = min(lo + stride, heads)
        pairs = [(h, n) for h in range(lo, hi) for n in range(histories)]
        attention(pairs, causal, g_s, dh_s, slope_s, hb_s, dz_s)
        for h in range(max(0, lo - stride), lo):
            add(nt_s, dz_s.at[:, h * block : (h + 1) * block], h * block, block)
    dn_all = dot_nt(dz_s[...], w_s[:, :cols_in])
    add(dt_s, hb_s, cols_in, heads * HEAD_DIM)
    for here, rstd in zip(halves, rstds):
        dn = dn_all[here, :]
        nf = nb_s[here, :].astype(f32)
        one = jnp.sum(dn, axis=1, keepdims=True) / width
        two = jnp.sum(dn * nf, axis=1, keepdims=True) / width
        branch = (dn - one - nf * two) * rstd
        gx_ref[here, :] = (dm_s[here, :own].astype(f32) + branch[:, :own]).astype(bf16)
        bs_ref[here, :] = branch[:, own:].astype(bf16)
    for h in range((heads - 1) // stride * stride, heads):
        add(nt_s, dz_s.at[:, h * block : (h + 1) * block], h * block, block)

    for copy in stores:
        only(steps - 1, copy.wait)


def group_call(group, blocks, users, parts, where, x, d, far, pieces, past):
    start, steps = group
    first, last = start == 0, start + steps == blocks
    rows, own = x.shape[0] // blocks, x.shape[1]
    width, cols = own * parts, pieces[0].shape[1] - SLOTS
    heads = cols // (5 * HEAD_DIM)
    cols_in = heads * 4 * HEAD_DIM
    smem = pl.BlockSpec(memory_space=pltpu.SMEM)
    anywhere = pl.BlockSpec(memory_space=pl.ANY)
    mine = pl.BlockSpec((rows, own), lambda i: (start + i, 0))
    theirs = pl.BlockSpec((2 * rows, width - own), lambda i: (i, 0))
    args = [where, x, d, far] + pieces + past
    specs = [smem, mine, mine, theirs] + [anywhere] * (users + len(past))
    if last:
        grads = [jax.ShapeDtypeStruct((width // 2, cols), bf16)] * 2
    else:
        grads = [jax.ShapeDtypeStruct((width, cols), f32)]
    flops = steps * (4 * rows * width * cols + 2 * rows * width * cols_in)
    return pl.pallas_call(
        functools.partial(group_kernel, start, steps, first, last, heads, parts, users),
        grid=(steps,),
        out_shape=[
            jax.ShapeDtypeStruct((blocks * rows, own), bf16),
            jax.ShapeDtypeStruct((blocks * rows, width - own), bf16),
        ]
        + grads,
        in_specs=specs,
        out_specs=[
            pl.BlockSpec((rows, own), lambda i: (start + i, 0)),
            pl.BlockSpec((rows, width - own), lambda i: (start + i, 0)),
        ]
        + [anywhere] * len(grads),
        input_output_aliases={} if first else {users + 5: 0, users + 6: 1},
        scratch_shapes=[
            pltpu.VMEM((width, cols + SLOTS), bf16),
            pltpu.VMEM((width, cols), f32),
            pltpu.VMEM((rows, width), bf16),
            pltpu.VMEM((width, rows), bf16),
            pltpu.VMEM((rows, width), bf16),
            pltpu.VMEM((width, rows), bf16),
            pltpu.VMEM((rows, cols_in), bf16),
            pltpu.VMEM((rows, cols - cols_in), bf16),
            pltpu.VMEM((rows, cols_in), bf16),
            pltpu.VMEM((rows, cols_in), f32),
            pltpu.VMEM((rows, cols - cols_in), f32),
            pltpu.VMEM((width, cols) if last else (16, 128), bf16),
            pltpu.SemaphoreType.DMA((users + 1,)),
            pltpu.SemaphoreType.DMA(((users if last else 1) * (heads + 1),)),
        ],
        compiler_params=pltpu.CompilerParams(vmem_limit_bytes=56 * 2**20),
        cost_estimate=pl.CostEstimate(
            flops=flops, bytes_accessed=16 * 2**20, transcendentals=steps * rows * cols
        ),
    )(*args)


def scatter_parts(keep, send, users):
    far = users // 4
    order = split_order(far)
    size = keep.shape[0] // (2 * far)

    def swap(block, bit):
        return lax.ppermute(block, "user", [(i, i ^ bit) for i in range(users)])

    got = swap(send, 1)

    def both(lo, hi):
        span = slice(lo * size, hi * size)
        return keep[span].astype(f32) + got[span].astype(f32)

    cuts = [(0, 1), (1, far - 1), (far - 1, far)]
    across = [swap(both(far + lo, far + hi).astype(bf16), 2) for lo, hi in cuts]
    moved = []
    for (lo, hi), other in zip(cuts[:2], across):
        near = (both(lo, hi) + other.astype(f32)).astype(bf16)
        for at in range(lo, hi):
            pairs = [(i, (i - 4 * order[at]) % users) for i in range(users)]
            block = near[(at - lo) * size : (at - lo + 1) * size]
            moved.append(lax.ppermute(block, "user", pairs))
    return got, [across[2]] + moved


def finish_kernel(cols_in, kept_ref, sent_ref, *refs):
    terms = refs[:-3]
    gx_ref, win_ref, wout_ref = refs[-3:]
    gx_ref[...] = (kept_ref[...].astype(f32) + sent_ref[...].astype(f32)).astype(bf16)

    @pl.when(pl.program_id(0) == 0)
    def _():
        total = terms[0][...].astype(f32)
        for term in terms[1:]:
            total = total + term[...].astype(f32)
        win_ref[...] = total[:, :cols_in]
        wout_ref[...] = total[:, cols_in:]


def finish(kept, sent, keep, got, rest, cols_in):
    rows, own = kept.shape
    size, cols = rest[0].shape
    slot = keep.shape[0] // (2 * size) - 1
    steps = 4
    lines = pl.BlockSpec((rows // steps, own), lambda i: (i, 0))
    specs = [lines] * 2
    specs += [pl.BlockSpec((size, cols), lambda i: (slot, 0))] * 2
    specs += [pl.BlockSpec((size, cols), lambda i: (0, 0))] * len(rest)
    return pl.pallas_call(
        functools.partial(finish_kernel, cols_in),
        grid=(steps,),
        out_shape=[
            jax.ShapeDtypeStruct((rows, own), bf16),
            jax.ShapeDtypeStruct((size, cols_in), f32),
            jax.ShapeDtypeStruct((size, cols - cols_in), f32),
        ],
        in_specs=specs,
        out_specs=[
            lines,
            pl.BlockSpec((size, cols_in), lambda i: (0, 0)),
            pl.BlockSpec((size, cols - cols_in), lambda i: (0, 0)),
        ],
        compiler_params=pltpu.CompilerParams(vmem_limit_bytes=32 * 2**20),
        cost_estimate=pl.CostEstimate(
            flops=rows * own, bytes_accessed=12 * 2**20, transcendentals=0
        ),
    )(kept, sent, keep, got, *rest)


def exchange(block, tensor):
    if tensor == 2:
        return lax.ppermute(block, "tensor", [(0, 1), (1, 0)])
    own = block.shape[1]
    every = lax.all_gather(block, "tensor", axis=1, tiled=True)
    return jnp.roll(every, -lax.axis_index("tensor") * own, axis=1)[:, own:]


def give_back(block, own, tensor):
    if tensor == 2:
        return lax.ppermute(block, "tensor", [(0, 1), (1, 0)])
    every = jnp.concatenate([jnp.zeros((block.shape[0], own), block.dtype), block], axis=1)
    every = jnp.roll(every, lax.axis_index("tensor") * own, axis=1)
    return lax.psum_scatter(every, "tensor", scatter_dimension=1, tiled=True)


def local(events, cotangent, w_in, w_out, slot_source, slot_length):
    tensor = lax.axis_size("tensor")
    users = lax.axis_size("user")
    hist, seq_len, own = events.shape
    x = events.reshape(hist * seq_len, own)
    d = cotangent.reshape(hist * seq_len, own)
    blocks = sum(steps for _, steps in GROUPS)
    rows = hist // blocks * seq_len
    far, ahead = [], None
    for start, steps in GROUPS:
        spans = [slice(i * rows, (i + 1) * rows) for i in range(start, start + steps)]
        if ahead is not None:
            x, d, _ = lax.optimization_barrier((x, d, ahead))
        ahead = jnp.concatenate([t[span] for span in spans for t in (x, d)], axis=0)
        far.append(exchange(ahead, tensor))

    user = lax.axis_index("user")
    slots = jnp.stack([slot_source, slot_length]).astype(bf16)
    slots = jnp.pad(slots, ((0, 0), (0, SLOTS // 2 - hist)), constant_values=-1)
    slots = jnp.pad(slots.reshape(1, SLOTS), ((0, w_in.shape[0] - 1), (0, 0)), constant_values=-1)
    pieces = gather_parts(jnp.concatenate([w_in, w_out, slots], axis=1), users)
    where = jnp.stack([lax.axis_index("tensor"), user]).astype(jnp.int32)

    past = []
    for group, theirs in zip(GROUPS, far):
        kept, bs, *grads = group_call(
            group, blocks, users, tensor, where, x, d, theirs, pieces, past
        )
        past = grads + [kept, bs]
    sent = give_back(bs, own, tensor)
    keep, send = grads
    got, rest = scatter_parts(keep, send, users)
    grad_x, grad_in, grad_out = finish(kept, sent, keep, got, rest, w_in.shape[1])
    return (grad_x.reshape(hist, seq_len, own), grad_in, grad_out)


def solution(mesh):
    in_specs = (
        P("user", None, "tensor"),
        P("user", None, "tensor"),
        P("user", "tensor"),
        P("user", "tensor"),
        P("user"),
        P("user"),
    )
    out_specs = (P("user", None, "tensor"), P("user", "tensor"), P("user", "tensor"))
    return jax.shard_map(local, mesh=mesh, in_specs=in_specs, out_specs=out_specs, check_vma=False)
```

```python
import functools

import jax
import jax.numpy as jnp
from jax import lax
from jax.experimental import pallas as pl
from jax.experimental.pallas import tpu as pltpu
from jax.sharding import PartitionSpec as P

HEAD_DIM = 128
SEQ_LEN = 128
SLOTS = 128
GROUPS = ((0, 2), (2, 1), (3, 1))

eps = 1e-05
f32 = jnp.float32
bf16 = jnp.bfloat16


def dot_nn(a, b):
    return lax.dot_general(a, b, (((1,), (0,)), ((), ())), preferred_element_type=f32)


def dot_nt(a, b):
    return lax.dot_general(a, b, (((1,), (1,)), ((), ())), preferred_element_type=f32)


def dot_tn(a, b):
    return lax.dot_general(a, b, (((0,), (0,)), ((), ())), preferred_element_type=f32)


def row_mean(t):
    return jnp.mean(t, axis=1, keepdims=True)


def gates(t):
    sig = 0.5 * jnp.tanh(0.5 * t) + 0.5
    silu = t * sig
    return silu, sig + silu * (1.0 - sig)


def attention(pairs, causal, g_s, dh_s, slope_s, hb_s, dz_s):
    scale = HEAD_DIM ** (-0.5)
    spans = [pl.ds(n * SEQ_LEN, SEQ_LEN) for _, n in pairs]
    lanes = [[pl.ds((4 * h + e) * HEAD_DIM, HEAD_DIM) for e in range(4)] for h, _ in pairs]
    heads = [pl.ds(h * HEAD_DIM, HEAD_DIM) for h, _ in pairs]
    every = range(len(pairs))
    def part(i, e):
        return g_s[spans[i], lanes[i][e]]

    s = [dot_nt(part(i, 2), part(i, 3)) * scale for i in every]
    pair = [gates(t) for t in s]
    attn = [jnp.where(causal, silu * (1.0 / SEQ_LEN), 0.0).astype(bf16) for silu, _ in pair]
    slope = [jnp.where(causal, t * (scale / SEQ_LEN), 0.0) for _, t in pair]
    y = [dot_nn(attn[i], part(i, 1)) for i in every]
    cen = [t - row_mean(t) for t in y]
    rstd = [lax.rsqrt(row_mean(t * t) + eps) for t in cen]
    yn = [cen[i] * rstd[i] for i in every]
    uf = [part(i, 0).astype(f32) for i in every]
    dh = [dh_s[spans[i], heads[i]] for i in every]
    dyn = [dh[i] * uf[i] for i in every]
    one = [row_mean(t) for t in dyn]
    two = [row_mean(dyn[i] * yn[i]) for i in every]
    dy = [((dyn[i] - one[i] - yn[i] * two[i]) * rstd[i]).astype(bf16) for i in every]
    grad_a = [dot_nt(dy[i], part(i, 1)) for i in every]
    ds = [(grad_a[i] * slope[i]).astype(bf16) for i in every]

    def store(i, e, grad):
        dz_s[spans[i], lanes[i][e]] = (grad * slope_s[spans[i], lanes[i][e]]).astype(bf16)

    for i in every:
        hb_s[spans[i], heads[i]] = (yn[i] * uf[i]).astype(bf16)
        store(i, 0, dh[i] * yn[i])
    for i in every:
        store(i, 1, dot_tn(attn[i], dy[i]))
    for i in every:
        store(i, 2, dot_nn(ds[i], part(i, 3)))
    for i in every:
        store(i, 3, dot_tn(ds[i], part(i, 2)))


def split_order(count):
    rest = sorted(range(1, count), key=lambda j: abs(j - count / 2))
    return rest + [0]


def piece_order(far, cut):
    slow = split_order(far)[:-1]
    return [
        (lo, [(j, xs, cs) for j in js])
        for lo, js in ((0, [0]), (0, slow), (cut, slow))
        for cs in range(2)
        for xs in range(2)
    ]


def gather_parts(shard, cut, users, user):
    def swap(block, bit):
        return lax.ppermute(block, "user", [(i, i ^ bit) for i in range(users)])

    def spread(block):
        across = swap(block, 2)
        return [block, across, swap(block, 1), swap(across, 1)]

    arrays, moved = spread(shard), []
    for part in (shard[:, :cut], shard[:, cut:]):
        if moved:
            part = jnp.where(user < 0, sum(t[:1, :1] for t in moved), part)
        moved = []
        for j in split_order(users // 4)[:-1]:
            pairs = [(i, (i - 4 * j) % users) for i in range(users)]
            moved.append(lax.ppermute(part, "user", pairs))
        block = jnp.concatenate(moved, axis=0)
        block = jnp.where(user < 0, arrays[-3][:1, :1], block)
        arrays += spread(block)
    return arrays


def group_kernel(start, steps, first, last, heads, parts, users, *refs):
    refs = list(refs)
    where_ref, xo_ref, do_ref, far_ref = refs[:4]
    pieces, refs = refs[4:16], refs[16:]
    acc_hbm = None if first else refs.pop(0)
    refs = refs if first else refs[2:]
    gx_ref, bs_ref = refs[:2]
    refs = refs[2:]
    grads_hbm = [refs.pop(0) for _ in range(2 if last else 1)]
    (w_s, acc_s, nb_s, nt_s, dm_s, dt_s, dz_s, hb_s, g_s, slope_s, dh_s, out_s) = refs[:12]
    load_sems, store_sems = refs[12:]
    rows, own = xo_ref.shape
    width = own * parts
    cols_in = heads * 4 * HEAD_DIM
    cols = cols_in + heads * HEAD_DIM
    histories = rows // SEQ_LEN
    me, user = where_ref[0], where_ref[1]
    step = pl.program_id(0)

    def only(index, run):
        if steps == 1:
            run()
        else:
            pl.when(step == index)(run)

    size = width // users
    far = users // 4
    zi, xi, ci = user // 4, lax.rem(user // 2, 2), lax.rem(user, 2)

    def rows_of(j, xs, cs):
        zd = lax.rem(zi + j, far)
        xd = xi if xs == 0 else 1 - xi
        cd = ci if cs == 0 else 1 - ci
        row = ((zd * 2 + xd) * 2 + cd) * size
        row = lax.rem(row // own - me + parts, parts) * own + lax.rem(row, own)
        return pl.ds(pl.multiple_of(row, size), size)

    loads = []
    for piece, (lo, offsets) in zip(pieces, piece_order(far, pieces[4].shape[1])):
        for at, offset in enumerate(offsets):
            there = w_s.at[rows_of(*offset), pl.ds(lo, piece.shape[1])]
            here = piece.at[pl.ds(at * size, size)]
            loads.append(pltpu.make_async_copy(here, there, load_sems.at[len(loads)]))
    if not first:
        acc_load = pltpu.make_async_copy(acc_hbm, acc_s, load_sems.at[2 * users])

    def begin():
        for copy in loads:
            copy.start()
        if first:
            acc_s[...] = jnp.zeros_like(acc_s)
        else:
            acc_load.start()

    def loaded():
        for copy in loads:
            copy.wait()

    only(0, begin)

    causal = lax.broadcasted_iota(jnp.int32, (SEQ_LEN, SEQ_LEN), 0) >= lax.broadcasted_iota(
        jnp.int32, (SEQ_LEN, SEQ_LEN), 1
    )
    position = lax.broadcasted_iota(jnp.int32, (SEQ_LEN, 1), 0).astype(f32)
    half = min(2 * SEQ_LEN, rows)
    halves = [slice(lo, lo + half) for lo in range(0, rows, half)]

    rstds = []
    for here in halves:
        xo = xo_ref[here, :].astype(f32)
        xr = far_ref[here, :].astype(f32)
        mean = (jnp.sum(xo, axis=1, keepdims=True) + jnp.sum(xr, axis=1, keepdims=True)) / width
        xo = xo - mean
        xr = xr - mean
        var = (
            jnp.sum(xo * xo, axis=1, keepdims=True) + jnp.sum(xr * xr, axis=1, keepdims=True)
        ) / width
        rstd = lax.rsqrt(var + eps)
        rstds.append(rstd)
        bo = (xo * rstd).astype(bf16)
        br = (xr * rstd).astype(bf16)
        nb_s[here, :own] = bo
        nb_s[here, own:] = br
        nt_s[:own, here] = bo.T
        nt_s[own:, here] = br.T
    only(0, loaded)
    for h in range(heads):
        c = slice(h * 4 * HEAD_DIM, (h + 1) * 4 * HEAD_DIM)
        silu, slope_s[:, c] = gates(dot_nn(nb_s[...], w_s[:, c]))
        g_s[:, c] = silu.astype(bf16)
    table = w_s[:, cols:].astype(f32)
    lengths = pltpu.roll(table, SLOTS // 2, 1)
    lane = lax.broadcasted_iota(jnp.int32, (1, SLOTS), 1)
    lengths = jnp.where(table == user.astype(f32), lengths, 0.0)
    lengths = jnp.sum(lengths, axis=0, keepdims=True)
    for here in halves:
        base = start * histories + step * histories
        valid = jnp.concatenate(
            [
                (
                    position
                    < jnp.sum(jnp.where(lane == base + n, lengths, 0.0), axis=1, keepdims=True)
                ).astype(f32)
                for n in range(here.start // SEQ_LEN, here.stop // SEQ_LEN)
            ],
            axis=0,
        ).astype(bf16)
        there = slice(rows + here.start, rows + here.stop)
        do = do_ref[here, :] * valid
        dr = far_ref[there, :] * valid
        dm_s[here, :own] = do
        dm_s[here, own:] = dr
        dt_s[:own, here] = do.T
        dt_s[own:, here] = dr.T
    dh_s[...] = dot_nn(dm_s[...], w_s[:, cols_in:cols])

    if not first:
        only(0, acc_load.wait)
    target = out_s if last else acc_s
    stores = []

    def ship(lo, wide):
        lanes = pl.ds(lo, wide)
        if not last:
            stores.append(
                pltpu.make_async_copy(
                    acc_s.at[:, lanes], grads_hbm[0].at[:, lanes], store_sems.at[len(stores)]
                )
            )
            only(steps - 1, stores[-1].start)
            return
        keep, send = grads_hbm
        for at, j in enumerate(split_order(far)):
            for xs in range(2):
                for cs in range(2):
                    there = keep if cs == 0 else send
                    stores.append(
                        pltpu.make_async_copy(
                            out_s.at[rows_of(far - j, xs, cs), lanes],
                            there.at[pl.ds((xs * far + at) * size, size), lanes],
                            store_sems.at[len(stores)],
                        )
                    )
                    only(steps - 1, stores[-1].start)

    def add(lhs, rhs, lo, wide):
        chunk = min(512, width)
        for r in range(0, width, chunk):
            term = dot_nn(lhs[r : r + chunk, :], rhs[...]) + acc_s[r : r + chunk, lo : lo + wide]
            target[r : r + chunk, lo : lo + wide] = term.astype(target.dtype)
        ship(lo, wide)

    block = 4 * HEAD_DIM
    stride = max(1, 8 // histories)
    for lo in range(0, heads, stride):
        hi = min(lo + stride, heads)
        units = [(h, n) for h in range(lo, hi) for n in range(histories)]
        attention(units, causal, g_s, dh_s, slope_s, hb_s, dz_s)
        for h in range(max(0, lo - stride), lo):
            add(nt_s, dz_s.at[:, h * block : (h + 1) * block], h * block, block)
    for h in range((heads - 1) // stride * stride, heads):
        add(nt_s, dz_s.at[:, h * block : (h + 1) * block], h * block, block)
    add(dt_s, hb_s, cols_in, heads * HEAD_DIM)
    dn_all = dot_nt(dz_s[...], w_s[:, :cols_in])
    for here, rstd in zip(halves, rstds):
        dn = dn_all[here, :]
        nf = nb_s[here, :].astype(f32)
        one = jnp.sum(dn, axis=1, keepdims=True) / width
        two = jnp.sum(dn * nf, axis=1, keepdims=True) / width
        branch = (dn - one - nf * two) * rstd
        gx_ref[here, :] = (dm_s[here, :own].astype(f32) + branch[:, :own]).astype(bf16)
        bs_ref[here, :] = branch[:, own:].astype(bf16)

    for copy in stores:
        only(steps - 1, copy.wait)


def group_call(group, blocks, users, parts, where, x, d, far, pieces, past):
    start, steps = group
    first, last = start == 0, start + steps == blocks
    rows, own = x.shape[0] // blocks, x.shape[1]
    width = own * parts
    cols = pieces[0].shape[1] - SLOTS
    heads = cols // (5 * HEAD_DIM)
    cols_in = heads * 4 * HEAD_DIM
    smem = pl.BlockSpec(memory_space=pltpu.SMEM)
    anywhere = pl.BlockSpec(memory_space=pl.ANY)
    mine = pl.BlockSpec((rows, own), lambda i: (start + i, 0))
    theirs = pl.BlockSpec((2 * rows, width - own), lambda i: (i, 0))
    args = [where, x, d, far] + pieces + past
    specs = [smem, mine, mine, theirs] + [anywhere] * (len(pieces) + len(past))
    if last:
        grads = [jax.ShapeDtypeStruct((width // 2, cols), bf16)] * 2
    else:
        grads = [jax.ShapeDtypeStruct((width, cols), f32)]
    flops = steps * (4 * rows * width * cols + 2 * rows * width * cols_in)
    return pl.pallas_call(
        functools.partial(group_kernel, start, steps, first, last, heads, parts, users),
        grid=(steps,),
        out_shape=[
            jax.ShapeDtypeStruct((blocks * rows, own), bf16),
            jax.ShapeDtypeStruct((blocks * rows, width - own), bf16),
        ]
        + grads,
        in_specs=specs,
        out_specs=[
            pl.BlockSpec((rows, own), lambda i: (start + i, 0)),
            pl.BlockSpec((rows, width - own), lambda i: (start + i, 0)),
        ]
        + [anywhere] * len(grads),
        input_output_aliases={} if first else {len(pieces) + 5: 0, len(pieces) + 6: 1},
        scratch_shapes=[
            pltpu.VMEM((width, cols + SLOTS), bf16),
            pltpu.VMEM((width, cols), f32),
            pltpu.VMEM((rows, width), bf16),
            pltpu.VMEM((width, rows), bf16),
            pltpu.VMEM((rows, width), bf16),
            pltpu.VMEM((width, rows), bf16),
            pltpu.VMEM((rows, cols_in), bf16),
            pltpu.VMEM((rows, cols - cols_in), bf16),
            pltpu.VMEM((rows, cols_in), bf16),
            pltpu.VMEM((rows, cols_in), f32),
            pltpu.VMEM((rows, cols - cols_in), f32),
            pltpu.VMEM((width, cols) if last else (16, 128), bf16),
            pltpu.SemaphoreType.DMA((2 * users + 1,)),
            pltpu.SemaphoreType.DMA(((users if last else 1) * (heads + 1),)),
        ],
        compiler_params=pltpu.CompilerParams(vmem_limit_bytes=56 * 2**20),
        cost_estimate=pl.CostEstimate(
            flops=flops, bytes_accessed=16 * 2**20, transcendentals=steps * rows * cols
        ),
    )(*args)


def scatter_parts(keep, send, users):
    far = users // 4
    order = split_order(far)
    size = keep.shape[0] // (2 * far)

    def swap(block, bit):
        return lax.ppermute(block, "user", [(i, i ^ bit) for i in range(users)])

    got = swap(send, 1)

    def both(lo, hi):
        span = slice(lo * size, hi * size)
        return keep[span].astype(f32) + got[span].astype(f32)

    cuts = [(0, 1), (1, far - 1), (far - 1, far)]
    across = [swap(both(far + lo, far + hi).astype(bf16), 2) for lo, hi in cuts]
    moved = []
    for (lo, hi), other in zip(cuts[:2], across):
        near = (both(lo, hi) + other.astype(f32)).astype(bf16)
        for at in range(lo, hi):
            pairs = [(i, (i - 4 * order[at]) % users) for i in range(users)]
            block = near[(at - lo) * size : (at - lo + 1) * size]
            moved.append(lax.ppermute(block, "user", pairs))
    return got, [across[2]] + moved


def finish_kernel(cols_in, kept_ref, sent_ref, *refs):
    terms = refs[:-3]
    gx_ref, win_ref, wout_ref = refs[-3:]
    gx_ref[...] = (kept_ref[...].astype(f32) + sent_ref[...].astype(f32)).astype(bf16)

    @pl.when(pl.program_id(0) == 0)
    def _():
        total = terms[0][...].astype(f32)
        for term in terms[1:]:
            total = total + term[...].astype(f32)
        win_ref[...] = total[:, :cols_in]
        wout_ref[...] = total[:, cols_in:]


def finish(kept, sent, keep, got, rest, cols_in):
    rows, own = kept.shape
    size, cols = rest[0].shape
    slot = keep.shape[0] // (2 * size) - 1
    steps = 4
    lines = pl.BlockSpec((rows // steps, own), lambda i: (i, 0))
    specs = [lines] * 2
    specs += [pl.BlockSpec((size, cols), lambda i: (slot, 0))] * 2
    specs += [pl.BlockSpec((size, cols), lambda i: (0, 0))] * len(rest)
    return pl.pallas_call(
        functools.partial(finish_kernel, cols_in),
        grid=(steps,),
        out_shape=[
            jax.ShapeDtypeStruct((rows, own), bf16),
            jax.ShapeDtypeStruct((size, cols_in), f32),
            jax.ShapeDtypeStruct((size, cols - cols_in), f32),
        ],
        in_specs=specs,
        out_specs=[
            lines,
            pl.BlockSpec((size, cols_in), lambda i: (0, 0)),
            pl.BlockSpec((size, cols - cols_in), lambda i: (0, 0)),
        ],
        compiler_params=pltpu.CompilerParams(vmem_limit_bytes=32 * 2**20),
        cost_estimate=pl.CostEstimate(
            flops=rows * own, bytes_accessed=12 * 2**20, transcendentals=0
        ),
    )(kept, sent, keep, got, *rest)


def exchange(block, tensor):
    if tensor == 2:
        return lax.ppermute(block, "tensor", [(0, 1), (1, 0)])
    own = block.shape[1]
    every = lax.all_gather(block, "tensor", axis=1, tiled=True)
    return jnp.roll(every, -lax.axis_index("tensor") * own, axis=1)[:, own:]


def give_back(block, own, tensor):
    if tensor == 2:
        return lax.ppermute(block, "tensor", [(0, 1), (1, 0)])
    every = jnp.concatenate([jnp.zeros((block.shape[0], own), block.dtype), block], axis=1)
    every = jnp.roll(every, lax.axis_index("tensor") * own, axis=1)
    return lax.psum_scatter(every, "tensor", scatter_dimension=1, tiled=True)


def local(events, cotangent, w_in, w_out, slot_source, slot_length):
    tensor = lax.axis_size("tensor")
    users = lax.axis_size("user")
    hist, seq_len, own = events.shape
    x = events.reshape(hist * seq_len, own)
    d = cotangent.reshape(hist * seq_len, own)
    blocks = sum(steps for _, steps in GROUPS)
    rows = hist // blocks * seq_len
    far, ahead = [], None
    for start, steps in GROUPS:
        spans = [slice(i * rows, (i + 1) * rows) for i in range(start, start + steps)]
        if ahead is not None:
            x, d, _ = lax.optimization_barrier((x, d, ahead))
        ahead = jnp.concatenate([t[span] for span in spans for t in (x, d)], axis=0)
        far.append(exchange(ahead, tensor))

    user = lax.axis_index("user")
    slots = jnp.stack([slot_source, slot_length]).astype(bf16)
    slots = jnp.pad(slots, ((0, 0), (0, SLOTS // 2 - hist)), constant_values=-1)
    slots = jnp.pad(slots.reshape(1, SLOTS), ((0, w_in.shape[0] - 1), (0, 0)), constant_values=-1)
    shard = jnp.concatenate([w_in, w_out, slots], axis=1)
    pieces = gather_parts(shard, shard.shape[1] // 256 * 128, users, user)
    where = jnp.stack([lax.axis_index("tensor"), user]).astype(jnp.int32)

    past = []
    for group, theirs in zip(GROUPS, far):
        kept, bs, *grads = group_call(
            group, blocks, users, tensor, where, x, d, theirs, pieces, past
        )
        past = grads + [kept, bs]
    sent = give_back(bs, own, tensor)
    keep, send = grads
    got, rest = scatter_parts(keep, send, users)
    grad_x, grad_in, grad_out = finish(kept, sent, keep, got, rest, w_in.shape[1])
    return (grad_x.reshape(hist, seq_len, own), grad_in, grad_out)


def solution(mesh):
    in_specs = (
        P("user", None, "tensor"),
        P("user", None, "tensor"),
        P("user", "tensor"),
        P("user", "tensor"),
        P("user"),
        P("user"),
    )
    out_specs = (P("user", None, "tensor"), P("user", "tensor"), P("user", "tensor"))
    return jax.shard_map(local, mesh=mesh, in_specs=in_specs, out_specs=out_specs, check_vma=False)
```

```python
import functools

import jax
import jax.numpy as jnp
from jax import lax
from jax.experimental import pallas as pl
from jax.experimental.pallas import tpu as pltpu
from jax.sharding import PartitionSpec as P

HEAD_DIM = 128
SEQ_LEN = 128
SLOTS = 128
GROUPS = ((0, 2), (2, 1), (3, 1))

eps = 1e-05
f32 = jnp.float32
bf16 = jnp.bfloat16


def dot_nn(a, b):
    return lax.dot_general(a, b, (((1,), (0,)), ((), ())), preferred_element_type=f32)


def dot_nt(a, b):
    return lax.dot_general(a, b, (((1,), (1,)), ((), ())), preferred_element_type=f32)


def dot_tn(a, b):
    return lax.dot_general(a, b, (((0,), (0,)), ((), ())), preferred_element_type=f32)


def row_mean(t):
    return jnp.mean(t, axis=1, keepdims=True)


def gates(t):
    sig = 0.5 * jnp.tanh(0.5 * t) + 0.5
    silu = t * sig
    return silu, sig + silu * (1.0 - sig)


def attention(pairs, causal, g_s, dh_s, slope_s, hb_s, dz_s):
    scale = HEAD_DIM ** (-0.5)
    spans = [pl.ds(n * SEQ_LEN, SEQ_LEN) for _, n in pairs]
    lanes = [[pl.ds((4 * h + e) * HEAD_DIM, HEAD_DIM) for e in range(4)] for h, _ in pairs]
    heads = [pl.ds(h * HEAD_DIM, HEAD_DIM) for h, _ in pairs]
    every = range(len(pairs))
    def part(i, e):
        return g_s[spans[i], lanes[i][e]]

    s = [dot_nt(part(i, 2), part(i, 3)) * scale for i in every]
    pair = [gates(t) for t in s]
    attn = [jnp.where(causal, silu * (1.0 / SEQ_LEN), 0.0).astype(bf16) for silu, _ in pair]
    slope = [jnp.where(causal, t * (scale / SEQ_LEN), 0.0) for _, t in pair]
    y = [dot_nn(attn[i], part(i, 1)) for i in every]
    cen = [t - row_mean(t) for t in y]
    rstd = [lax.rsqrt(row_mean(t * t) + eps) for t in cen]
    yn = [cen[i] * rstd[i] for i in every]
    uf = [part(i, 0).astype(f32) for i in every]
    dh = [dh_s[spans[i], heads[i]] for i in every]
    dyn = [dh[i] * uf[i] for i in every]
    one = [row_mean(t) for t in dyn]
    two = [row_mean(dyn[i] * yn[i]) for i in every]
    dy = [((dyn[i] - one[i] - yn[i] * two[i]) * rstd[i]).astype(bf16) for i in every]
    grad_a = [dot_nt(dy[i], part(i, 1)) for i in every]
    ds = [(grad_a[i] * slope[i]).astype(bf16) for i in every]

    def store(i, e, grad):
        dz_s[spans[i], lanes[i][e]] = (grad * slope_s[spans[i], lanes[i][e]]).astype(bf16)

    for i in every:
        hb_s[spans[i], heads[i]] = (yn[i] * uf[i]).astype(bf16)
        store(i, 0, dh[i] * yn[i])
    for i in every:
        store(i, 1, dot_tn(attn[i], dy[i]))
    for i in every:
        store(i, 2, dot_nn(ds[i], part(i, 3)))
    for i in every:
        store(i, 3, dot_tn(ds[i], part(i, 2)))


def split_order(count):
    rest = sorted(range(1, count), key=lambda j: abs(j - count / 2))
    return rest + [0]


def piece_order(far, cut):
    slow = split_order(far)[:-1]
    return [
        (lo, [(j, xs, cs) for j in js])
        for lo, js in ((0, [0]), (0, slow), (cut, slow))
        for cs in range(2)
        for xs in range(2)
    ]


def gather_parts(shard, cut, users, user):
    def swap(block, bit):
        return lax.ppermute(block, "user", [(i, i ^ bit) for i in range(users)])

    def spread(block):
        across = swap(block, 2)
        return [block, across, swap(block, 1), swap(across, 1)]

    arrays, moved = spread(shard), []
    for part in (shard[:, :cut], shard[:, cut:]):
        if moved:
            part = jnp.where(user < 0, sum(t[:1, :1] for t in moved), part)
        moved = []
        for j in split_order(users // 4)[:-1]:
            pairs = [(i, (i - 4 * j) % users) for i in range(users)]
            moved.append(lax.ppermute(part, "user", pairs))
        block = jnp.concatenate(moved, axis=0)
        block = jnp.where(user < 0, arrays[-3][:1, :1], block)
        arrays += spread(block)
    return arrays


def group_kernel(start, steps, first, last, heads, parts, users, shared, *refs):
    refs = list(refs)
    where_ref, xo_ref, do_ref, far_ref = refs[:4]
    pieces, refs = refs[4:16], refs[16:]
    acc_hbm = None if first else refs.pop(0)
    refs = refs[shared:]
    gx_ref, bs_ref = refs[:2]
    refs = refs[2:]
    grads_hbm = [refs.pop(0) for _ in range(2 if last else 1)]
    (w_s, acc_s, nb_s, nt_s, dm_s, dt_s, dz_s, hb_s, g_s, slope_s, dh_s, out_s) = refs[:12]
    load_sems, store_sems = refs[12:]
    rows, own = xo_ref.shape
    width = own * parts
    cols_in = heads * 4 * HEAD_DIM
    cols = cols_in + heads * HEAD_DIM
    histories = rows // SEQ_LEN
    me, user = where_ref[0], where_ref[1]
    step = pl.program_id(0)

    def only(index, run):
        if steps == 1:
            run()
        else:
            pl.when(step == index)(run)

    size = width // users
    far = users // 4
    zi, xi, ci = user // 4, lax.rem(user // 2, 2), lax.rem(user, 2)

    def rows_of(j, xs, cs):
        zd = lax.rem(zi + j, far)
        xd = xi if xs == 0 else 1 - xi
        cd = ci if cs == 0 else 1 - ci
        row = ((zd * 2 + xd) * 2 + cd) * size
        row = lax.rem(row // own - me + parts, parts) * own + lax.rem(row, own)
        return pl.ds(pl.multiple_of(row, size), size)

    loads = []
    for piece, (lo, offsets) in zip(pieces, piece_order(far, pieces[4].shape[1])):
        for at, offset in enumerate(offsets):
            there = w_s.at[rows_of(*offset), pl.ds(lo, piece.shape[1])]
            here = piece.at[pl.ds(at * size, size)]
            loads.append(pltpu.make_async_copy(here, there, load_sems.at[len(loads)]))
    if not first:
        acc_load = pltpu.make_async_copy(acc_hbm, acc_s, load_sems.at[2 * users])

    def begin():
        for copy in loads:
            copy.start()
        if first:
            acc_s[...] = jnp.zeros_like(acc_s)
        else:
            acc_load.start()

    def loaded():
        for copy in loads:
            copy.wait()

    only(0, begin)

    causal = lax.broadcasted_iota(jnp.int32, (SEQ_LEN, SEQ_LEN), 0) >= lax.broadcasted_iota(
        jnp.int32, (SEQ_LEN, SEQ_LEN), 1
    )
    position = lax.broadcasted_iota(jnp.int32, (SEQ_LEN, 1), 0).astype(f32)
    half = min(2 * SEQ_LEN, rows)
    halves = [slice(lo, lo + half) for lo in range(0, rows, half)]

    rstds = []
    for here in halves:
        xo = xo_ref[here, :].astype(f32)
        xr = far_ref[here, :].astype(f32)
        mean = (jnp.sum(xo, axis=1, keepdims=True) + jnp.sum(xr, axis=1, keepdims=True)) / width
        xo = xo - mean
        xr = xr - mean
        var = (
            jnp.sum(xo * xo, axis=1, keepdims=True) + jnp.sum(xr * xr, axis=1, keepdims=True)
        ) / width
        rstd = lax.rsqrt(var + eps)
        rstds.append(rstd)
        bo = (xo * rstd).astype(bf16)
        br = (xr * rstd).astype(bf16)
        nb_s[here, :own] = bo
        nb_s[here, own:] = br
        nt_s[:own, here] = bo.T
        nt_s[own:, here] = br.T
    only(0, loaded)
    for h in range(heads):
        c = slice(h * 4 * HEAD_DIM, (h + 1) * 4 * HEAD_DIM)
        silu, slope_s[:, c] = gates(dot_nn(nb_s[...], w_s[:, c]))
        g_s[:, c] = silu.astype(bf16)
    table = w_s[:, cols:].astype(f32)
    lengths = pltpu.roll(table, SLOTS // 2, 1)
    lane = lax.broadcasted_iota(jnp.int32, (1, SLOTS), 1)
    lengths = jnp.where(table == user.astype(f32), lengths, 0.0)
    lengths = jnp.sum(lengths, axis=0, keepdims=True)
    for here in halves:
        base = start * histories + step * histories
        valid = jnp.concatenate(
            [
                (
                    position
                    < jnp.sum(jnp.where(lane == base + n, lengths, 0.0), axis=1, keepdims=True)
                ).astype(f32)
                for n in range(here.start // SEQ_LEN, here.stop // SEQ_LEN)
            ],
            axis=0,
        ).astype(bf16)
        there = slice(rows + here.start, rows + here.stop)
        do = do_ref[here, :] * valid
        dr = far_ref[there, :] * valid
        dm_s[here, :own] = do
        dm_s[here, own:] = dr
        dt_s[:own, here] = do.T
        dt_s[own:, here] = dr.T
    dh_s[...] = dot_nn(dm_s[...], w_s[:, cols_in:cols])

    if not first:
        only(0, acc_load.wait)
    target = out_s if last else acc_s
    stores = []

    def ship(lo, wide):
        lanes = pl.ds(lo, wide)
        if not last:
            stores.append(
                pltpu.make_async_copy(
                    acc_s.at[:, lanes], grads_hbm[0].at[:, lanes], store_sems.at[len(stores)]
                )
            )
            only(steps - 1, stores[-1].start)
            return
        keep, send = grads_hbm
        for at, j in enumerate(split_order(far)):
            for xs in range(2):
                for cs in range(2):
                    there = keep if cs == 0 else send
                    stores.append(
                        pltpu.make_async_copy(
                            out_s.at[rows_of(far - j, xs, cs), lanes],
                            there.at[pl.ds((xs * far + at) * size, size), lanes],
                            store_sems.at[len(stores)],
                        )
                    )
                    only(steps - 1, stores[-1].start)

    def add(lhs, rhs, lo, wide):
        chunk = min(512, width)
        for r in range(0, width, chunk):
            term = dot_nn(lhs[r : r + chunk, :], rhs[...]) + acc_s[r : r + chunk, lo : lo + wide]
            target[r : r + chunk, lo : lo + wide] = term.astype(target.dtype)
        ship(lo, wide)

    block = 4 * HEAD_DIM
    stride = max(1, 8 // histories)
    for lo in range(0, heads, stride):
        hi = min(lo + stride, heads)
        units = [(h, n) for h in range(lo, hi) for n in range(histories)]
        attention(units, causal, g_s, dh_s, slope_s, hb_s, dz_s)
        for h in range(max(0, lo - stride), lo):
            add(nt_s, dz_s.at[:, h * block : (h + 1) * block], h * block, block)
    for h in range((heads - 1) // stride * stride, heads):
        add(nt_s, dz_s.at[:, h * block : (h + 1) * block], h * block, block)
    add(dt_s, hb_s, cols_in, heads * HEAD_DIM)
    dn_all = dot_nt(dz_s[...], w_s[:, :cols_in])
    for here, rstd in zip(halves, rstds):
        dn = dn_all[here, :]
        nf = nb_s[here, :].astype(f32)
        one = jnp.sum(dn, axis=1, keepdims=True) / width
        two = jnp.sum(dn * nf, axis=1, keepdims=True) / width
        branch = (dn - one - nf * two) * rstd
        gx_ref[here, :] = (dm_s[here, :own].astype(f32) + branch[:, :own]).astype(bf16)
        bs_ref[here, :] = branch[:, own:].astype(bf16)

    for copy in stores:
        only(steps - 1, copy.wait)


def group_call(group, blocks, users, parts, where, x, d, far, pieces, past):
    start, steps = group
    first, last = start == 0, start + steps == blocks
    rows, own = x.shape[0] // blocks, x.shape[1]
    width = own * parts
    cols = pieces[0].shape[1] - SLOTS
    heads = cols // (5 * HEAD_DIM)
    cols_in = heads * 4 * HEAD_DIM
    smem = pl.BlockSpec(memory_space=pltpu.SMEM)
    anywhere = pl.BlockSpec(memory_space=pl.ANY)
    mine = pl.BlockSpec((rows, own), lambda i: (start + i, 0))
    theirs = pl.BlockSpec((2 * rows, width - own), lambda i: (i, 0))
    shared = max(0, len(past) - 1)
    alone = GROUPS[0][1]
    base, held = (0, alone) if first else (alone, blocks - alone)
    args = [where, x, d, far] + pieces + past
    specs = [smem, mine, mine, theirs] + [anywhere] * (len(pieces) + len(past))
    if last:
        grads = [jax.ShapeDtypeStruct((width // 2, cols), bf16)] * 2
    else:
        grads = [jax.ShapeDtypeStruct((width, cols), f32)]
    flops = steps * (4 * rows * width * cols + 2 * rows * width * cols_in)
    return pl.pallas_call(
        functools.partial(group_kernel, start, steps, first, last, heads, parts, users, shared),
        grid=(steps,),
        out_shape=[
            jax.ShapeDtypeStruct((blocks * rows, own), bf16),
            jax.ShapeDtypeStruct((held * rows, width - own), bf16),
        ]
        + grads,
        in_specs=specs,
        out_specs=[
            pl.BlockSpec((rows, own), lambda i: (start + i, 0)),
            pl.BlockSpec((rows, width - own), lambda i: (start - base + i, 0)),
        ]
        + [anywhere] * len(grads),
        input_output_aliases={len(pieces) + 5 + i: i for i in range(shared)},
        scratch_shapes=[
            pltpu.VMEM((width, cols + SLOTS), bf16),
            pltpu.VMEM((width, cols), f32),
            pltpu.VMEM((rows, width), bf16),
            pltpu.VMEM((width, rows), bf16),
            pltpu.VMEM((rows, width), bf16),
            pltpu.VMEM((width, rows), bf16),
            pltpu.VMEM((rows, cols_in), bf16),
            pltpu.VMEM((rows, cols - cols_in), bf16),
            pltpu.VMEM((rows, cols_in), bf16),
            pltpu.VMEM((rows, cols_in), f32),
            pltpu.VMEM((rows, cols - cols_in), f32),
            pltpu.VMEM((width, cols) if last else (16, 128), bf16),
            pltpu.SemaphoreType.DMA((2 * users + 1,)),
            pltpu.SemaphoreType.DMA(((users if last else 1) * (heads + 1),)),
        ],
        compiler_params=pltpu.CompilerParams(vmem_limit_bytes=56 * 2**20),
        cost_estimate=pl.CostEstimate(
            flops=flops, bytes_accessed=16 * 2**20, transcendentals=steps * rows * cols
        ),
    )(*args)


def scatter_parts(keep, send, users, user, early):
    far = users // 4
    order = split_order(far)
    size = keep.shape[0] // (2 * far)

    def swap(block, bit):
        return lax.ppermute(block, "user", [(i, i ^ bit) for i in range(users)])

    got = swap(jnp.where(user < 0, early[:1, :1], send), 1)

    def both(lo, hi):
        span = slice(lo * size, hi * size)
        return keep[span].astype(f32) + got[span].astype(f32)

    cuts = [(0, 1), (1, far - 1), (far - 1, far)]
    across, moved = [], []
    for at, (lo, hi) in enumerate(cuts):
        block = both(far + lo, far + hi).astype(bf16)
        if at == 2:
            block = jnp.where(user < 0, across[1][:1, :1], block)
        across.append(swap(block, 2))
    for (lo, hi), other in zip(cuts[:2], across):
        near = (both(lo, hi) + other.astype(f32)).astype(bf16)
        for at in range(lo, hi):
            pairs = [(i, (i - 4 * order[at]) % users) for i in range(users)]
            block = near[(at - lo) * size : (at - lo + 1) * size]
            moved.append(lax.ppermute(block, "user", pairs))
    return got, [across[-1]] + moved


def finish_kernel(cols_in, alone, kept_ref, sent_a, sent_b, *refs):
    terms = refs[:-3]
    gx_ref, win_ref, wout_ref = refs[-3:]
    step = pl.program_id(0)
    for at, sent_ref in ((step < alone, sent_a), (step >= alone, sent_b)):

        @pl.when(at)
        def _(sent_ref=sent_ref):
            gx_ref[...] = (kept_ref[...].astype(f32) + sent_ref[...].astype(f32)).astype(bf16)

    @pl.when(step == 0)
    def _():
        total = terms[0][...].astype(f32)
        for term in terms[1:]:
            total = total + term[...].astype(f32)
        win_ref[...] = total[:, :cols_in]
        wout_ref[...] = total[:, cols_in:]


def finish(kept, sent, keep, got, rest, cols_in):
    rows, own = kept.shape
    size, cols = rest[0].shape
    slot = keep.shape[0] // (2 * size) - 1
    alone = GROUPS[0][1]
    steps = sum(count for _, count in GROUPS)
    lines = pl.BlockSpec((rows // steps, own), lambda i: (i, 0))
    specs = [
        lines,
        pl.BlockSpec((rows // steps, own), lambda i: (jnp.minimum(i, alone - 1), 0)),
        pl.BlockSpec((rows // steps, own), lambda i: (jnp.maximum(i - alone, 0), 0)),
    ]
    specs += [pl.BlockSpec((size, cols), lambda i: (slot, 0))] * 2
    specs += [pl.BlockSpec((size, cols), lambda i: (0, 0))] * len(rest)
    return pl.pallas_call(
        functools.partial(finish_kernel, cols_in, alone),
        grid=(steps,),
        out_shape=[
            jax.ShapeDtypeStruct((rows, own), bf16),
            jax.ShapeDtypeStruct((size, cols_in), f32),
            jax.ShapeDtypeStruct((size, cols - cols_in), f32),
        ],
        in_specs=specs,
        out_specs=[
            lines,
            pl.BlockSpec((size, cols_in), lambda i: (0, 0)),
            pl.BlockSpec((size, cols - cols_in), lambda i: (0, 0)),
        ],
        compiler_params=pltpu.CompilerParams(vmem_limit_bytes=32 * 2**20),
        cost_estimate=pl.CostEstimate(
            flops=rows * own, bytes_accessed=12 * 2**20, transcendentals=0
        ),
    )(kept, *sent, keep, got, *rest)


def exchange(block, tensor):
    if tensor == 2:
        return lax.ppermute(block, "tensor", [(0, 1), (1, 0)])
    own = block.shape[1]
    every = lax.all_gather(block, "tensor", axis=1, tiled=True)
    return jnp.roll(every, -lax.axis_index("tensor") * own, axis=1)[:, own:]


def give_back(block, own, tensor):
    if tensor == 2:
        return lax.ppermute(block, "tensor", [(0, 1), (1, 0)])
    every = jnp.concatenate([jnp.zeros((block.shape[0], own), block.dtype), block], axis=1)
    every = jnp.roll(every, lax.axis_index("tensor") * own, axis=1)
    return lax.psum_scatter(every, "tensor", scatter_dimension=1, tiled=True)


def local(events, cotangent, w_in, w_out, slot_source, slot_length):
    tensor = lax.axis_size("tensor")
    users = lax.axis_size("user")
    hist, seq_len, own = events.shape
    x = events.reshape(hist * seq_len, own)
    d = cotangent.reshape(hist * seq_len, own)
    blocks = sum(steps for _, steps in GROUPS)
    rows = hist // blocks * seq_len
    far, ahead = [], None
    for start, steps in GROUPS:
        spans = [slice(i * rows, (i + 1) * rows) for i in range(start, start + steps)]
        if ahead is not None:
            x, d, _ = lax.optimization_barrier((x, d, ahead))
        ahead = jnp.concatenate([t[span] for span in spans for t in (x, d)], axis=0)
        far.append(exchange(ahead, tensor))

    user = lax.axis_index("user")
    slots = jnp.stack([slot_source, slot_length]).astype(bf16)
    slots = jnp.pad(slots, ((0, 0), (0, SLOTS // 2 - hist)), constant_values=-1)
    slots = jnp.pad(slots.reshape(1, SLOTS), ((0, w_in.shape[0] - 1), (0, 0)), constant_values=-1)
    shard = jnp.concatenate([w_in, w_out, slots], axis=1)
    pieces = gather_parts(shard, shard.shape[1] // 256 * 128, users, user)
    where = jnp.stack([lax.axis_index("tensor"), user]).astype(jnp.int32)

    past, early = [], None
    for group, theirs in zip(GROUPS, far):
        kept, bs, *grads = group_call(
            group, blocks, users, tensor, where, x, d, theirs, pieces, past
        )
        if early is None:
            early = give_back(bs, own, tensor)
            past = grads + [kept]
        else:
            past = grads + [kept, bs]
    sent = [early, give_back(bs, own, tensor)]
    keep, send = grads
    got, rest = scatter_parts(keep, send, users, user, early)
    grad_x, grad_in, grad_out = finish(kept, sent, keep, got, rest, w_in.shape[1])
    return (grad_x.reshape(hist, seq_len, own), grad_in, grad_out)


def solution(mesh):
    in_specs = (
        P("user", None, "tensor"),
        P("user", None, "tensor"),
        P("user", "tensor"),
        P("user", "tensor"),
        P("user"),
        P("user"),
    )
    out_specs = (P("user", None, "tensor"), P("user", "tensor"), P("user", "tensor"))
    return jax.shard_map(local, mesh=mesh, in_specs=in_specs, out_specs=out_specs, check_vma=False)
```

```python
import functools

import jax
import jax.numpy as jnp
from jax import lax
from jax.experimental import pallas as pl
from jax.experimental.pallas import tpu as pltpu
from jax.sharding import PartitionSpec as P

HEAD_DIM = 128
SEQ_LEN = 128
SLOTS = 128
GROUPS = ((0, 2), (2, 1), (3, 1))

eps = 1e-05
f32 = jnp.float32
bf16 = jnp.bfloat16


def dot_nn(a, b):
    return lax.dot_general(a, b, (((1,), (0,)), ((), ())), preferred_element_type=f32)


def dot_nt(a, b):
    return lax.dot_general(a, b, (((1,), (1,)), ((), ())), preferred_element_type=f32)


def dot_tn(a, b):
    return lax.dot_general(a, b, (((0,), (0,)), ((), ())), preferred_element_type=f32)


def row_mean(t):
    return jnp.mean(t, axis=1, keepdims=True)


def gates(t):
    sig = 0.5 * jnp.tanh(0.5 * t) + 0.5
    silu = t * sig
    return silu, sig + silu * (1.0 - sig)


def attention(pairs, causal, g_s, dh_s, slope_s, hb_s, dz_s):
    scale = HEAD_DIM ** (-0.5)
    spans = [pl.ds(n * SEQ_LEN, SEQ_LEN) for _, n in pairs]
    lanes = [[pl.ds((4 * h + e) * HEAD_DIM, HEAD_DIM) for e in range(4)] for h, _ in pairs]
    heads = [pl.ds(h * HEAD_DIM, HEAD_DIM) for h, _ in pairs]
    every = range(len(pairs))
    def part(i, e):
        return g_s[spans[i], lanes[i][e]]

    s = [dot_nt(part(i, 2), part(i, 3)) * scale for i in every]
    pair = [gates(t) for t in s]
    attn = [jnp.where(causal, silu * (1.0 / SEQ_LEN), 0.0).astype(bf16) for silu, _ in pair]
    slope = [jnp.where(causal, t * (scale / SEQ_LEN), 0.0) for _, t in pair]
    y = [dot_nn(attn[i], part(i, 1)) for i in every]
    cen = [t - row_mean(t) for t in y]
    rstd = [lax.rsqrt(row_mean(t * t) + eps) for t in cen]
    yn = [cen[i] * rstd[i] for i in every]
    uf = [part(i, 0).astype(f32) for i in every]
    dh = [dh_s[spans[i], heads[i]] for i in every]
    dyn = [dh[i] * uf[i] for i in every]
    one = [row_mean(t) for t in dyn]
    two = [row_mean(dyn[i] * yn[i]) for i in every]
    dy = [((dyn[i] - one[i] - yn[i] * two[i]) * rstd[i]).astype(bf16) for i in every]
    grad_a = [dot_nt(dy[i], part(i, 1)) for i in every]
    ds = [(grad_a[i] * slope[i]).astype(bf16) for i in every]

    def store(i, e, grad):
        dz_s[spans[i], lanes[i][e]] = (grad * slope_s[spans[i], lanes[i][e]]).astype(bf16)

    for i in every:
        hb_s[spans[i], heads[i]] = (yn[i] * uf[i]).astype(bf16)
        store(i, 0, dh[i] * yn[i])
    for i in every:
        store(i, 1, dot_tn(attn[i], dy[i]))
    for i in every:
        store(i, 2, dot_nn(ds[i], part(i, 3)))
    for i in every:
        store(i, 3, dot_tn(ds[i], part(i, 2)))


def split_order(count):
    rest = sorted(range(1, count), key=lambda j: abs(j - count / 2))
    return rest + [0]


def stage_kernel(rows, x_ref, d_ref, w_ref, head_ref, out_ref, sems):
    jobs = [(w_ref.at[:, pl.ds(0, head_ref.shape[1])], head_ref)]
    for i in range(GROUPS[0][1]):
        span = pl.ds(i * rows, rows)
        jobs.append((x_ref.at[span], out_ref.at[pl.ds(2 * i * rows, rows)]))
        jobs.append((d_ref.at[span], out_ref.at[pl.ds((2 * i + 1) * rows, rows)]))
    copies = [pltpu.make_async_copy(a, b, sems.at[n]) for n, (a, b) in enumerate(jobs)]
    for copy in copies:
        copy.start()
    for copy in copies:
        copy.wait()


def stage(x, d, w_in, rows, cut):
    anywhere = pl.BlockSpec(memory_space=pl.ANY)
    own = x.shape[1]
    shapes = [jax.ShapeDtypeStruct((w_in.shape[0], cut), bf16)]
    shapes += [jax.ShapeDtypeStruct((2 * GROUPS[0][1] * rows, own), bf16)]
    return pl.pallas_call(
        functools.partial(stage_kernel, rows),
        out_shape=shapes,
        in_specs=[anywhere] * 3,
        out_specs=[anywhere] * len(shapes),
        scratch_shapes=[pltpu.SemaphoreType.DMA((2 * GROUPS[0][1] + 1,))],
        cost_estimate=pl.CostEstimate(flops=0, bytes_accessed=4 * x.size, transcendentals=0),
    )(x, d, w_in)


def piece_order(far, cut):
    slow = split_order(far)[:-1]
    return [
        (lo, [(j, xs, cs) for j in js])
        for lo, js in ((0, [0]), (0, slow), (cut, slow))
        for cs in range(2)
        for xs in range(2)
    ]


def gather_parts(head, shard, users, user):
    def swap(block, bit):
        return lax.ppermute(block, "user", [(i, i ^ bit) for i in range(users)])

    def spread(block):
        across = swap(block, 2)
        return [block, across, swap(block, 1), swap(across, 1)]

    arrays, moved = spread(shard), []
    for part in (head, shard[:, head.shape[1] :]):
        if moved:
            part = jnp.where(user < 0, sum(t[:1, :1] for t in moved), part)
        moved = []
        for j in split_order(users // 4)[:-1]:
            pairs = [(i, (i - 4 * j) % users) for i in range(users)]
            moved.append(lax.ppermute(part, "user", pairs))
        block = jnp.concatenate(moved, axis=0)
        block = jnp.where(user < 0, arrays[-3][:1, :1], block)
        arrays += spread(block)
    return arrays


def group_kernel(start, steps, first, last, heads, parts, users, *refs):
    refs = list(refs)
    where_ref, xo_ref, do_ref, far_ref = refs[:4]
    pieces, refs = refs[4:16], refs[16:]
    acc_hbm = None if first else refs.pop(0)
    refs = refs if first else refs[2:]
    gx_ref, bs_ref = refs[:2]
    refs = refs[2:]
    grads_hbm = [refs.pop(0) for _ in range(2 if last else 1)]
    (w_s, acc_s, nb_s, nt_s, dm_s, dt_s, dz_s, hb_s, g_s, slope_s, dh_s, out_s) = refs[:12]
    load_sems, store_sems = refs[12:]
    rows, own = xo_ref.shape
    width = own * parts
    cols_in = heads * 4 * HEAD_DIM
    cols = cols_in + heads * HEAD_DIM
    histories = rows // SEQ_LEN
    me, user = where_ref[0], where_ref[1]
    step = pl.program_id(0)

    def only(index, run):
        if steps == 1:
            run()
        else:
            pl.when(step == index)(run)

    size = width // users
    far = users // 4
    zi, xi, ci = user // 4, lax.rem(user // 2, 2), lax.rem(user, 2)

    def rows_of(j, xs, cs):
        zd = lax.rem(zi + j, far)
        xd = xi if xs == 0 else 1 - xi
        cd = ci if cs == 0 else 1 - ci
        row = ((zd * 2 + xd) * 2 + cd) * size
        row = lax.rem(row // own - me + parts, parts) * own + lax.rem(row, own)
        return pl.ds(pl.multiple_of(row, size), size)

    loads = []
    for piece, (lo, offsets) in zip(pieces, piece_order(far, pieces[4].shape[1])):
        for at, offset in enumerate(offsets):
            there = w_s.at[rows_of(*offset), pl.ds(lo, piece.shape[1])]
            here = piece.at[pl.ds(at * size, size)]
            loads.append(pltpu.make_async_copy(here, there, load_sems.at[len(loads)]))
    if not first:
        acc_load = pltpu.make_async_copy(acc_hbm, acc_s, load_sems.at[2 * users])

    def begin():
        for copy in loads:
            copy.start()
        if first:
            acc_s[...] = jnp.zeros_like(acc_s)
        else:
            acc_load.start()

    def loaded():
        for copy in loads:
            copy.wait()

    only(0, begin)

    causal = lax.broadcasted_iota(jnp.int32, (SEQ_LEN, SEQ_LEN), 0) >= lax.broadcasted_iota(
        jnp.int32, (SEQ_LEN, SEQ_LEN), 1
    )
    position = lax.broadcasted_iota(jnp.int32, (SEQ_LEN, 1), 0).astype(f32)
    half = min(2 * SEQ_LEN, rows)
    halves = [slice(lo, lo + half) for lo in range(0, rows, half)]

    rstds = []
    for here in halves:
        xo = xo_ref[here, :].astype(f32)
        xr = far_ref[here, :].astype(f32)
        mean = (jnp.sum(xo, axis=1, keepdims=True) + jnp.sum(xr, axis=1, keepdims=True)) / width
        xo = xo - mean
        xr = xr - mean
        var = (
            jnp.sum(xo * xo, axis=1, keepdims=True) + jnp.sum(xr * xr, axis=1, keepdims=True)
        ) / width
        rstd = lax.rsqrt(var + eps)
        rstds.append(rstd)
        bo = (xo * rstd).astype(bf16)
        br = (xr * rstd).astype(bf16)
        nb_s[here, :own] = bo
        nb_s[here, own:] = br
        nt_s[:own, here] = bo.T
        nt_s[own:, here] = br.T
    only(0, loaded)
    for h in range(heads):
        c = slice(h * 4 * HEAD_DIM, (h + 1) * 4 * HEAD_DIM)
        silu, slope_s[:, c] = gates(dot_nn(nb_s[...], w_s[:, c]))
        g_s[:, c] = silu.astype(bf16)
    table = w_s[:, cols:].astype(f32)
    lengths = pltpu.roll(table, SLOTS // 2, 1)
    lane = lax.broadcasted_iota(jnp.int32, (1, SLOTS), 1)
    lengths = jnp.where(table == user.astype(f32), lengths, 0.0)
    lengths = jnp.sum(lengths, axis=0, keepdims=True)
    for here in halves:
        base = start * histories + step * histories
        valid = jnp.concatenate(
            [
                (
                    position
                    < jnp.sum(jnp.where(lane == base + n, lengths, 0.0), axis=1, keepdims=True)
                ).astype(f32)
                for n in range(here.start // SEQ_LEN, here.stop // SEQ_LEN)
            ],
            axis=0,
        ).astype(bf16)
        there = slice(rows + here.start, rows + here.stop)
        do = do_ref[here, :] * valid
        dr = far_ref[there, :] * valid
        dm_s[here, :own] = do
        dm_s[here, own:] = dr
        dt_s[:own, here] = do.T
        dt_s[own:, here] = dr.T
    dh_s[...] = dot_nn(dm_s[...], w_s[:, cols_in:cols])

    if not first:
        only(0, acc_load.wait)
    target = out_s if last else acc_s
    stores = []

    def ship(lo, wide):
        lanes = pl.ds(lo, wide)
        if not last:
            stores.append(
                pltpu.make_async_copy(
                    acc_s.at[:, lanes], grads_hbm[0].at[:, lanes], store_sems.at[len(stores)]
                )
            )
            only(steps - 1, stores[-1].start)
            return
        keep, send = grads_hbm
        for at, j in enumerate(split_order(far)):
            for xs in range(2):
                for cs in range(2):
                    there = keep if cs == 0 else send
                    stores.append(
                        pltpu.make_async_copy(
                            out_s.at[rows_of(far - j, xs, cs), lanes],
                            there.at[pl.ds((xs * far + at) * size, size), lanes],
                            store_sems.at[len(stores)],
                        )
                    )
                    only(steps - 1, stores[-1].start)

    def add(lhs, rhs, lo, wide):
        chunk = min(512, width)
        for r in range(0, width, chunk):
            term = dot_nn(lhs[r : r + chunk, :], rhs[...]) + acc_s[r : r + chunk, lo : lo + wide]
            target[r : r + chunk, lo : lo + wide] = term.astype(target.dtype)
        ship(lo, wide)

    block = 4 * HEAD_DIM
    stride = max(1, 8 // histories)
    for lo in range(0, heads, stride):
        hi = min(lo + stride, heads)
        units = [(h, n) for h in range(lo, hi) for n in range(histories)]
        attention(units, causal, g_s, dh_s, slope_s, hb_s, dz_s)
        for h in range(max(0, lo - stride), lo):
            add(nt_s, dz_s.at[:, h * block : (h + 1) * block], h * block, block)
    for h in range((heads - 1) // stride * stride, heads):
        add(nt_s, dz_s.at[:, h * block : (h + 1) * block], h * block, block)
    add(dt_s, hb_s, cols_in, heads * HEAD_DIM)
    dn_all = dot_nt(dz_s[...], w_s[:, :cols_in])
    for here, rstd in zip(halves, rstds):
        dn = dn_all[here, :]
        nf = nb_s[here, :].astype(f32)
        one = jnp.sum(dn, axis=1, keepdims=True) / width
        two = jnp.sum(dn * nf, axis=1, keepdims=True) / width
        branch = (dn - one - nf * two) * rstd
        gx_ref[here, :] = (dm_s[here, :own].astype(f32) + branch[:, :own]).astype(bf16)
        bs_ref[here, :] = branch[:, own:].astype(bf16)

    for copy in stores:
        only(steps - 1, copy.wait)


def group_call(group, blocks, users, parts, where, x, d, far, pieces, past):
    start, steps = group
    first, last = start == 0, start + steps == blocks
    rows, own = x.shape[0] // blocks, x.shape[1]
    width = own * parts
    cols = pieces[0].shape[1] - SLOTS
    heads = cols // (5 * HEAD_DIM)
    cols_in = heads * 4 * HEAD_DIM
    smem = pl.BlockSpec(memory_space=pltpu.SMEM)
    anywhere = pl.BlockSpec(memory_space=pl.ANY)
    mine = pl.BlockSpec((rows, own), lambda i: (start + i, 0))
    theirs = pl.BlockSpec((2 * rows, width - own), lambda i: (i, 0))
    args = [where, x, d, far] + pieces + past
    specs = [smem, mine, mine, theirs] + [anywhere] * (len(pieces) + len(past))
    if last:
        grads = [jax.ShapeDtypeStruct((width // 2, cols), bf16)] * 2
    else:
        grads = [jax.ShapeDtypeStruct((width, cols), f32)]
    flops = steps * (4 * rows * width * cols + 2 * rows * width * cols_in)
    return pl.pallas_call(
        functools.partial(group_kernel, start, steps, first, last, heads, parts, users),
        grid=(steps,),
        out_shape=[
            jax.ShapeDtypeStruct((blocks * rows, own), bf16),
            jax.ShapeDtypeStruct((blocks * rows, width - own), bf16),
        ]
        + grads,
        in_specs=specs,
        out_specs=[
            pl.BlockSpec((rows, own), lambda i: (start + i, 0)),
            pl.BlockSpec((rows, width - own), lambda i: (start + i, 0)),
        ]
        + [anywhere] * len(grads),
        input_output_aliases={} if first else {len(pieces) + 5: 0, len(pieces) + 6: 1},
        scratch_shapes=[
            pltpu.VMEM((width, cols + SLOTS), bf16),
            pltpu.VMEM((width, cols), f32),
            pltpu.VMEM((rows, width), bf16),
            pltpu.VMEM((width, rows), bf16),
            pltpu.VMEM((rows, width), bf16),
            pltpu.VMEM((width, rows), bf16),
            pltpu.VMEM((rows, cols_in), bf16),
            pltpu.VMEM((rows, cols - cols_in), bf16),
            pltpu.VMEM((rows, cols_in), bf16),
            pltpu.VMEM((rows, cols_in), f32),
            pltpu.VMEM((rows, cols - cols_in), f32),
            pltpu.VMEM((width, cols) if last else (16, 128), bf16),
            pltpu.SemaphoreType.DMA((2 * users + 1,)),
            pltpu.SemaphoreType.DMA(((users if last else 1) * (heads + 1),)),
        ],
        compiler_params=pltpu.CompilerParams(vmem_limit_bytes=56 * 2**20),
        cost_estimate=pl.CostEstimate(
            flops=flops, bytes_accessed=16 * 2**20, transcendentals=steps * rows * cols
        ),
    )(*args)


def scatter_parts(keep, send, users):
    far = users // 4
    order = split_order(far)
    size = keep.shape[0] // (2 * far)

    def swap(block, bit):
        return lax.ppermute(block, "user", [(i, i ^ bit) for i in range(users)])

    got = swap(send, 1)

    def both(lo, hi):
        span = slice(lo * size, hi * size)
        return keep[span].astype(f32) + got[span].astype(f32)

    cuts = [(0, 1), (1, far - 1), (far - 1, far)]
    across = [swap(both(far + lo, far + hi).astype(bf16), 2) for lo, hi in cuts]
    moved = []
    for (lo, hi), other in zip(cuts[:2], across):
        near = (both(lo, hi) + other.astype(f32)).astype(bf16)
        for at in range(lo, hi):
            pairs = [(i, (i - 4 * order[at]) % users) for i in range(users)]
            block = near[(at - lo) * size : (at - lo + 1) * size]
            moved.append(lax.ppermute(block, "user", pairs))
    return got, [across[2]] + moved


def finish_kernel(cols_in, kept_ref, sent_ref, *refs):
    terms = refs[:-3]
    gx_ref, win_ref, wout_ref = refs[-3:]
    gx_ref[...] = (kept_ref[...].astype(f32) + sent_ref[...].astype(f32)).astype(bf16)

    @pl.when(pl.program_id(0) == 0)
    def _():
        total = terms[0][...].astype(f32)
        for term in terms[1:]:
            total = total + term[...].astype(f32)
        win_ref[...] = total[:, :cols_in]
        wout_ref[...] = total[:, cols_in:]


def finish(kept, sent, keep, got, rest, cols_in):
    rows, own = kept.shape
    size, cols = rest[0].shape
    slot = keep.shape[0] // (2 * size) - 1
    steps = 4
    lines = pl.BlockSpec((rows // steps, own), lambda i: (i, 0))
    specs = [lines] * 2
    specs += [pl.BlockSpec((size, cols), lambda i: (slot, 0))] * 2
    specs += [pl.BlockSpec((size, cols), lambda i: (0, 0))] * len(rest)
    return pl.pallas_call(
        functools.partial(finish_kernel, cols_in),
        grid=(steps,),
        out_shape=[
            jax.ShapeDtypeStruct((rows, own), bf16),
            jax.ShapeDtypeStruct((size, cols_in), f32),
            jax.ShapeDtypeStruct((size, cols - cols_in), f32),
        ],
        in_specs=specs,
        out_specs=[
            lines,
            pl.BlockSpec((size, cols_in), lambda i: (0, 0)),
            pl.BlockSpec((size, cols - cols_in), lambda i: (0, 0)),
        ],
        compiler_params=pltpu.CompilerParams(vmem_limit_bytes=32 * 2**20),
        cost_estimate=pl.CostEstimate(
            flops=rows * own, bytes_accessed=12 * 2**20, transcendentals=0
        ),
    )(kept, sent, keep, got, *rest)


def exchange(block, tensor):
    if tensor == 2:
        return lax.ppermute(block, "tensor", [(0, 1), (1, 0)])
    own = block.shape[1]
    every = lax.all_gather(block, "tensor", axis=1, tiled=True)
    return jnp.roll(every, -lax.axis_index("tensor") * own, axis=1)[:, own:]


def give_back(block, own, tensor):
    if tensor == 2:
        return lax.ppermute(block, "tensor", [(0, 1), (1, 0)])
    every = jnp.concatenate([jnp.zeros((block.shape[0], own), block.dtype), block], axis=1)
    every = jnp.roll(every, lax.axis_index("tensor") * own, axis=1)
    return lax.psum_scatter(every, "tensor", scatter_dimension=1, tiled=True)


def local(events, cotangent, w_in, w_out, slot_source, slot_length):
    tensor = lax.axis_size("tensor")
    users = lax.axis_size("user")
    hist, seq_len, own = events.shape
    x = events.reshape(hist * seq_len, own)
    d = cotangent.reshape(hist * seq_len, own)
    blocks = sum(steps for _, steps in GROUPS)
    rows = hist // blocks * seq_len
    cut = (w_in.shape[1] + w_out.shape[1] + SLOTS) // 128 * 5 // 8 * 128
    head, ahead = stage(x, d, w_in, rows, cut)
    far = [exchange(ahead, tensor)]
    for start, steps in GROUPS[1:]:
        spans = [slice(i * rows, (i + 1) * rows) for i in range(start, start + steps)]
        x_late, d_late, _ = lax.optimization_barrier((x, d, ahead))
        ahead = jnp.concatenate([t[span] for span in spans for t in (x_late, d_late)], axis=0)
        far.append(exchange(ahead, tensor))

    user = lax.axis_index("user")
    slots = jnp.stack([slot_source, slot_length]).astype(bf16)
    slots = jnp.pad(slots, ((0, 0), (0, SLOTS // 2 - hist)), constant_values=-1)
    slots = jnp.pad(slots.reshape(1, SLOTS), ((0, w_in.shape[0] - 1), (0, 0)), constant_values=-1)
    shard = jnp.concatenate([w_in, w_out, slots], axis=1)
    pieces = gather_parts(head, shard, users, user)
    where = jnp.stack([lax.axis_index("tensor"), user]).astype(jnp.int32)

    past = []
    for group, theirs in zip(GROUPS, far):
        kept, bs, *grads = group_call(
            group, blocks, users, tensor, where, x, d, theirs, pieces, past
        )
        past = grads + [kept, bs]
    sent = give_back(bs, own, tensor)
    keep, send = grads
    got, rest = scatter_parts(keep, send, users)
    grad_x, grad_in, grad_out = finish(kept, sent, keep, got, rest, w_in.shape[1])
    return (grad_x.reshape(hist, seq_len, own), grad_in, grad_out)


def solution(mesh):
    in_specs = (
        P("user", None, "tensor"),
        P("user", None, "tensor"),
        P("user", "tensor"),
        P("user", "tensor"),
        P("user"),
        P("user"),
    )
    out_specs = (P("user", None, "tensor"), P("user", "tensor"), P("user", "tensor"))
    return jax.shard_map(local, mesh=mesh, in_specs=in_specs, out_specs=out_specs, check_vma=False)
```

```python
import functools

import jax
import jax.numpy as jnp
from jax import lax
from jax.experimental import pallas as pl
from jax.experimental.pallas import tpu as pltpu
from jax.sharding import PartitionSpec as P

HEAD_DIM = 128
SEQ_LEN = 128
SLOTS = 128
GROUPS = ((0, 2), (2, 1), (3, 1))

eps = 1e-05
f32 = jnp.float32
bf16 = jnp.bfloat16


def dot_nn(a, b):
    return lax.dot_general(a, b, (((1,), (0,)), ((), ())), preferred_element_type=f32)


def dot_nt(a, b):
    return lax.dot_general(a, b, (((1,), (1,)), ((), ())), preferred_element_type=f32)


def dot_tn(a, b):
    return lax.dot_general(a, b, (((0,), (0,)), ((), ())), preferred_element_type=f32)


def row_mean(t):
    return jnp.mean(t, axis=1, keepdims=True)


def gates(t):
    sig = 0.5 * jnp.tanh(0.5 * t) + 0.5
    silu = t * sig
    return silu, sig + silu * (1.0 - sig)


def attention(pairs, causal, g_s, dh_s, slope_s, hb_s, dz_s):
    scale = HEAD_DIM ** (-0.5)
    spans = [pl.ds(n * SEQ_LEN, SEQ_LEN) for _, n in pairs]
    lanes = [[pl.ds((4 * h + e) * HEAD_DIM, HEAD_DIM) for e in range(4)] for h, _ in pairs]
    heads = [pl.ds(h * HEAD_DIM, HEAD_DIM) for h, _ in pairs]
    every = range(len(pairs))
    def part(i, e):
        return g_s[spans[i], lanes[i][e]]

    s = [dot_nt(part(i, 2), part(i, 3)) * scale for i in every]
    pair = [gates(t) for t in s]
    attn = [jnp.where(causal, silu * (1.0 / SEQ_LEN), 0.0).astype(bf16) for silu, _ in pair]
    slope = [jnp.where(causal, t * (scale / SEQ_LEN), 0.0) for _, t in pair]
    y = [dot_nn(attn[i], part(i, 1)) for i in every]
    cen = [t - row_mean(t) for t in y]
    rstd = [lax.rsqrt(row_mean(t * t) + eps) for t in cen]
    yn = [cen[i] * rstd[i] for i in every]
    uf = [part(i, 0).astype(f32) for i in every]
    dh = [dh_s[spans[i], heads[i]] for i in every]
    dyn = [dh[i] * uf[i] for i in every]
    one = [row_mean(t) for t in dyn]
    two = [row_mean(dyn[i] * yn[i]) for i in every]
    dy = [((dyn[i] - one[i] - yn[i] * two[i]) * rstd[i]).astype(bf16) for i in every]
    grad_a = [dot_nt(dy[i], part(i, 1)) for i in every]
    ds = [(grad_a[i] * slope[i]).astype(bf16) for i in every]

    def store(i, e, grad):
        dz_s[spans[i], lanes[i][e]] = (grad * slope_s[spans[i], lanes[i][e]]).astype(bf16)

    for i in every:
        hb_s[spans[i], heads[i]] = (yn[i] * uf[i]).astype(bf16)
        store(i, 0, dh[i] * yn[i])
    for i in every:
        store(i, 1, dot_tn(attn[i], dy[i]))
    for i in every:
        store(i, 2, dot_nn(ds[i], part(i, 3)))
    for i in every:
        store(i, 3, dot_tn(ds[i], part(i, 2)))


def split_order(count):
    rest = sorted(range(1, count), key=lambda j: abs(j - count / 2))
    return rest + [0]


def piece_order(far, cut):
    slow = split_order(far)[:-1]
    return [
        (lo, [(j, xs, cs) for j in js])
        for lo, js in ((0, [0]), (0, slow), (cut, slow))
        for cs in range(2)
        for xs in range(2)
    ]


def gather_parts(shard, cut, users, user):
    def swap(block, bit):
        return lax.ppermute(block, "user", [(i, i ^ bit) for i in range(users)])

    def spread(block):
        across = swap(block, 2)
        return [block, across, swap(block, 1), swap(across, 1)]

    arrays, moved = spread(shard), []
    for part in (shard[:, :cut], shard[:, cut:]):
        if moved:
            part = jnp.where(user < 0, sum(t[:1, :1] for t in moved), part)
        moved = []
        for j in split_order(users // 4)[:-1]:
            pairs = [(i, (i - 4 * j) % users) for i in range(users)]
            moved.append(lax.ppermute(part, "user", pairs))
        block = jnp.concatenate(moved, axis=0)
        block = jnp.where(user < 0, arrays[-3][:1, :1], block)
        arrays += spread(block)
    return arrays


def group_kernel(start, steps, first, last, heads, parts, users, *refs):
    refs = list(refs)
    where_ref, xo_ref, do_ref, far_ref = refs[:4]
    pieces, refs = refs[4:16], refs[16:]
    acc_hbm = None if first else refs.pop(0)
    refs = refs if first else refs[2:]
    gx_ref, bs_ref = refs[:2]
    refs = refs[2:]
    grads_hbm = [refs.pop(0) for _ in range(2 if last else 1)]
    (w_s, acc_s, nb_s, nt_s, dm_s, dt_s, dz_s, hb_s, g_s, slope_s, dh_s, out_s) = refs[:12]
    load_sems, store_sems = refs[12:]
    rows, own = xo_ref.shape
    width = own * parts
    cols_in = heads * 4 * HEAD_DIM
    cols = cols_in + heads * HEAD_DIM
    histories = rows // SEQ_LEN
    me, user = where_ref[0], where_ref[1]
    step = pl.program_id(0)

    def only(index, run):
        if steps == 1:
            run()
        else:
            pl.when(step == index)(run)

    size = width // users
    far = users // 4
    zi, xi, ci = user // 4, lax.rem(user // 2, 2), lax.rem(user, 2)

    def rows_of(j, xs, cs):
        zd = lax.rem(zi + j, far)
        xd = xi if xs == 0 else 1 - xi
        cd = ci if cs == 0 else 1 - ci
        row = ((zd * 2 + xd) * 2 + cd) * size
        row = lax.rem(row // own - me + parts, parts) * own + lax.rem(row, own)
        return pl.ds(pl.multiple_of(row, size), size)

    loads = []
    for piece, (lo, offsets) in zip(pieces, piece_order(far, pieces[4].shape[1])):
        for at, offset in enumerate(offsets):
            there = w_s.at[rows_of(*offset), pl.ds(lo, piece.shape[1])]
            here = piece.at[pl.ds(at * size, size)]
            loads.append(pltpu.make_async_copy(here, there, load_sems.at[len(loads)]))
    if not first:
        acc_load = pltpu.make_async_copy(acc_hbm, acc_s, load_sems.at[2 * users])

    def begin():
        for copy in loads:
            copy.start()
        if first:
            acc_s[...] = jnp.zeros_like(acc_s)
        else:
            acc_load.start()

    def loaded():
        for copy in loads:
            copy.wait()

    only(0, begin)

    causal = lax.broadcasted_iota(jnp.int32, (SEQ_LEN, SEQ_LEN), 0) >= lax.broadcasted_iota(
        jnp.int32, (SEQ_LEN, SEQ_LEN), 1
    )
    position = lax.broadcasted_iota(jnp.int32, (SEQ_LEN, 1), 0).astype(f32)
    half = min(2 * SEQ_LEN, rows)
    halves = [slice(lo, lo + half) for lo in range(0, rows, half)]

    rstds = []
    for here in halves:
        xo = xo_ref[here, :].astype(f32)
        xr = far_ref[here, :].astype(f32)
        mean = (jnp.sum(xo, axis=1, keepdims=True) + jnp.sum(xr, axis=1, keepdims=True)) / width
        xo = xo - mean
        xr = xr - mean
        var = (
            jnp.sum(xo * xo, axis=1, keepdims=True) + jnp.sum(xr * xr, axis=1, keepdims=True)
        ) / width
        rstd = lax.rsqrt(var + eps)
        rstds.append(rstd)
        bo = (xo * rstd).astype(bf16)
        br = (xr * rstd).astype(bf16)
        nb_s[here, :own] = bo
        nb_s[here, own:] = br
        nt_s[:own, here] = bo.T
        nt_s[own:, here] = br.T
    only(0, loaded)
    table = w_s[:, cols:].astype(f32)
    lengths = pltpu.roll(table, SLOTS // 2, 1)
    lane = lax.broadcasted_iota(jnp.int32, (1, SLOTS), 1)
    lengths = jnp.where(table == user.astype(f32), lengths, 0.0)
    lengths = jnp.sum(lengths, axis=0, keepdims=True)
    for here in halves:
        base = start * histories + step * histories
        valid = jnp.concatenate(
            [
                (
                    position
                    < jnp.sum(jnp.where(lane == base + n, lengths, 0.0), axis=1, keepdims=True)
                ).astype(f32)
                for n in range(here.start // SEQ_LEN, here.stop // SEQ_LEN)
            ],
            axis=0,
        ).astype(bf16)
        there = slice(rows + here.start, rows + here.stop)
        do = do_ref[here, :] * valid
        dr = far_ref[there, :] * valid
        dm_s[here, :own] = do
        dm_s[here, own:] = dr
        dt_s[:own, here] = do.T
        dt_s[own:, here] = dr.T
    dh_s[...] = dot_nn(dm_s[...], w_s[:, cols_in:cols])

    if not first:
        only(0, acc_load.wait)
    target = out_s if last else acc_s
    stores = []

    def ship(lo, wide):
        lanes = pl.ds(lo, wide)
        if not last:
            stores.append(
                pltpu.make_async_copy(
                    acc_s.at[:, lanes], grads_hbm[0].at[:, lanes], store_sems.at[len(stores)]
                )
            )
            only(steps - 1, stores[-1].start)
            return
        keep, send = grads_hbm
        for at, j in enumerate(split_order(far)):
            for xs in range(2):
                for cs in range(2):
                    there = keep if cs == 0 else send
                    stores.append(
                        pltpu.make_async_copy(
                            out_s.at[rows_of(far - j, xs, cs), lanes],
                            there.at[pl.ds((xs * far + at) * size, size), lanes],
                            store_sems.at[len(stores)],
                        )
                    )
                    only(steps - 1, stores[-1].start)

    def add(lhs, rhs, lo, wide):
        chunk = min(512, width)
        for r in range(0, width, chunk):
            term = dot_nn(lhs[r : r + chunk, :], rhs[...]) + acc_s[r : r + chunk, lo : lo + wide]
            target[r : r + chunk, lo : lo + wide] = term.astype(target.dtype)
        ship(lo, wide)

    block = 4 * HEAD_DIM

    def project(h):
        c = slice(h * block, (h + 1) * block)
        silu, slope_s[:, c] = gates(dot_nn(nb_s[...], w_s[:, c]))
        g_s[:, c] = silu.astype(bf16)

    project(0)
    for h in range(heads):
        if h + 1 < heads:
            project(h + 1)
        units = [(h, n) for n in range(histories)]
        attention(units, causal, g_s, dh_s, slope_s, hb_s, dz_s)
        if h > 0:
            add(nt_s, dz_s.at[:, (h - 1) * block : h * block], (h - 1) * block, block)
    add(nt_s, dz_s.at[:, (heads - 1) * block : cols_in], (heads - 1) * block, block)
    add(dt_s, hb_s, cols_in, heads * HEAD_DIM)
    dn_all = dot_nt(dz_s[...], w_s[:, :cols_in])
    for here, rstd in zip(halves, rstds):
        dn = dn_all[here, :]
        nf = nb_s[here, :].astype(f32)
        one = jnp.sum(dn, axis=1, keepdims=True) / width
        two = jnp.sum(dn * nf, axis=1, keepdims=True) / width
        branch = (dn - one - nf * two) * rstd
        gx_ref[here, :] = (dm_s[here, :own].astype(f32) + branch[:, :own]).astype(bf16)
        bs_ref[here, :] = branch[:, own:].astype(bf16)

    for copy in stores:
        only(steps - 1, copy.wait)


def group_call(group, blocks, users, parts, where, x, d, far, pieces, past):
    start, steps = group
    first, last = start == 0, start + steps == blocks
    rows, own = x.shape[0] // blocks, x.shape[1]
    width = own * parts
    cols = pieces[0].shape[1] - SLOTS
    heads = cols // (5 * HEAD_DIM)
    cols_in = heads * 4 * HEAD_DIM
    smem = pl.BlockSpec(memory_space=pltpu.SMEM)
    anywhere = pl.BlockSpec(memory_space=pl.ANY)
    mine = pl.BlockSpec((rows, own), lambda i: (start + i, 0))
    theirs = pl.BlockSpec((2 * rows, width - own), lambda i: (i, 0))
    args = [where, x, d, far] + pieces + past
    specs = [smem, mine, mine, theirs] + [anywhere] * (len(pieces) + len(past))
    if last:
        grads = [jax.ShapeDtypeStruct((width // 2, cols), bf16)] * 2
    else:
        grads = [jax.ShapeDtypeStruct((width, cols), f32)]
    flops = steps * (4 * rows * width * cols + 2 * rows * width * cols_in)
    return pl.pallas_call(
        functools.partial(group_kernel, start, steps, first, last, heads, parts, users),
        grid=(steps,),
        out_shape=[
            jax.ShapeDtypeStruct((blocks * rows, own), bf16),
            jax.ShapeDtypeStruct((blocks * rows, width - own), bf16),
        ]
        + grads,
        in_specs=specs,
        out_specs=[
            pl.BlockSpec((rows, own), lambda i: (start + i, 0)),
            pl.BlockSpec((rows, width - own), lambda i: (start + i, 0)),
        ]
        + [anywhere] * len(grads),
        input_output_aliases={} if first else {len(pieces) + 5: 0, len(pieces) + 6: 1},
        scratch_shapes=[
            pltpu.VMEM((width, cols + SLOTS), bf16),
            pltpu.VMEM((width, cols), f32),
            pltpu.VMEM((rows, width), bf16),
            pltpu.VMEM((width, rows), bf16),
            pltpu.VMEM((rows, width), bf16),
            pltpu.VMEM((width, rows), bf16),
            pltpu.VMEM((rows, cols_in), bf16),
            pltpu.VMEM((rows, cols - cols_in), bf16),
            pltpu.VMEM((rows, cols_in), bf16),
            pltpu.VMEM((rows, cols_in), f32),
            pltpu.VMEM((rows, cols - cols_in), f32),
            pltpu.VMEM((width, cols) if last else (16, 128), bf16),
            pltpu.SemaphoreType.DMA((2 * users + 1,)),
            pltpu.SemaphoreType.DMA(((users if last else 1) * (heads + 1),)),
        ],
        compiler_params=pltpu.CompilerParams(vmem_limit_bytes=56 * 2**20),
        cost_estimate=pl.CostEstimate(
            flops=flops, bytes_accessed=16 * 2**20, transcendentals=steps * rows * cols
        ),
    )(*args)


def scatter_parts(keep, send, users):
    far = users // 4
    order = split_order(far)
    size = keep.shape[0] // (2 * far)

    def swap(block, bit):
        return lax.ppermute(block, "user", [(i, i ^ bit) for i in range(users)])

    got = swap(send, 1)

    def both(lo, hi):
        span = slice(lo * size, hi * size)
        return keep[span].astype(f32) + got[span].astype(f32)

    cuts = [(0, 1), (1, far - 1), (far - 1, far)]
    across = [swap(both(far + lo, far + hi).astype(bf16), 2) for lo, hi in cuts]
    moved = []
    for (lo, hi), other in zip(cuts[:2], across):
        near = (both(lo, hi) + other.astype(f32)).astype(bf16)
        for at in range(lo, hi):
            pairs = [(i, (i - 4 * order[at]) % users) for i in range(users)]
            block = near[(at - lo) * size : (at - lo + 1) * size]
            moved.append(lax.ppermute(block, "user", pairs))
    return got, [across[2]] + moved


def finish_kernel(cols_in, kept_ref, sent_ref, *refs):
    terms = refs[:-3]
    gx_ref, win_ref, wout_ref = refs[-3:]
    gx_ref[...] = (kept_ref[...].astype(f32) + sent_ref[...].astype(f32)).astype(bf16)

    @pl.when(pl.program_id(0) == 0)
    def _():
        total = terms[0][...].astype(f32)
        for term in terms[1:]:
            total = total + term[...].astype(f32)
        win_ref[...] = total[:, :cols_in]
        wout_ref[...] = total[:, cols_in:]


def finish(kept, sent, keep, got, rest, cols_in):
    rows, own = kept.shape
    size, cols = rest[0].shape
    slot = keep.shape[0] // (2 * size) - 1
    steps = 4
    lines = pl.BlockSpec((rows // steps, own), lambda i: (i, 0))
    specs = [lines] * 2
    specs += [pl.BlockSpec((size, cols), lambda i: (slot, 0))] * 2
    specs += [pl.BlockSpec((size, cols), lambda i: (0, 0))] * len(rest)
    return pl.pallas_call(
        functools.partial(finish_kernel, cols_in),
        grid=(steps,),
        out_shape=[
            jax.ShapeDtypeStruct((rows, own), bf16),
            jax.ShapeDtypeStruct((size, cols_in), f32),
            jax.ShapeDtypeStruct((size, cols - cols_in), f32),
        ],
        in_specs=specs,
        out_specs=[
            lines,
            pl.BlockSpec((size, cols_in), lambda i: (0, 0)),
            pl.BlockSpec((size, cols - cols_in), lambda i: (0, 0)),
        ],
        compiler_params=pltpu.CompilerParams(vmem_limit_bytes=32 * 2**20),
        cost_estimate=pl.CostEstimate(
            flops=rows * own, bytes_accessed=12 * 2**20, transcendentals=0
        ),
    )(kept, sent, keep, got, *rest)


def exchange(block, tensor):
    if tensor == 2:
        return lax.ppermute(block, "tensor", [(0, 1), (1, 0)])
    own = block.shape[1]
    every = lax.all_gather(block, "tensor", axis=1, tiled=True)
    return jnp.roll(every, -lax.axis_index("tensor") * own, axis=1)[:, own:]


def give_back(block, own, tensor):
    if tensor == 2:
        return lax.ppermute(block, "tensor", [(0, 1), (1, 0)])
    every = jnp.concatenate([jnp.zeros((block.shape[0], own), block.dtype), block], axis=1)
    every = jnp.roll(every, lax.axis_index("tensor") * own, axis=1)
    return lax.psum_scatter(every, "tensor", scatter_dimension=1, tiled=True)


def local(events, cotangent, w_in, w_out, slot_source, slot_length):
    tensor = lax.axis_size("tensor")
    users = lax.axis_size("user")
    hist, seq_len, own = events.shape
    x = events.reshape(hist * seq_len, own)
    d = cotangent.reshape(hist * seq_len, own)
    blocks = sum(steps for _, steps in GROUPS)
    rows = hist // blocks * seq_len
    far, ahead = [], None
    for start, steps in GROUPS:
        spans = [slice(i * rows, (i + 1) * rows) for i in range(start, start + steps)]
        if ahead is not None:
            x, d, _ = lax.optimization_barrier((x, d, ahead))
        ahead = jnp.concatenate([t[span] for span in spans for t in (x, d)], axis=0)
        far.append(exchange(ahead, tensor))

    user = lax.axis_index("user")
    slots = jnp.stack([slot_source, slot_length]).astype(bf16)
    slots = jnp.pad(slots, ((0, 0), (0, SLOTS // 2 - hist)), constant_values=-1)
    slots = jnp.pad(slots.reshape(1, SLOTS), ((0, w_in.shape[0] - 1), (0, 0)), constant_values=-1)
    shard = jnp.concatenate([w_in, w_out, slots], axis=1)
    pieces = gather_parts(shard, shard.shape[1] // 256 * 128, users, user)
    where = jnp.stack([lax.axis_index("tensor"), user]).astype(jnp.int32)

    past = []
    for group, theirs in zip(GROUPS, far):
        kept, bs, *grads = group_call(
            group, blocks, users, tensor, where, x, d, theirs, pieces, past
        )
        past = grads + [kept, bs]
    sent = give_back(bs, own, tensor)
    keep, send = grads
    got, rest = scatter_parts(keep, send, users)
    grad_x, grad_in, grad_out = finish(kept, sent, keep, got, rest, w_in.shape[1])
    return (grad_x.reshape(hist, seq_len, own), grad_in, grad_out)


def solution(mesh):
    in_specs = (
        P("user", None, "tensor"),
        P("user", None, "tensor"),
        P("user", "tensor"),
        P("user", "tensor"),
        P("user"),
        P("user"),
    )
    out_specs = (P("user", None, "tensor"), P("user", "tensor"), P("user", "tensor"))
    return jax.shard_map(local, mesh=mesh, in_specs=in_specs, out_specs=out_specs, check_vma=False)
```

```python
import functools

import jax
import jax.numpy as jnp
from jax import lax
from jax.experimental import pallas as pl
from jax.experimental.pallas import tpu as pltpu
from jax.sharding import PartitionSpec as P

HEAD_DIM = 128
SEQ_LEN = 128
SLOTS = 128
GROUPS = ((0, 2), (2, 1), (3, 1))

eps = 1e-05
f32 = jnp.float32
bf16 = jnp.bfloat16


def dot_nn(a, b):
    return lax.dot_general(a, b, (((1,), (0,)), ((), ())), preferred_element_type=f32)


def dot_nt(a, b):
    return lax.dot_general(a, b, (((1,), (1,)), ((), ())), preferred_element_type=f32)


def dot_tn(a, b):
    return lax.dot_general(a, b, (((0,), (0,)), ((), ())), preferred_element_type=f32)


def row_mean(t):
    return jnp.mean(t, axis=1, keepdims=True)


def gates(t):
    sig = 0.5 * jnp.tanh(0.5 * t) + 0.5
    silu = t * sig
    return silu, sig + silu * (1.0 - sig)


def attention(pairs, causal, g_s, dh_s, slope_s, hb_s, dz_s):
    scale = HEAD_DIM ** (-0.5)
    spans = [pl.ds(n * SEQ_LEN, SEQ_LEN) for _, n in pairs]
    lanes = [[pl.ds((4 * h + e) * HEAD_DIM, HEAD_DIM) for e in range(4)] for h, _ in pairs]
    heads = [pl.ds(h * HEAD_DIM, HEAD_DIM) for h, _ in pairs]
    every = range(len(pairs))
    def part(i, e):
        return g_s[spans[i], lanes[i][e]]

    s = [dot_nt(part(i, 2), part(i, 3)) * scale for i in every]
    pair = [gates(t) for t in s]
    attn = [jnp.where(causal, silu * (1.0 / SEQ_LEN), 0.0).astype(bf16) for silu, _ in pair]
    slope = [jnp.where(causal, t * (scale / SEQ_LEN), 0.0) for _, t in pair]
    y = [dot_nn(attn[i], part(i, 1)) for i in every]
    cen = [t - row_mean(t) for t in y]
    rstd = [lax.rsqrt(row_mean(t * t) + eps) for t in cen]
    yn = [cen[i] * rstd[i] for i in every]
    uf = [part(i, 0).astype(f32) for i in every]
    dh = [dh_s[spans[i], heads[i]] for i in every]
    dyn = [dh[i] * uf[i] for i in every]
    one = [row_mean(t) for t in dyn]
    two = [row_mean(dyn[i] * yn[i]) for i in every]
    dy = [((dyn[i] - one[i] - yn[i] * two[i]) * rstd[i]).astype(bf16) for i in every]
    grad_a = [dot_nt(dy[i], part(i, 1)) for i in every]
    ds = [(grad_a[i] * slope[i]).astype(bf16) for i in every]

    def store(i, e, grad):
        dz_s[spans[i], lanes[i][e]] = (grad * slope_s[spans[i], lanes[i][e]]).astype(bf16)

    for i in every:
        hb_s[spans[i], heads[i]] = (yn[i] * uf[i]).astype(bf16)
        store(i, 0, dh[i] * yn[i])
    for i in every:
        store(i, 1, dot_tn(attn[i], dy[i]))
    for i in every:
        store(i, 2, dot_nn(ds[i], part(i, 3)))
    for i in every:
        store(i, 3, dot_tn(ds[i], part(i, 2)))


def split_order(count):
    rest = sorted(range(1, count), key=lambda j: abs(j - count / 2))
    return rest + [0]


def piece_order(far, cut):
    slow = split_order(far)[:-1]
    return [
        (lo, [(j, xs, cs) for j in js])
        for lo, js in ((0, [0]), (0, slow), (cut, slow))
        for cs in range(2)
        for xs in range(2)
    ]


def gather_parts(shard, cut, users, user):
    def swap(block, bit):
        return lax.ppermute(block, "user", [(i, i ^ bit) for i in range(users)])

    def spread(block):
        across = swap(block, 2)
        return [block, across, swap(block, 1), swap(across, 1)]

    arrays, moved = spread(shard), []
    for part in (shard[:, :cut], shard[:, cut:]):
        if moved:
            part = jnp.where(user < 0, sum(t[:1, :1] for t in moved), part)
        moved = []
        for j in split_order(users // 4)[:-1]:
            pairs = [(i, (i - 4 * j) % users) for i in range(users)]
            moved.append(lax.ppermute(part, "user", pairs))
        block = jnp.concatenate(moved, axis=0)
        block = jnp.where(user < 0, arrays[-3][:1, :1], block)
        arrays += spread(block)
    return arrays


def group_kernel(start, steps, first, last, heads, parts, users, *refs):
    refs = list(refs)
    where_ref, xo_ref, do_ref, far_ref = refs[:4]
    pieces, refs = refs[4:16], refs[16:]
    acc_hbm = None if first else refs.pop(0)
    refs = refs if first else refs[2:]
    gx_ref, bs_ref = refs[:2]
    refs = refs[2:]
    grads_hbm = [refs.pop(0) for _ in range(2 if last else 1)]
    (w_s, acc_s, nb_s, nt_s, dm_s, dt_s, dz_s, hb_s, g_s, slope_s, dh_s, out_s) = refs[:12]
    load_sems, store_sems = refs[12:]
    rows, own = xo_ref.shape
    width = own * parts
    cols_in = heads * 4 * HEAD_DIM
    cols = cols_in + heads * HEAD_DIM
    histories = rows // SEQ_LEN
    me, user = where_ref[0], where_ref[1]
    step = pl.program_id(0)

    def only(index, run):
        if steps == 1:
            run()
        else:
            pl.when(step == index)(run)

    size = width // users
    far = users // 4
    zi, xi, ci = user // 4, lax.rem(user // 2, 2), lax.rem(user, 2)

    def rows_of(j, xs, cs):
        zd = lax.rem(zi + j, far)
        xd = xi if xs == 0 else 1 - xi
        cd = ci if cs == 0 else 1 - ci
        row = ((zd * 2 + xd) * 2 + cd) * size
        row = lax.rem(row // own - me + parts, parts) * own + lax.rem(row, own)
        return pl.ds(pl.multiple_of(row, size), size)

    loads = []
    for piece, (lo, offsets) in zip(pieces, piece_order(far, pieces[4].shape[1])):
        for at, offset in enumerate(offsets):
            there = w_s.at[rows_of(*offset), pl.ds(lo, piece.shape[1])]
            here = piece.at[pl.ds(at * size, size)]
            loads.append(pltpu.make_async_copy(here, there, load_sems.at[len(loads)]))
    if not first:
        acc_load = pltpu.make_async_copy(acc_hbm, acc_s, load_sems.at[2 * users])

    def begin():
        for copy in loads:
            copy.start()
        if first:
            acc_s[...] = jnp.zeros_like(acc_s)
        else:
            acc_load.start()

    def loaded():
        for copy in loads:
            copy.wait()

    only(0, begin)

    causal = lax.broadcasted_iota(jnp.int32, (SEQ_LEN, SEQ_LEN), 0) >= lax.broadcasted_iota(
        jnp.int32, (SEQ_LEN, SEQ_LEN), 1
    )
    position = lax.broadcasted_iota(jnp.int32, (SEQ_LEN, 1), 0).astype(f32)
    half = min(2 * SEQ_LEN, rows)
    halves = [slice(lo, lo + half) for lo in range(0, rows, half)]

    rstds = []
    for here in halves:
        xo = xo_ref[here, :].astype(f32)
        xr = far_ref[here, :].astype(f32)
        mean = (jnp.sum(xo, axis=1, keepdims=True) + jnp.sum(xr, axis=1, keepdims=True)) / width
        xo = xo - mean
        xr = xr - mean
        var = (
            jnp.sum(xo * xo, axis=1, keepdims=True) + jnp.sum(xr * xr, axis=1, keepdims=True)
        ) / width
        rstd = lax.rsqrt(var + eps)
        rstds.append(rstd)
        bo = (xo * rstd).astype(bf16)
        br = (xr * rstd).astype(bf16)
        nb_s[here, :own] = bo
        nb_s[here, own:] = br
        nt_s[:own, here] = bo.T
        nt_s[own:, here] = br.T
    only(0, loaded)
    for h in range(heads):
        c = slice(h * 4 * HEAD_DIM, (h + 1) * 4 * HEAD_DIM)
        silu, slope_s[:, c] = gates(dot_nn(nb_s[...], w_s[:, c]))
        g_s[:, c] = silu.astype(bf16)
    table = w_s[:, cols:].astype(f32)
    lengths = pltpu.roll(table, SLOTS // 2, 1)
    lane = lax.broadcasted_iota(jnp.int32, (1, SLOTS), 1)
    lengths = jnp.where(table == user.astype(f32), lengths, 0.0)
    lengths = jnp.sum(lengths, axis=0, keepdims=True)
    for here in halves:
        base = start * histories + step * histories
        valid = jnp.concatenate(
            [
                (
                    position
                    < jnp.sum(jnp.where(lane == base + n, lengths, 0.0), axis=1, keepdims=True)
                ).astype(f32)
                for n in range(here.start // SEQ_LEN, here.stop // SEQ_LEN)
            ],
            axis=0,
        ).astype(bf16)
        there = slice(rows + here.start, rows + here.stop)
        do = do_ref[here, :] * valid
        dr = far_ref[there, :] * valid
        dm_s[here, :own] = do
        dm_s[here, own:] = dr
        dt_s[:own, here] = do.T
        dt_s[own:, here] = dr.T
    dh_s[...] = dot_nn(dm_s[...], w_s[:, cols_in:cols])

    if not first:
        only(0, acc_load.wait)
    target = out_s if last else acc_s
    stores = []

    def ship(lo, wide):
        lanes = pl.ds(lo, wide)
        if not last:
            stores.append(
                pltpu.make_async_copy(
                    acc_s.at[:, lanes], grads_hbm[0].at[:, lanes], store_sems.at[len(stores)]
                )
            )
            only(steps - 1, stores[-1].start)
            return
        keep, send = grads_hbm
        for at, j in enumerate(split_order(far)):
            for xs in range(2):
                for cs in range(2):
                    there = keep if cs == 0 else send
                    stores.append(
                        pltpu.make_async_copy(
                            out_s.at[rows_of(far - j, xs, cs), lanes],
                            there.at[pl.ds((xs * far + at) * size, size), lanes],
                            store_sems.at[len(stores)],
                        )
                    )
                    only(steps - 1, stores[-1].start)

    def add(lhs, rhs, lo, wide):
        chunk = min(512, width)
        for r in range(0, width, chunk):
            term = dot_nn(lhs[r : r + chunk, :], rhs[...]) + acc_s[r : r + chunk, lo : lo + wide]
            target[r : r + chunk, lo : lo + wide] = term.astype(target.dtype)
        ship(lo, wide)

    block = 4 * HEAD_DIM
    stride = max(1, 16 // histories)
    for lo in range(0, heads, stride):
        hi = min(lo + stride, heads)
        units = [(h, n) for h in range(lo, hi) for n in range(histories)]
        attention(units, causal, g_s, dh_s, slope_s, hb_s, dz_s)
        for h in range(max(0, lo - stride), lo):
            add(nt_s, dz_s.at[:, h * block : (h + 1) * block], h * block, block)
    for h in range((heads - 1) // stride * stride, heads):
        add(nt_s, dz_s.at[:, h * block : (h + 1) * block], h * block, block)
    add(dt_s, hb_s, cols_in, heads * HEAD_DIM)
    dn_all = dot_nt(dz_s[...], w_s[:, :cols_in])
    for here, rstd in zip(halves, rstds):
        dn = dn_all[here, :]
        nf = nb_s[here, :].astype(f32)
        one = jnp.sum(dn, axis=1, keepdims=True) / width
        two = jnp.sum(dn * nf, axis=1, keepdims=True) / width
        branch = (dn - one - nf * two) * rstd
        gx_ref[here, :] = (dm_s[here, :own].astype(f32) + branch[:, :own]).astype(bf16)
        bs_ref[here, :] = branch[:, own:].astype(bf16)

    for copy in stores:
        only(steps - 1, copy.wait)


def group_call(group, blocks, users, parts, where, x, d, far, pieces, past):
    start, steps = group
    first, last = start == 0, start + steps == blocks
    rows, own = x.shape[0] // blocks, x.shape[1]
    width = own * parts
    cols = pieces[0].shape[1] - SLOTS
    heads = cols // (5 * HEAD_DIM)
    cols_in = heads * 4 * HEAD_DIM
    smem = pl.BlockSpec(memory_space=pltpu.SMEM)
    anywhere = pl.BlockSpec(memory_space=pl.ANY)
    mine = pl.BlockSpec((rows, own), lambda i: (start + i, 0))
    theirs = pl.BlockSpec((2 * rows, width - own), lambda i: (i, 0))
    args = [where, x, d, far] + pieces + past
    specs = [smem, mine, mine, theirs] + [anywhere] * (len(pieces) + len(past))
    if last:
        grads = [jax.ShapeDtypeStruct((width // 2, cols), bf16)] * 2
    else:
        grads = [jax.ShapeDtypeStruct((width, cols), f32)]
    flops = steps * (4 * rows * width * cols + 2 * rows * width * cols_in)
    return pl.pallas_call(
        functools.partial(group_kernel, start, steps, first, last, heads, parts, users),
        grid=(steps,),
        out_shape=[
            jax.ShapeDtypeStruct((blocks * rows, own), bf16),
            jax.ShapeDtypeStruct((blocks * rows, width - own), bf16),
        ]
        + grads,
        in_specs=specs,
        out_specs=[
            pl.BlockSpec((rows, own), lambda i: (start + i, 0)),
            pl.BlockSpec((rows, width - own), lambda i: (start + i, 0)),
        ]
        + [anywhere] * len(grads),
        input_output_aliases={} if first else {len(pieces) + 5: 0, len(pieces) + 6: 1},
        scratch_shapes=[
            pltpu.VMEM((width, cols + SLOTS), bf16),
            pltpu.VMEM((width, cols), f32),
            pltpu.VMEM((rows, width), bf16),
            pltpu.VMEM((width, rows), bf16),
            pltpu.VMEM((rows, width), bf16),
            pltpu.VMEM((width, rows), bf16),
            pltpu.VMEM((rows, cols_in), bf16),
            pltpu.VMEM((rows, cols - cols_in), bf16),
            pltpu.VMEM((rows, cols_in), bf16),
            pltpu.VMEM((rows, cols_in), f32),
            pltpu.VMEM((rows, cols - cols_in), f32),
            pltpu.VMEM((width, cols) if last else (16, 128), bf16),
            pltpu.SemaphoreType.DMA((2 * users + 1,)),
            pltpu.SemaphoreType.DMA(((users if last else 1) * (heads + 1),)),
        ],
        compiler_params=pltpu.CompilerParams(vmem_limit_bytes=56 * 2**20),
        cost_estimate=pl.CostEstimate(
            flops=flops, bytes_accessed=16 * 2**20, transcendentals=steps * rows * cols
        ),
    )(*args)


def scatter_parts(keep, send, users):
    far = users // 4
    order = split_order(far)
    size = keep.shape[0] // (2 * far)

    def swap(block, bit):
        return lax.ppermute(block, "user", [(i, i ^ bit) for i in range(users)])

    got = swap(send, 1)

    def both(lo, hi):
        span = slice(lo * size, hi * size)
        return keep[span].astype(f32) + got[span].astype(f32)

    cuts = [(0, 1), (1, far - 1), (far - 1, far)]
    across = [swap(both(far + lo, far + hi).astype(bf16), 2) for lo, hi in cuts]
    moved = []
    for (lo, hi), other in zip(cuts[:2], across):
        near = (both(lo, hi) + other.astype(f32)).astype(bf16)
        for at in range(lo, hi):
            pairs = [(i, (i - 4 * order[at]) % users) for i in range(users)]
            block = near[(at - lo) * size : (at - lo + 1) * size]
            moved.append(lax.ppermute(block, "user", pairs))
    return got, [across[2]] + moved


def finish_kernel(cols_in, kept_ref, sent_ref, *refs):
    terms = refs[:-3]
    gx_ref, win_ref, wout_ref = refs[-3:]
    gx_ref[...] = (kept_ref[...].astype(f32) + sent_ref[...].astype(f32)).astype(bf16)

    @pl.when(pl.program_id(0) == 0)
    def _():
        total = terms[0][...].astype(f32)
        for term in terms[1:]:
            total = total + term[...].astype(f32)
        win_ref[...] = total[:, :cols_in]
        wout_ref[...] = total[:, cols_in:]


def finish(kept, sent, keep, got, rest, cols_in):
    rows, own = kept.shape
    size, cols = rest[0].shape
    slot = keep.shape[0] // (2 * size) - 1
    steps = 4
    lines = pl.BlockSpec((rows // steps, own), lambda i: (i, 0))
    specs = [lines] * 2
    specs += [pl.BlockSpec((size, cols), lambda i: (slot, 0))] * 2
    specs += [pl.BlockSpec((size, cols), lambda i: (0, 0))] * len(rest)
    return pl.pallas_call(
        functools.partial(finish_kernel, cols_in),
        grid=(steps,),
        out_shape=[
            jax.ShapeDtypeStruct((rows, own), bf16),
            jax.ShapeDtypeStruct((size, cols_in), f32),
            jax.ShapeDtypeStruct((size, cols - cols_in), f32),
        ],
        in_specs=specs,
        out_specs=[
            lines,
            pl.BlockSpec((size, cols_in), lambda i: (0, 0)),
            pl.BlockSpec((size, cols - cols_in), lambda i: (0, 0)),
        ],
        compiler_params=pltpu.CompilerParams(vmem_limit_bytes=32 * 2**20),
        cost_estimate=pl.CostEstimate(
            flops=rows * own, bytes_accessed=12 * 2**20, transcendentals=0
        ),
    )(kept, sent, keep, got, *rest)


def exchange(block, tensor):
    if tensor == 2:
        return lax.ppermute(block, "tensor", [(0, 1), (1, 0)])
    own = block.shape[1]
    every = lax.all_gather(block, "tensor", axis=1, tiled=True)
    return jnp.roll(every, -lax.axis_index("tensor") * own, axis=1)[:, own:]


def give_back(block, own, tensor):
    if tensor == 2:
        return lax.ppermute(block, "tensor", [(0, 1), (1, 0)])
    every = jnp.concatenate([jnp.zeros((block.shape[0], own), block.dtype), block], axis=1)
    every = jnp.roll(every, lax.axis_index("tensor") * own, axis=1)
    return lax.psum_scatter(every, "tensor", scatter_dimension=1, tiled=True)


def local(events, cotangent, w_in, w_out, slot_source, slot_length):
    tensor = lax.axis_size("tensor")
    users = lax.axis_size("user")
    hist, seq_len, own = events.shape
    x = events.reshape(hist * seq_len, own)
    d = cotangent.reshape(hist * seq_len, own)
    blocks = sum(steps for _, steps in GROUPS)
    rows = hist // blocks * seq_len
    far, ahead = [], None
    for start, steps in GROUPS:
        spans = [slice(i * rows, (i + 1) * rows) for i in range(start, start + steps)]
        if ahead is not None:
            x, d, _ = lax.optimization_barrier((x, d, ahead))
        ahead = jnp.concatenate([t[span] for span in spans for t in (x, d)], axis=0)
        far.append(exchange(ahead, tensor))

    user = lax.axis_index("user")
    slots = jnp.stack([slot_source, slot_length]).astype(bf16)
    slots = jnp.pad(slots, ((0, 0), (0, SLOTS // 2 - hist)), constant_values=-1)
    slots = jnp.pad(slots.reshape(1, SLOTS), ((0, w_in.shape[0] - 1), (0, 0)), constant_values=-1)
    shard = jnp.concatenate([w_in, w_out, slots], axis=1)
    pieces = gather_parts(shard, shard.shape[1] // 256 * 128, users, user)
    where = jnp.stack([lax.axis_index("tensor"), user]).astype(jnp.int32)

    past = []
    for group, theirs in zip(GROUPS, far):
        kept, bs, *grads = group_call(
            group, blocks, users, tensor, where, x, d, theirs, pieces, past
        )
        past = grads + [kept, bs]
    sent = give_back(bs, own, tensor)
    keep, send = grads
    got, rest = scatter_parts(keep, send, users)
    grad_x, grad_in, grad_out = finish(kept, sent, keep, got, rest, w_in.shape[1])
    return (grad_x.reshape(hist, seq_len, own), grad_in, grad_out)


def solution(mesh):
    in_specs = (
        P("user", None, "tensor"),
        P("user", None, "tensor"),
        P("user", "tensor"),
        P("user", "tensor"),
        P("user"),
        P("user"),
    )
    out_specs = (P("user", None, "tensor"), P("user", "tensor"), P("user", "tensor"))
    return jax.shard_map(local, mesh=mesh, in_specs=in_specs, out_specs=out_specs, check_vma=False)
```
